32 devices in a mesh: batch: 16 (over z, x, core), blk: 2 (over y).
Axes of the slice: x: 2, y: 2, z: 4, core: 2. Of those that a mesh axis runs over, the one named last changes fastest.
Arguments:
- inputs: bfloat16 [32, 1024, 768], P('batch', 'blk'), may hold values from -6 to 6
- first_values: bfloat16 [32, 1024, 384], P('batch', 'blk'), may hold values from -6 to 6
- segments: int32 [32, 1024], P('batch', 'blk'), may hold values from -1 to 3, as said below
- ln1_gain: bfloat16 [768], replicated, may hold values from 0.5 to 1.5
- first_norm_bias: bfloat16 [768], replicated, may hold values from -3 to 3
- w_qkv: bfloat16 [768, 1920], replicated, may hold values from -0.21875 to 0.21875
- b_query: bfloat16 [768], replicated, may hold values from -3 to 3
- b_value: bfloat16 [384], replicated, may hold values from -3 to 3
- w_out: bfloat16 [768, 768], replicated, may hold values from -0.875 to 0.875
- b_out: bfloat16 [768], replicated, may hold values from -3 to 3
- ln2_gain: bfloat16 [768], replicated, may hold values from 0.5 to 1.5
- second_norm_bias: bfloat16 [768], replicated, may hold values from -3 to 3
- w_fc: bfloat16 [768, 3072], replicated, may hold values from -0.21875 to 0.21875
- b_fc: bfloat16 [3072], replicated, may hold values from -3 to 3
- w_proj: bfloat16 [3072, 768], replicated, may hold values from -0.109375 to 0.109375
- b_proj: bfloat16 [768], replicated, may hold values from -3 to 3
- cotangent: bfloat16 [32, 1024, 768], P('batch', 'blk'), may hold values from -6 to 6
Outputs:
- layer_out: bfloat16 [32, 1024, 768], P('batch', 'blk')
- grad_inputs: bfloat16 [32, 1024, 768], P('batch', 'blk')
- grad_first: bfloat16 [32, 1024, 384], P('batch', 'blk')
- grad_ln1_gain: float32 [768], P('batch')
- grad_ln1_bias: float32 [768], P('batch')
- grad_w_qkv: float32 [768, 1920], P('batch')
- grad_b_query: float32 [768], P('batch')
- grad_b_value: float32 [384], P('batch')
- grad_w_out: float32 [768, 768], P('batch')
- grad_b_out: float32 [768], P('batch')
- grad_ln2_gain: float32 [768], P('batch')
- grad_ln2_bias: float32 [768], P('batch')
- grad_w_fc: float32 [768, 3072], P('batch')
- grad_b_fc: float32 [3072], P('batch')
- grad_w_proj: float32 [3072, 768], P('batch')
- grad_b_proj: float32 [768], P('batch')
The draws below stay inside these ranges and needn't reach their ends.
Inputs may be any that keep to these rules, and one draw needn't show every extreme that they name: `segments`: along each row the document numbers never fall before the padding; padding tokens carry -1 and form the row's tail.
All inputs are finite; a program needn't handle non-finite values.
Results may differ from the reference program's by a relative error of at most 0.02.
Values may be sent and summed in bfloat16 or wider, within the bound.
A program may use at most 320 MiB of HBM per device.

```python
import jax
import jax.numpy as jnp
from jax import lax

D = 768
HEADS = 12
HEAD_DIM = 64
FF = 3072
SEQ = 1024
MICRO = 2
ROWS_MB = 1
VAL_W = 384
QKV_W = 1920
BLK_TOK = 512
ROWS = 32


def draw_segments(key, part):
    key = jax.random.fold_in(key, 11)
    key_pick, key_start, key_pad, key_tail = jax.random.split(key, 4)
    local_rows = MICRO * ROWS_MB
    group_count = ROWS // local_rows
    chosen = jax.random.randint(key_pick, (group_count,), 0, local_rows)
    row_ids = jnp.arange(ROWS)
    long_row = row_ids % local_rows == chosen[row_ids // local_rows]
    starts = jax.random.randint(key_start, (ROWS, SEQ), 0, SEQ) < 4
    position = jnp.arange(SEQ)
    middle_state = (position >= BLK_TOK // 2) & (position < SEQ - BLK_TOK // 2)
    forced = (position == SEQ // 8) | (position == SEQ // 4) | (position == SEQ // 2)
    starts = starts | jnp.logical_not(long_row)[:, None] & forced[None, :]
    starts = starts & jnp.logical_not(long_row[:, None] & middle_state[None, :])
    ids = jnp.minimum(jnp.cumsum(starts.astype(jnp.int32), axis=1), 3)
    pad_normal = jax.random.randint(key_pad, (ROWS,), 1, SEQ // 4 + 1)
    pad_long = jax.random.randint(key_tail, (ROWS,), 0, BLK_TOK // 2)
    padding = jnp.where(long_row, pad_long, pad_normal)
    ids = jnp.where(position[None, :] >= SEQ - padding[:, None], -1, ids)
    return ids.astype(jnp.int32)


def levels(rng, shape, cuts, low, top_value):
    loudness, own = 1.0, jax.random.fold_in(rng, 6)
    for dim, shards_of in cuts:
        draws = jnp.exp(jax.random.uniform(jax.random.fold_in(own, dim), (shards_of,), jnp.float32, low / len(cuts), top_value / len(cuts)))
        loudness = loudness * jnp.repeat(draws, shape[dim] // shards_of).reshape([-1 if axis == dim else 1 for axis in range(len(shape))])
    return loudness


def bell_draw(own_key, extent, spread, limit, pieces=(), dtype=jnp.bfloat16):
    level = levels(own_key, extent, pieces, -0.22, 0.18) if pieces else 1.0
    array = jax.random.normal(own_key, extent, jnp.float32) * spread * level
    return jnp.minimum(jnp.maximum(array, -limit), limit).astype(dtype)


def setup_inputs(seed: int = 0) -> dict:
    splits = jax.random.split(jax.random.key(seed), 18)
    inputs = bell_draw(splits[0], (ROWS, SEQ, D), 1.0, 6.0, ((0, 16), (1, 2)))
    first_values = bell_draw(splits[1], (ROWS, SEQ, VAL_W), 1.0, 6.0, ((0, 16), (1, 2)))
    segments = draw_segments(jax.random.fold_in(splits[17], 71), 0)
    ln1_gain = jnp.clip(1.0 + 0.1 * jax.random.normal(splits[3], (D,), jnp.float32), 0.5, 1.5).astype(jnp.bfloat16)
    first_norm_bias = bell_draw(splits[4], (D,), 0.5, 3.0)
    w_qkv = bell_draw(splits[5], (D, QKV_W), D ** -0.5, 0.21875)
    b_query = bell_draw(splits[6], (D,), 0.5, 3.0)
    b_value = bell_draw(splits[7], (VAL_W,), 0.5, 3.0)
    w_out = bell_draw(splits[8], (D, D), (D // 16) ** -0.5, 0.875)
    b_out = bell_draw(splits[9], (D,), 0.5, 3.0)
    ln2_gain = jnp.clip(1.0 + 0.1 * jax.random.normal(splits[10], (D,), jnp.float32), 0.5, 1.5).astype(jnp.bfloat16)
    second_norm_bias = bell_draw(splits[11], (D,), 0.5, 3.0)
    w_fc = bell_draw(splits[12], (D, FF), D ** -0.5, 0.21875)
    b_fc = bell_draw(splits[13], (FF,), 0.5, 3.0)
    w_proj = bell_draw(splits[14], (FF, D), FF ** -0.5, 0.109375)
    b_proj = bell_draw(splits[15], (D,), 0.5, 3.0)
    cotangent = bell_draw(splits[16], (ROWS, SEQ, D), 1.0, 6.0, ((0, 16), (1, 2)))
    return {"inputs": inputs, "first_values": first_values, "segments": segments, "ln1_gain": ln1_gain, "first_norm_bias": first_norm_bias, "w_qkv": w_qkv, "b_query": b_query, "b_value": b_value, "w_out": w_out, "b_out": b_out, "ln2_gain": ln2_gain, "second_norm_bias": second_norm_bias, "w_fc": w_fc, "b_fc": b_fc, "w_proj": w_proj, "b_proj": b_proj, "cotangent": cotangent}


EPS = 1e-05
NEG = -1e+30
HIGH = lax.Precision.HIGHEST

@jax.custom_vjp
def low(v):
    return lax.optimization_barrier(v.astype(jnp.bfloat16)).astype(jnp.float32)

@jax.custom_vjp
def low_back(v):
    return v

def low_keep(v):
    return (low(v), None)

def low_pass(kept, grad):
    return (grad,)

def back_keep(v):
    return (v, None)

def back_low(kept, grad):
    return (low(grad),)
low.defvjp(low_keep, low_pass)
low_back.defvjp(back_keep, back_low)

def layer_norm(values_in, norm_gain, shift_bias):
    mean_val = lax.optimization_barrier(jnp.mean(values_in, axis=-1, keepdims=True))
    centred_rows = values_in - mean_val
    var_val = lax.optimization_barrier(jnp.mean(centred_rows * centred_rows, axis=-1, keepdims=True))
    return centred_rows * lax.rsqrt(var_val + EPS) * norm_gain + shift_bias

def gelu_tanh(values_in):
    cubic = values_in + 0.044715 * values_in * values_in * values_in
    return 0.5 * values_in * (1.0 + jnp.tanh(0.7978845608028654 * cubic))

def matmul(left, right):
    return jnp.einsum('gsd,de->gse', left, right, precision=HIGH)

def split_heads(values_in):
    return values_in.reshape(values_in.shape[0], values_in.shape[1], HEADS, HEAD_DIM)

def layer(params, rows_in, first_in, seg_rows):
    ln1_gain, first_norm_bias, w_qkv, b_query, b_value, w_out, b_out, ln2_gain, second_norm_bias, w_fc, b_fc, w_proj, b_proj = params
    groups = rows_in.shape[0]
    act1 = low(layer_norm(rows_in, ln1_gain, first_norm_bias))
    projected = matmul(act1, w_qkv)
    query = low(low_back(projected[..., :D] + b_query))
    keys = low(low_back(projected[..., D:2 * D]))
    fresh = low(low_back(projected[..., 2 * D:] + b_value))
    values = jnp.concatenate([fresh, first_in], axis=-1)
    raw = low_back(jnp.einsum('gqhd,gkhd->gqhk', split_heads(query), split_heads(keys), precision=HIGH))
    position = jnp.arange(SEQ)
    same = seg_rows[:, :, None] == seg_rows[:, None, :]
    causal = position[None, :] <= position[:, None]
    live = seg_rows[:, :, None] >= 0
    diagonal = position[None, :] == position[:, None]
    mask = (same & causal[None] & live | diagonal[None])[:, :, None, :]
    scores = jnp.where(mask, raw * HEAD_DIM ** (-0.5), NEG)
    highest = lax.optimization_barrier(jnp.max(scores, axis=-1, keepdims=True))
    expo = jnp.exp(scores - highest)
    probs = low(expo / lax.optimization_barrier(jnp.sum(expo, axis=-1, keepdims=True)))
    attention = jnp.einsum('gqhk,gkhd->gqhd', probs, split_heads(values), precision=HIGH)
    attention = low(low_back(attention.reshape(groups, SEQ, D)))
    middle_state = rows_in + low_back(matmul(attention, w_out) + b_out)
    act2 = low(layer_norm(middle_state, ln2_gain, second_norm_bias))
    hidden = low(gelu_tanh(low_back(matmul(act2, w_fc) + b_fc)))
    return middle_state + matmul(hidden, w_proj) + b_proj

def reference(inputs, first_values, segments, ln1_gain, first_norm_bias, w_qkv, b_query, b_value, w_out, b_out, ln2_gain, second_norm_bias, w_fc, b_fc, w_proj, b_proj, cotangent):
    params = tuple((item.astype(jnp.float32) for item in (ln1_gain, first_norm_bias, w_qkv, b_query, b_value, w_out, b_out, ln2_gain, second_norm_bias, w_fc, b_fc, w_proj, b_proj)))
    group = 2
    steps_count = ROWS // group
    rows_all = inputs.astype(jnp.float32).reshape(steps_count, group, SEQ, D)
    first_all = first_values.astype(jnp.float32).reshape(steps_count, group, SEQ, VAL_W)
    seg_all = segments.reshape(steps_count, group, SEQ)
    cot_all = cotangent.astype(jnp.float32).reshape(steps_count, group, SEQ, D)

    def step(totals, item):
        rows_in, first_in, seg_rows, cot_rows = item

        def run(pars, rows_arg, first_arg):
            return layer(pars, rows_arg, first_arg, seg_rows)
        result, pull = jax.vjp(run, params, rows_in, first_in)
        grad_pars, grad_rows, grad_first = pull(cot_rows)
        totals = jax.tree.map(lambda left, right: left + right, totals, grad_pars)
        return (totals, (result.astype(jnp.bfloat16), grad_rows.astype(jnp.bfloat16), grad_first.astype(jnp.bfloat16)))
    start_totals = tuple((jnp.zeros_like(item) for item in params))
    totals, stacked = lax.scan(step, start_totals, (rows_all, first_all, seg_all, cot_all))
    layer_out = stacked[0].reshape(ROWS, SEQ, D)
    grad_inputs = stacked[1].reshape(ROWS, SEQ, D)
    grad_first = stacked[2].reshape(ROWS, SEQ, VAL_W)
    return (layer_out, grad_inputs, grad_first, totals[0], totals[1], totals[2], totals[3], totals[4], totals[5], totals[6], totals[7], totals[8], totals[9], totals[10], totals[11], totals[12])
```

```python
import functools

import jax
import jax.numpy as jnp
from jax import lax
from jax.experimental import pallas as pl
from jax.experimental.pallas import tpu as pltpu
from jax.sharding import PartitionSpec as P

HEADS = 12
HEAD_DIM = 64
PAIRS = HEADS // 2
LANES = 2 * HEAD_DIM
EPS = 1e-05
NEG = -1e30
QB = 256
F32 = jnp.float32
BF = jnp.bfloat16
MIB = 2**20
MESH = pl.DeviceIdType.MESH


def nn(a, b):
    return lax.dot_general(a, b, (((1,), (0,)), ((), ())), preferred_element_type=F32)


def nt(a, b):
    return lax.dot_general(a, b, (((1,), (1,)), ((), ())), preferred_element_type=F32)


def tn(a, b):
    return lax.dot_general(a, b, (((0,), (0,)), ((), ())), preferred_element_type=F32)


def norm_parts(rows):
    mean = jnp.mean(rows, axis=-1, keepdims=True)
    centred = rows - mean
    inverse = lax.rsqrt(jnp.mean(centred * centred, axis=-1, keepdims=True) + EPS)
    return centred * inverse, inverse


def norm_pull(grad, xhat, inverse, gain):
    scaled = grad * gain
    first = jnp.mean(scaled, axis=-1, keepdims=True)
    second = jnp.mean(scaled * xhat, axis=-1, keepdims=True)
    return inverse * (scaled - first - xhat * second)


def column_sum(rows):
    return jnp.sum(rows, axis=0, keepdims=True)


def front_kernel(
    x_in,
    fv_in,
    seg_in,
    cot_in,
    g1_ref,
    b1_ref,
    wqkv_in,
    bq_ref,
    bv_ref,
    wout_in,
    bout_ref,
    g2_ref,
    b2_ref,
    x_out,
    q_out,
    k_out,
    v_out,
    att_out,
    act2_out,
    mid_out,
    lse_ref,
    bias_out,
    cot_out,
    xs,
    qs,
    ks,
    vs,
    atts,
    act2s,
    mids,
    bias,
    wqkv,
    wout,
    segrow,
    segsend,
    segcol,
    in_sem,
    out_sem,
    send_sem,
    recv_sem,
):
    half = x_in.shape[1]
    tokens = 2 * half
    width = x_in.shape[2]
    val = fv_in.shape[2]
    steps = tokens // QB
    me = lax.axis_index("blk")
    other = 1 - me
    mine = pl.multiple_of(me * half, half)
    theirs = pl.multiple_of(other * half, half)

    def local_in(i, src, dst):
        copy = pltpu.make_async_copy(src, dst, in_sem.at[i])
        copy.start()
        return copy

    own_x = local_in(0, x_in.at[me], xs.at[pl.ds(mine, half)])
    own_fv = local_in(1, fv_in.at[me], vs.at[pl.ds(mine, half), pl.ds(val, val)])
    own_w = local_in(2, wqkv_in, wqkv)
    own_wo = local_in(3, wout_in, wout)
    own_cot = local_in(4, cot_in.at[me], cot_out.at[pl.ds(mine, half)])
    first, second = seg_in[0:1, :], seg_in[1:2, :]
    segsend[...] = jnp.broadcast_to(jnp.where(me == 0, second, first), segsend.shape)

    barrier = pltpu.get_barrier_semaphore()
    pl.semaphore_signal(barrier, inc=1, device_id={"blk": other}, device_id_type=MESH)
    pl.semaphore_wait(barrier, 1)

    def remote(i, src, dst):
        copy = pltpu.make_async_remote_copy(
            src_ref=src,
            dst_ref=dst,
            send_sem=send_sem.at[i],
            recv_sem=recv_sem.at[i],
            device_id={"blk": other},
            device_id_type=MESH,
        )
        copy.start()
        return copy

    part = half // 2
    far_x = [
        remote(
            c,
            x_in.at[other, pl.ds(c * part, part)],
            xs.at[pl.ds(pl.multiple_of(mine + c * part, part), part)],
        )
        for c in range(2)
    ]
    far_seg = remote(2, segsend, segrow.at[:, pl.ds(mine, half)])
    far_fv = remote(3, fv_in.at[other], vs.at[pl.ds(mine, half), pl.ds(val, val)])
    far_cot = remote(4, cot_in.at[other], cot_out.at[pl.ds(mine, half)])

    own_row = jnp.broadcast_to(jnp.where(me == 0, first, second), (8, half))
    segrow[:, pl.ds(mine, half)] = own_row

    def project(start):
        rows = pl.ds(pl.multiple_of(start, QB), QB)
        xhat, _ = norm_parts(xs[rows, :].astype(F32))
        act1 = (xhat * g1_ref[...].astype(F32) + b1_ref[...].astype(F32)).astype(BF)
        out = nn(act1, wqkv[...])
        query = (out[:, :width] + bq_ref[...].astype(F32)).astype(BF)
        qs[rows, :] = query * jnp.asarray(HEAD_DIM**-0.5, BF)
        ks[rows, :] = out[:, width : 2 * width].astype(BF)
        vs[rows, pl.ds(0, val)] = (out[:, 2 * width :] + bv_ref[...].astype(F32)).astype(BF)

    own_x.wait()
    own_w.wait()
    for c in range(2):
        project(mine + c * QB)
    for c in range(2):
        far_x[c].wait()
        project(theirs + c * part)

    outs = []

    def local_out(src, dst):
        copy = pltpu.make_async_copy(src, dst, out_sem.at[len(outs)])
        copy.start()
        outs.append(copy)

    local_out(xs, x_out)
    local_out(qs, q_out)
    local_out(ks, k_out)

    far_seg.wait()
    for c in range(tokens // LANES):
        row = segrow[0:1, c * LANES : (c + 1) * LANES].astype(F32)
        segcol[c * LANES : (c + 1) * LANES, :] = jnp.broadcast_to(row, (LANES, LANES)).T
    for j in range(steps):
        key = segcol[j * QB : (j + 1) * QB, :]
        key = jnp.concatenate([key] * (QB // LANES), axis=1)
        for i in range(j, steps):
            query = segrow[0:1, i * QB : (i + 1) * QB].astype(F32)
            seen = (key == query) & (query >= 0.0)
            if i == j:
                down = lax.broadcasted_iota(jnp.int32, (QB, QB), 0)
                across = lax.broadcasted_iota(jnp.int32, (QB, QB), 1)
                seen = (seen & (down <= across)) | (down == across)
            bias[j * QB : (j + 1) * QB, i * QB : (i + 1) * QB] = jnp.where(seen, 0.0, NEG)
        cut = (pl.ds(j * QB, QB), pl.ds(j * QB, tokens - j * QB))
        local_out(bias.at[cut], bias_out.at[cut])
    own_fv.wait()
    far_fv.wait()
    local_out(vs, v_out)

    low = lax.broadcasted_iota(jnp.int32, (1, LANES), 1) < HEAD_DIM

    @pl.loop(0, PAIRS)
    def _(p):
        cols = pl.ds(pl.multiple_of(p * LANES, LANES), LANES)
        k = ks[:, cols]
        v = vs[:, cols]

        def score(i, h):
            q = qs[i * QB : (i + 1) * QB, cols]
            q = jnp.where(low if h == 0 else ~low, q, jnp.zeros_like(q))
            span = (i + 1) * QB
            return nt(k[:span], q) + bias[:span, i * QB : span]

        done = {}

        def finish(i, h, s):
            span = (i + 1) * QB
            top = jnp.max(s, axis=0, keepdims=True)
            e = jnp.exp(s - top)
            total = jnp.sum(e, axis=0, keepdims=True)
            done[h] = tn((e * (1.0 / total)).astype(BF), v[:span])
            lse_ref[p, h : h + 1, i * QB : span] = top + jnp.log(total)
            if h == 1:
                atts[i * QB : span, cols] = jnp.where(low, done[0], done[1]).astype(BF)

        waiting = []
        for i in range(steps):
            for h in range(2):
                waiting.append((i, h, score(i, h)))
                if len(waiting) > 2:
                    finish(*waiting.pop(0))
        for item in waiting:
            finish(*item)

    local_out(atts, att_out)
    own_wo.wait()
    for c in range(steps):
        rows = slice(c * QB, (c + 1) * QB)
        middle = xs[rows, :].astype(F32) + nn(atts[rows, :], wout[...]) + bout_ref[...].astype(F32)
        mids[rows, :] = middle
        xhat, _ = norm_parts(middle)
        act2s[rows, :] = (xhat * g2_ref[...].astype(F32) + b2_ref[...].astype(F32)).astype(BF)
    local_out(mids, mid_out)
    local_out(act2s, act2_out)
    for copy in outs:
        copy.wait()
    own_cot.wait()
    far_cot.wait()


def front(x, fv, seg, cot, g1, b1, wqkv, bq, bv, wout, bout, g2, b2):
    half, width, val = x.shape[1], x.shape[2], fv.shape[2]
    tokens = 2 * half
    hbm = pl.BlockSpec(memory_space=pl.ANY)
    vmem = pl.BlockSpec(memory_space=pltpu.VMEM)
    flat = jax.ShapeDtypeStruct((tokens, width), BF)
    shape = jax.ShapeDtypeStruct
    return pl.pallas_call(
        front_kernel,
        in_specs=[hbm, hbm, vmem, hbm, vmem, vmem, hbm, vmem, vmem, hbm, vmem, vmem, vmem],
        out_specs=[hbm] * 7 + [vmem] + [hbm] * 2,
        out_shape=[
            flat,
            flat,
            flat,
            flat,
            flat,
            flat,
            shape((tokens, width), F32),
            shape((PAIRS, 2, tokens), F32),
            shape((tokens, tokens), F32),
            flat,
        ],
        scratch_shapes=[
            pltpu.VMEM((tokens, width), BF),
            pltpu.VMEM((tokens, width), BF),
            pltpu.VMEM((tokens, width), BF),
            pltpu.VMEM((tokens, width), BF),
            pltpu.VMEM((tokens, width), BF),
            pltpu.VMEM((tokens, width), BF),
            pltpu.VMEM((tokens, width), F32),
            pltpu.VMEM((tokens, tokens), F32),
            pltpu.VMEM(wqkv.shape, BF),
            pltpu.VMEM(wout.shape, BF),
            pltpu.VMEM((8, tokens), jnp.int32),
            pltpu.VMEM((8, half), jnp.int32),
            pltpu.VMEM((tokens, LANES), F32),
            pltpu.SemaphoreType.DMA((5,)),
            pltpu.SemaphoreType.DMA((7 + tokens // QB,)),
            pltpu.SemaphoreType.DMA((5,)),
            pltpu.SemaphoreType.DMA((5,)),
        ],
        compiler_params=pltpu.CompilerParams(
            collective_id=0, has_side_effects=True, vmem_limit_bytes=56 * MIB
        ),
        name="front",
    )(x, fv, seg, cot, g1, b1, wqkv, bq, bv, wout, bout, g2, b2)


def feed_kernel(
    act2,
    cot,
    mid,
    att,
    g2_ref,
    bproj_ref,
    wout,
    wfc,
    bfc_ref,
    wproj,
    lout,
    gmid,
    gatt,
    dots,
    dwout,
    dwfc,
    dwproj,
    dbfc,
    small,
    acc,
    dact,
    act2t,
    hid,
    dpre,
    sel,
):
    t = pl.program_id(0)
    tokens, width = act2.shape
    steps = tokens // QB

    @pl.when(t == 0)
    def _():
        act2t[...] = act2[...].T
        acc[...] = jnp.zeros_like(acc)
        dact[...] = jnp.zeros_like(dact)
        head = lax.broadcasted_iota(jnp.int32, sel.shape, 0)
        feature = lax.broadcasted_iota(jnp.int32, sel.shape, 1)
        inside = (feature >= head * HEAD_DIM) & (feature < (head + 1) * HEAD_DIM)
        sel[...] = jnp.where(inside, 1.0, 0.0).astype(BF)

    total = None
    for c in range(steps):
        rows = slice(c * QB, (c + 1) * QB)
        u = nn(act2[rows, :], wfc[...]) + bfc_ref[...].astype(F32)
        square = u * u
        bend = jnp.tanh(u * (0.7978845608028654 + (0.7978845608028654 * 0.044715) * square))
        halfway = 0.5 + 0.5 * bend
        hidden = (u * halfway).astype(BF)
        hid[rows, :] = hidden
        acc[rows, :] += nn(hidden, wproj[...])
        slope = halfway + (u * (0.5 - 0.5 * bend * bend)) * (
            0.7978845608028654 + (3 * 0.7978845608028654 * 0.044715) * square
        )
        grad = (nt(cot[rows, :], wproj[...]) * slope).astype(BF)
        dpre[rows, :] = grad
        dact[rows, :] += nt(grad, wfc[...])
        part = column_sum(grad.astype(F32))
        total = part if total is None else total + part
    dbfc[...] = total
    dwproj[...] = tn(hid[...], cot[...]).astype(BF)
    dwfc[...] = nn(act2t[...], dpre[...]).astype(BF)

    @pl.when(t == pl.num_programs(0) - 1)
    def _():
        gain = g2_ref[...].astype(F32)
        sums = [None] * 4
        for c in range(steps):
            rows = slice(c * QB, (c + 1) * QB)
            middle = mid[rows, :]
            upstream = cot[rows, :].astype(F32)
            lout[rows, :] = (middle + acc[rows, :] + bproj_ref[...].astype(F32)).astype(BF)
            xhat, inverse = norm_parts(middle)
            da = dact[rows, :]
            grad_middle = upstream + norm_pull(da, xhat, inverse, gain)
            gmid[rows, :] = grad_middle
            branch = grad_middle.astype(BF)
            hid[rows, :width] = branch
            parts = [
                column_sum(upstream),
                column_sum(da * xhat),
                column_sum(da),
                column_sum(branch.astype(F32)),
            ]
            sums = [b if a is None else a + b for a, b in zip(sums, parts)]
            ga = nt(branch, wout[...]).astype(BF)
            gatt[rows, :] = ga
            product = ga.astype(F32) * att[rows, :].astype(F32)
            big = product.astype(BF)
            rest = (product - big.astype(F32)).astype(BF)
            both = nt(sel[...], big) + nt(sel[...], rest)
            for p in range(PAIRS):
                dots[p, :, rows] = both[2 * p : 2 * p + 2, :]
        small[...] = jnp.concatenate(sums + [jnp.zeros((4, width), F32)], axis=0)
        dwout[...] = tn(att[...], hid[:, :width]).astype(BF)


def feed(act2, cot, mid, att, g2, bproj, wout, wfc, bfc, wproj):
    tokens, width = act2.shape
    ff = wfc.shape[1]
    tile = 768
    shape = jax.ShapeDtypeStruct
    flat = shape((tokens, width), BF)

    def whole(s):
        return pl.BlockSpec(s, lambda t: (0,) * len(s))

    rows = whole((tokens, width))
    line = whole((1, width))
    return pl.pallas_call(
        feed_kernel,
        grid=(ff // tile,),
        in_specs=[
            rows,
            rows,
            rows,
            rows,
            line,
            line,
            whole(wout.shape),
            pl.BlockSpec((width, tile), lambda t: (0, t)),
            pl.BlockSpec((1, tile), lambda t: (0, t)),
            pl.BlockSpec((tile, width), lambda t: (t, 0)),
        ],
        out_specs=[
            rows,
            rows,
            rows,
            whole((PAIRS, 2, tokens)),
            whole(wout.shape),
            pl.BlockSpec((width, tile), lambda t: (0, t)),
            pl.BlockSpec((tile, width), lambda t: (t, 0)),
            pl.BlockSpec((1, tile), lambda t: (0, t)),
            whole((8, width)),
        ],
        out_shape=[
            flat,
            shape((tokens, width), F32),
            flat,
            shape((PAIRS, 2, tokens), F32),
            shape(wout.shape, BF),
            shape(wfc.shape, BF),
            shape(wproj.shape, BF),
            shape((1, ff), F32),
            shape((8, width), F32),
        ],
        scratch_shapes=[
            pltpu.VMEM((tokens, width), F32),
            pltpu.VMEM((tokens, width), F32),
            pltpu.VMEM((width, tokens), BF),
            pltpu.VMEM((tokens, tile), BF),
            pltpu.VMEM((tokens, tile), BF),
            pltpu.VMEM((16, width), BF),
        ],
        compiler_params=pltpu.CompilerParams(vmem_limit_bytes=60 * MIB),
        name="feed",
    )(act2, cot, mid, att, g2, bproj, wout, wfc, bfc, wproj)


def back_kernel(q_ref, k_ref, v_ref, do_ref, lse_ref, d_ref, bias, dq_ref, dk_ref, dv_ref, dqa):
    tokens = q_ref.shape[0]
    steps = tokens // QB
    low = lax.broadcasted_iota(jnp.int32, (1, LANES), 1) < HEAD_DIM
    masks = [low, ~low]
    zero = jnp.zeros((), BF)
    q, k, v, do = q_ref[...], k_ref[...], v_ref[...], do_ref[...]
    qm = [jnp.where(m, q, zero) for m in masks]
    km = [jnp.where(m, k, zero) for m in masks]
    dom = [jnp.where(m, do, zero) for m in masks]
    for j in range(steps):
        a = j * QB
        keys = slice(a, a + QB)
        dk = dv = dq = None
        for h in range(2):
            s = nt(k[keys], qm[h][a:]) + bias[keys, a:]
            probs = jnp.exp(s - lse_ref[0, h : h + 1, a:])
            dp = nt(v[keys], dom[h][a:])
            ds = (probs * (dp - d_ref[0, h : h + 1, a:])).astype(BF)
            dvh = nn(probs.astype(BF), dom[h][a:])
            dkh = nn(ds, qm[h][a:])
            dqh = tn(ds, km[h][keys])
            dk = dkh if dk is None else dk + dkh
            dv = dvh if dv is None else dv + dvh
            dq = dqh if dq is None else dq + dqh
        dk_ref[keys, :] = dk.astype(BF)
        dv_ref[keys, :] = dv.astype(BF)
        if j == 0:
            dqa[...] = dq
        else:
            dqa[a:, :] += dq
    dq_ref[...] = (dqa[...] * HEAD_DIM**-0.5).astype(BF)


def back(q, k, v, do, lse, dots, bias):
    tokens, width = q.shape
    pair = pl.BlockSpec((tokens, LANES), lambda p: (0, p))
    stat = pl.BlockSpec((1, 2, tokens), lambda p: (p, 0, 0))
    flat = jax.ShapeDtypeStruct((tokens, width), BF)
    return pl.pallas_call(
        back_kernel,
        grid=(PAIRS,),
        in_specs=[pair] * 4
        + [stat, stat, pl.BlockSpec((tokens, tokens), lambda p: (0, 0))],
        out_specs=[pair] * 3,
        out_shape=[flat] * 3,
        scratch_shapes=[pltpu.VMEM((tokens, LANES), F32)],
        compiler_params=pltpu.CompilerParams(vmem_limit_bytes=60 * MIB),
        name="back",
    )(q, k, v, do, lse, dots, bias)


def swap_back(rows, half):
    me = lax.axis_index("blk")
    own = lax.dynamic_slice_in_dim(rows, me * half, half, 0)
    give = lax.dynamic_slice_in_dim(rows, (1 - me) * half, half, 0)
    got = lax.ppermute(give, "blk", [(0, 1), (1, 0)])
    return jnp.stack([jnp.where(me == 0, own, got), jnp.where(me == 0, got, own)])


def paired(
    inputs,
    first_values,
    segments,
    ln1_gain,
    first_norm_bias,
    w_qkv,
    b_query,
    b_value,
    w_out,
    b_out,
    ln2_gain,
    second_norm_bias,
    w_fc,
    b_fc,
    w_proj,
    b_proj,
    cotangent,
):
    half, width = inputs.shape[1], inputs.shape[2]
    val = first_values.shape[2]
    line = lambda a: a.reshape(1, -1)
    x, q, k, v, att, act2, mid, lse, bias, cot = front(
        inputs,
        first_values,
        segments,
        cotangent,
        line(ln1_gain),
        line(first_norm_bias),
        w_qkv,
        line(b_query),
        line(b_value),
        w_out,
        line(b_out),
        line(ln2_gain),
        line(second_norm_bias),
    )
    lout, gmid, gatt, dots, dwout, dwfc, dwproj, dbfc, small = feed(
        act2, cot, mid, att, line(ln2_gain), line(b_proj), w_out, w_fc, line(b_fc), w_proj
    )
    dq, dk, dv = back(q, k, v, gatt, lse, dots, bias)
    gain = ln1_gain.astype(F32)
    xhat, inverse = norm_parts(x.astype(F32))
    act1 = (xhat * gain + first_norm_bias.astype(F32)).astype(BF)
    gqkv = jnp.concatenate([dq, dk, dv[:, :val]], axis=1)
    dwqkv = tn(act1, gqkv).astype(BF)
    da = nt(gqkv, w_qkv)
    gx = (gmid + norm_pull(da, xhat, inverse, gain)).astype(BF)
    gathered = (
        jnp.sum(da * xhat, axis=0),
        jnp.sum(da, axis=0),
        dwqkv,
        jnp.sum(dq.astype(F32), axis=0),
        jnp.sum(dv[:, :val].astype(F32), axis=0),
        dwout,
        small[3],
        small[1],
        small[2],
        dwfc,
        dbfc[0],
        dwproj,
        small[0],
    )
    totals = tuple(
        lax.psum_scatter(part.astype(BF), "batch", scatter_dimension=0, tiled=True)
        for part in gathered
    )
    totals = tuple(part.astype(F32) for part in lax.psum(totals, "blk"))
    return (
        swap_back(lout, half),
        swap_back(gx, half),
        swap_back(dv[:, val:], half),
    ) + totals


MICRO = 2


def as_sent(shard):
    return jax.tree.map(lambda a: a.astype(jnp.bfloat16) if a.dtype == jnp.float32 else a, shard)


def apply_norm(values_in, norm_gain, shift_bias):
    mean_val = jnp.mean(values_in, axis=-1, keepdims=True)
    centred_rows = values_in - mean_val
    inverse_deviation = lax.rsqrt(
        jnp.mean(centred_rows * centred_rows, axis=-1, keepdims=True) + EPS
    )
    standardized = centred_rows * inverse_deviation
    return (standardized * norm_gain + shift_bias, standardized, inverse_deviation)


def apply_norm_backward(upstream_gradient, standardized, inverse_deviation, norm_gain):
    scaled_rows = upstream_gradient * norm_gain
    first_average = jnp.mean(scaled_rows, axis=-1, keepdims=True)
    second_average = jnp.mean(scaled_rows * standardized, axis=-1, keepdims=True)
    incoming_gradient = inverse_deviation * (
        scaled_rows - first_average - standardized * second_average
    )
    return (
        incoming_gradient,
        jnp.sum(upstream_gradient * standardized, axis=(0, 1)),
        jnp.sum(upstream_gradient, axis=(0, 1)),
    )


def gelu_tanh(values_in):
    cubic = values_in + 0.044715 * values_in * values_in * values_in
    return 0.5 * values_in * (1.0 + jnp.tanh(0.7978845608028654 * cubic))


def heads_of(values_in):
    return values_in.reshape(values_in.shape[0], values_in.shape[1], HEADS, HEAD_DIM)


def visible(seg_query, seg_key, query_pos, key_pos):
    same = seg_query[:, :, None] == seg_key[:, None, :]
    causal = key_pos[None, :] <= query_pos[:, None]
    live = seg_query[:, :, None] >= 0
    diagonal = key_pos[None, :] == query_pos[:, None]
    return (same & causal[None] & live | diagonal[None])[:, :, None, :]


def score_block(query4, key4, mask):
    raw = jnp.einsum("rqhd,rkhd->rqhk", query4, key4, preferred_element_type=jnp.float32)
    return jnp.where(mask, raw * HEAD_DIM ** (-0.5), NEG)


def grad_block(query4, key4, value4, dout4, log_total, out_dot, mask):
    probs = jnp.where(mask, jnp.exp(score_block(query4, key4, mask) - log_total[..., None]), 0.0)
    probs_low = probs.astype(jnp.bfloat16)
    grad_probs = jnp.einsum("rqhd,rkhd->rqhk", dout4, value4, preferred_element_type=jnp.float32)
    grad_scores = (probs * (grad_probs - out_dot[..., None]) * HEAD_DIM ** (-0.5)).astype(
        jnp.bfloat16
    )
    return (probs_low, grad_scores)


def spread(
    inputs,
    first_values,
    segments,
    ln1_gain,
    first_norm_bias,
    w_qkv,
    b_query,
    b_value,
    w_out,
    b_out,
    ln2_gain,
    second_norm_bias,
    w_fc,
    b_fc,
    w_proj,
    b_proj,
    cotangent,
):
    all_seg = lax.all_gather(segments, "blk", axis=1, tiled=True)
    block_len = inputs.shape[1]
    model_width = inputs.shape[2]
    val_width = first_values.shape[2]
    rows_mb = inputs.shape[0] // MICRO
    own_pos = lax.axis_index("blk") * block_len + jnp.arange(block_len)
    first_gain = ln1_gain.astype(jnp.float32)
    second_gain = ln2_gain.astype(jnp.float32)
    outputs = []
    input_grads = []
    first_grads = []
    totals = None
    for micro_step in range(MICRO):
        first_row = micro_step * rows_mb
        last_row = first_row + rows_mb
        residual_stream = inputs[first_row:last_row].astype(jnp.float32)
        first_part = first_values[first_row:last_row]
        seg_local = segments[first_row:last_row]
        seg_row = all_seg[first_row:last_row]
        cot_part = cotangent[first_row:last_row]
        first_normed_rows, first_standardized, first_inverse_deviation = apply_norm(
            residual_stream, first_gain, first_norm_bias.astype(jnp.float32)
        )
        act1 = first_normed_rows.astype(jnp.bfloat16)
        projected = jnp.einsum("rbd,de->rbe", act1, w_qkv, preferred_element_type=jnp.float32)
        queries = (projected[..., :model_width] + b_query.astype(jnp.float32)).astype(jnp.bfloat16)
        keys_low = projected[..., model_width : 2 * model_width].astype(jnp.bfloat16)
        fresh = (projected[..., 2 * model_width :] + b_value.astype(jnp.float32)).astype(
            jnp.bfloat16
        )
        values_low = jnp.concatenate([fresh, first_part], axis=-1)
        query4 = heads_of(queries)
        key_part = lax.all_gather(keys_low, "blk", axis=1, tiled=True)
        value_part = lax.all_gather(values_low, "blk", axis=1, tiled=True)
        span = key_part.shape[1]
        key_pos = jnp.arange(span)
        mask = visible(seg_local, seg_row, own_pos, key_pos)
        scores = score_block(query4, heads_of(key_part), mask)
        old_max = jnp.full((rows_mb, block_len, HEADS), NEG, jnp.float32)
        new_max = jnp.maximum(old_max, jnp.max(scores, axis=-1))
        weights = jnp.where(mask, jnp.exp(scores - new_max[..., None]), 0.0)
        new_sum = jnp.sum(weights, axis=-1)
        new_acc = jnp.einsum(
            "rqhk,rkhd->rqhd",
            weights.astype(jnp.bfloat16),
            heads_of(value_part),
            preferred_element_type=jnp.float32,
        )
        attention4 = new_acc / new_sum[..., None]
        log_total = new_max + jnp.log(new_sum)
        attention_low = attention4.reshape(rows_mb, block_len, model_width).astype(jnp.bfloat16)
        branch = jnp.einsum("rbd,de->rbe", attention_low, w_out, preferred_element_type=jnp.float32)
        middle_state = residual_stream + branch + b_out.astype(jnp.float32)
        second_normed_rows, second_standardized, second_inverse_deviation = apply_norm(
            middle_state, second_gain, second_norm_bias.astype(jnp.float32)
        )
        act2 = second_normed_rows.astype(jnp.bfloat16)
        pre_gelu = jnp.einsum(
            "rbd,df->rbf", act2, w_fc, preferred_element_type=jnp.float32
        ) + b_fc.astype(jnp.float32)
        hidden = gelu_tanh(pre_gelu).astype(jnp.bfloat16)
        result = middle_state + jnp.einsum(
            "rbf,fd->rbd", hidden, w_proj, preferred_element_type=jnp.float32
        )
        result = result + b_proj.astype(jnp.float32)
        outputs.append(result.astype(jnp.bfloat16))
        upstream_gradient = cot_part.astype(jnp.float32)
        grad_wproj = jnp.einsum("rbf,rbd->fd", hidden, cot_part, preferred_element_type=jnp.float32)
        grad_bproj = jnp.sum(upstream_gradient, axis=(0, 1))
        grad_hidden = jnp.einsum(
            "rbd,fd->rbf", cot_part, w_proj, preferred_element_type=jnp.float32
        )
        gelu_value, gelu_pull = jax.vjp(gelu_tanh, pre_gelu)
        grad_pre = gelu_pull(grad_hidden)[0].astype(jnp.bfloat16)
        grad_wfc = jnp.einsum("rbd,rbf->df", act2, grad_pre, preferred_element_type=jnp.float32)
        grad_bfc = jnp.sum(grad_pre.astype(jnp.float32), axis=(0, 1))
        second_activation_gradient = jnp.einsum(
            "rbf,df->rbd", grad_pre, w_fc, preferred_element_type=jnp.float32
        )
        second_norm_gradient, second_gain_gradient, second_bias_gradient = apply_norm_backward(
            second_activation_gradient, second_standardized, second_inverse_deviation, second_gain
        )
        grad_middle = upstream_gradient + second_norm_gradient
        grad_branch = grad_middle.astype(jnp.bfloat16)
        grad_wout = jnp.einsum(
            "rbd,rbe->de", attention_low, grad_branch, preferred_element_type=jnp.float32
        )
        grad_bout = jnp.sum(grad_branch.astype(jnp.float32), axis=(0, 1))
        grad_attention = jnp.einsum(
            "rbe,de->rbd", grad_branch, w_out, preferred_element_type=jnp.float32
        ).astype(jnp.bfloat16)
        dout4 = heads_of(grad_attention)
        out_dot = jnp.sum(dout4.astype(jnp.float32) * attention4, axis=-1)
        back_key_part = lax.all_gather(keys_low, "blk", axis=1, tiled=True)
        back_value_part = lax.all_gather(values_low, "blk", axis=1, tiled=True)
        back_span = back_key_part.shape[1]
        back_key_pos = jnp.arange(back_span)
        back_mask = visible(seg_local, seg_row, own_pos, back_key_pos)
        part_key4 = heads_of(back_key_part)
        probs_low, grad_scores = grad_block(
            query4, part_key4, heads_of(back_value_part), dout4, log_total, out_dot, back_mask
        )
        query_acc = jnp.einsum(
            "rqhk,rkhd->rqhd", grad_scores, part_key4, preferred_element_type=jnp.float32
        )
        key_piece = jnp.einsum(
            "rqhk,rqhd->rkhd", grad_scores, query4, preferred_element_type=jnp.float32
        ).reshape(rows_mb, back_span, model_width)
        value_piece = jnp.einsum(
            "rqhk,rqhd->rkhd", probs_low, dout4, preferred_element_type=jnp.float32
        ).reshape(rows_mb, back_span, model_width)
        query_acc, key_acc, value_acc = (query_acc, key_piece, value_piece)
        grad_keys, grad_values = (
            lax.psum_scatter(
                key_acc.astype(jnp.bfloat16), "blk", scatter_dimension=1, tiled=True
            ).astype(jnp.float32),
            lax.psum_scatter(
                value_acc.astype(jnp.bfloat16), "blk", scatter_dimension=1, tiled=True
            ).astype(jnp.float32),
        )
        grad_query = query_acc.reshape(rows_mb, block_len, model_width)
        grad_qkv = jnp.concatenate(
            [
                grad_query.astype(jnp.bfloat16),
                grad_keys.astype(jnp.bfloat16),
                grad_values[..., :val_width].astype(jnp.bfloat16),
            ],
            axis=-1,
        )
        first_grads.append(grad_values[..., val_width:].astype(jnp.bfloat16))
        grad_wqkv = jnp.einsum("rbd,rbe->de", act1, grad_qkv, preferred_element_type=jnp.float32)
        grad_bquery = jnp.sum(grad_qkv[..., :model_width].astype(jnp.float32), axis=(0, 1))
        grad_bvalue = jnp.sum(grad_qkv[..., 2 * model_width :].astype(jnp.float32), axis=(0, 1))
        first_activation_gradient = jnp.einsum(
            "rbe,de->rbd", grad_qkv, w_qkv, preferred_element_type=jnp.float32
        )
        first_norm_gradient, first_gain_gradient, first_bias_gradient = apply_norm_backward(
            first_activation_gradient, first_standardized, first_inverse_deviation, first_gain
        )
        input_grads.append((grad_middle + first_norm_gradient).astype(jnp.bfloat16))
        gradient_set = (
            first_gain_gradient,
            first_bias_gradient,
            grad_wqkv,
            grad_bquery,
            grad_bvalue,
            grad_wout,
            grad_bout,
            second_gain_gradient,
            second_bias_gradient,
            grad_wfc,
            grad_bfc,
            grad_wproj,
            grad_bproj,
        )
        if totals is None:
            totals = gradient_set
        else:
            totals = tuple((older + newer for older, newer in zip(totals, gradient_set)))
    totals = jax.tree.map(
        lambda part: part.astype(jnp.float32),
        lax.psum_scatter(as_sent(totals), "batch", scatter_dimension=0, tiled=True),
    )
    totals = jax.tree.map(lambda part: part.astype(jnp.float32), lax.psum(as_sent(totals), "blk"))
    return (
        jnp.concatenate(outputs, axis=0),
        jnp.concatenate(input_grads, axis=0),
        jnp.concatenate(first_grads, axis=0),
    ) + tuple(totals)


def layer(inputs, *rest):
    whole_rows = lax.axis_size("blk") == inputs.shape[0] == 2 and inputs.shape[1] == 2 * QB
    return (paired if whole_rows else spread)(inputs, *rest)


def solution(mesh):
    rows = P("batch", "blk", None)
    flat = P("batch")
    wide = P("batch", None)
    return jax.shard_map(
        layer,
        mesh=mesh,
        in_specs=(rows, rows, P("batch", "blk")) + (P(),) * 13 + (rows,),
        out_specs=(rows, rows, rows)
        + (flat, flat, wide, flat, flat, wide, flat, flat, flat, wide, flat, wide, flat),
        check_vma=False,
    )
```

```python
import functools

import jax
import jax.numpy as jnp
from jax import lax
from jax.experimental import pallas as pl
from jax.experimental.pallas import tpu as pltpu
from jax.sharding import PartitionSpec as P

HEADS = 12
HEAD_DIM = 64
PAIRS = HEADS // 2
LANES = 2 * HEAD_DIM
EPS = 1e-05
NEG = -1e30
QB = 256
F32 = jnp.float32
BF = jnp.bfloat16
MIB = 2**20
MESH = pl.DeviceIdType.MESH


def nn(a, b):
    return lax.dot_general(a, b, (((1,), (0,)), ((), ())), preferred_element_type=F32)


def nt(a, b):
    return lax.dot_general(a, b, (((1,), (1,)), ((), ())), preferred_element_type=F32)


def tn(a, b):
    return lax.dot_general(a, b, (((0,), (0,)), ((), ())), preferred_element_type=F32)


def norm_parts(rows):
    mean = jnp.mean(rows, axis=-1, keepdims=True)
    centred = rows - mean
    inverse = lax.rsqrt(jnp.mean(centred * centred, axis=-1, keepdims=True) + EPS)
    return centred * inverse, inverse


def norm_pull(grad, xhat, inverse, gain):
    scaled = grad * gain
    first = jnp.mean(scaled, axis=-1, keepdims=True)
    second = jnp.mean(scaled * xhat, axis=-1, keepdims=True)
    return inverse * (scaled - first - xhat * second)


def column_sum(rows):
    return jnp.sum(rows, axis=0, keepdims=True)


def spot():
    b = lax.axis_index("batch")
    core = lax.rem(b, 2)
    x = lax.rem(lax.div(b, 2), 2)
    near = lax.rem(lax.div(b, 4), 2)
    far = lax.div(b, 8)
    return b, core, x, near, far


def partners():
    b, core, x, near, far = spot()
    return [
        {"batch": b + 1 - 2 * core},
        {"batch": b + 2 - 4 * x},
        {"batch": b + 4 - 8 * near},
        {"batch": b + 8 - 16 * far},
        {"blk": 1 - lax.axis_index("blk")},
    ]


def greet(friends):
    barrier = pltpu.get_barrier_semaphore()
    for friend in friends:
        pl.semaphore_signal(barrier, inc=1, device_id=friend, device_id_type=MESH)
    pl.semaphore_wait(barrier, len(friends))


def push(src, dst, send_sem, recv_sem, friend):
    copy = pltpu.make_async_remote_copy(
        src_ref=src,
        dst_ref=dst,
        send_sem=send_sem,
        recv_sem=recv_sem,
        device_id=friend,
        device_id_type=MESH,
    )
    return copy


def add_into(dst, src):
    dst[...] = (dst[...].astype(F32) + src[...].astype(F32)).astype(dst.dtype)


def front_kernel(
    x_in,
    fv_in,
    seg_in,
    cot_in,
    g1_ref,
    b1_ref,
    wqkv_in,
    bq_ref,
    bv_ref,
    wout_in,
    bout_ref,
    g2_ref,
    b2_ref,
    x_out,
    q_out,
    k_out,
    v_out,
    att_out,
    act2_out,
    mid_out,
    lse_ref,
    bias_out,
    cot_out,
    xs,
    qs,
    ks,
    vs,
    atts,
    act2s,
    mids,
    bias,
    wqkv,
    wout,
    segrow,
    segsend,
    segcol,
    in_sem,
    out_sem,
    send_sem,
    recv_sem,
):
    half = x_in.shape[1]
    tokens = 2 * half
    width = x_in.shape[2]
    val = fv_in.shape[2]
    steps = tokens // QB
    me = lax.axis_index("blk")
    other = 1 - me
    mine = pl.multiple_of(me * half, half)
    theirs = pl.multiple_of(other * half, half)

    def local_in(i, src, dst):
        copy = pltpu.make_async_copy(src, dst, in_sem.at[i])
        copy.start()
        return copy

    own_x = local_in(0, x_in.at[me], xs.at[pl.ds(mine, half)])
    own_fv = local_in(1, fv_in.at[me], vs.at[pl.ds(mine, half), pl.ds(val, val)])
    own_w = local_in(2, wqkv_in, wqkv)
    own_wo = local_in(3, wout_in, wout)
    own_cot = local_in(4, cot_in.at[me], cot_out.at[pl.ds(mine, half)])
    first, second = seg_in[0:1, :], seg_in[1:2, :]
    segsend[...] = jnp.broadcast_to(jnp.where(me == 0, second, first), segsend.shape)

    barrier = pltpu.get_barrier_semaphore()
    pl.semaphore_signal(barrier, inc=1, device_id={"blk": other}, device_id_type=MESH)
    pl.semaphore_wait(barrier, 1)

    def remote(i, src, dst):
        copy = pltpu.make_async_remote_copy(
            src_ref=src,
            dst_ref=dst,
            send_sem=send_sem.at[i],
            recv_sem=recv_sem.at[i],
            device_id={"blk": other},
            device_id_type=MESH,
        )
        copy.start()
        return copy

    part = half // 2
    far_x = [
        remote(
            c,
            x_in.at[other, pl.ds(c * part, part)],
            xs.at[pl.ds(pl.multiple_of(mine + c * part, part), part)],
        )
        for c in range(2)
    ]
    far_seg = remote(2, segsend, segrow.at[:, pl.ds(mine, half)])
    far_fv = remote(3, fv_in.at[other], vs.at[pl.ds(mine, half), pl.ds(val, val)])
    far_cot = remote(4, cot_in.at[other], cot_out.at[pl.ds(mine, half)])

    own_row = jnp.broadcast_to(jnp.where(me == 0, first, second), (8, half))
    segrow[:, pl.ds(mine, half)] = own_row

    def project(start):
        rows = pl.ds(pl.multiple_of(start, QB), QB)
        xhat, _ = norm_parts(xs[rows, :].astype(F32))
        act1 = (xhat * g1_ref[...].astype(F32) + b1_ref[...].astype(F32)).astype(BF)
        out = nn(act1, wqkv[...])
        query = (out[:, :width] + bq_ref[...].astype(F32)).astype(BF)
        qs[rows, :] = query * jnp.asarray(HEAD_DIM**-0.5, BF)
        ks[rows, :] = out[:, width : 2 * width].astype(BF)
        vs[rows, pl.ds(0, val)] = (out[:, 2 * width :] + bv_ref[...].astype(F32)).astype(BF)

    own_x.wait()
    own_w.wait()
    for c in range(2):
        project(mine + c * QB)
    for c in range(2):
        far_x[c].wait()
        project(theirs + c * part)

    outs = []

    def local_out(src, dst):
        copy = pltpu.make_async_copy(src, dst, out_sem.at[len(outs)])
        copy.start()
        outs.append(copy)

    local_out(xs, x_out)
    local_out(qs, q_out)
    local_out(ks, k_out)

    far_seg.wait()
    for c in range(tokens // LANES):
        row = segrow[0:1, c * LANES : (c + 1) * LANES].astype(F32)
        segcol[c * LANES : (c + 1) * LANES, :] = jnp.broadcast_to(row, (LANES, LANES)).T
    for j in range(steps):
        key = segcol[j * QB : (j + 1) * QB, :]
        key = jnp.concatenate([key] * (QB // LANES), axis=1)
        for i in range(j, steps):
            query = segrow[0:1, i * QB : (i + 1) * QB].astype(F32)
            seen = (key == query) & (query >= 0.0)
            if i == j:
                down = lax.broadcasted_iota(jnp.int32, (QB, QB), 0)
                across = lax.broadcasted_iota(jnp.int32, (QB, QB), 1)
                seen = (seen & (down <= across)) | (down == across)
            bias[j * QB : (j + 1) * QB, i * QB : (i + 1) * QB] = jnp.where(seen, 0.0, NEG)
        cut = (pl.ds(j * QB, QB), pl.ds(j * QB, tokens - j * QB))
        local_out(bias.at[cut], bias_out.at[cut])
    own_fv.wait()
    far_fv.wait()
    local_out(vs, v_out)

    low = lax.broadcasted_iota(jnp.int32, (1, LANES), 1) < HEAD_DIM

    @pl.loop(0, PAIRS)
    def _(p):
        cols = pl.ds(pl.multiple_of(p * LANES, LANES), LANES)
        k = ks[:, cols]
        v = vs[:, cols]

        def score(i, h):
            q = qs[i * QB : (i + 1) * QB, cols]
            q = jnp.where(low if h == 0 else ~low, q, jnp.zeros_like(q))
            span = (i + 1) * QB
            return nt(k[:span], q) + bias[:span, i * QB : span]

        done = {}

        def finish(i, h, s):
            span = (i + 1) * QB
            top = jnp.max(s, axis=0, keepdims=True)
            e = jnp.exp(s - top)
            total = jnp.sum(e, axis=0, keepdims=True)
            done[h] = tn((e * (1.0 / total)).astype(BF), v[:span])
            lse_ref[p, h : h + 1, i * QB : span] = top + jnp.log(total)
            if h == 1:
                atts[i * QB : span, cols] = jnp.where(low, done[0], done[1]).astype(BF)

        waiting = []
        for i in range(steps):
            for h in range(2):
                waiting.append((i, h, score(i, h)))
                if len(waiting) > 2:
                    finish(*waiting.pop(0))
        for item in waiting:
            finish(*item)

    local_out(atts, att_out)
    own_wo.wait()
    for c in range(steps):
        rows = slice(c * QB, (c + 1) * QB)
        middle = xs[rows, :].astype(F32) + nn(atts[rows, :], wout[...]) + bout_ref[...].astype(F32)
        mids[rows, :] = middle
        xhat, _ = norm_parts(middle)
        act2s[rows, :] = (xhat * g2_ref[...].astype(F32) + b2_ref[...].astype(F32)).astype(BF)
    local_out(mids, mid_out)
    local_out(act2s, act2_out)
    for copy in outs:
        copy.wait()
    own_cot.wait()
    far_cot.wait()


def front(x, fv, seg, cot, g1, b1, wqkv, bq, bv, wout, bout, g2, b2):
    half, width, val = x.shape[1], x.shape[2], fv.shape[2]
    tokens = 2 * half
    hbm = pl.BlockSpec(memory_space=pl.ANY)
    vmem = pl.BlockSpec(memory_space=pltpu.VMEM)
    flat = jax.ShapeDtypeStruct((tokens, width), BF)
    shape = jax.ShapeDtypeStruct
    return pl.pallas_call(
        front_kernel,
        in_specs=[hbm, hbm, vmem, hbm, vmem, vmem, hbm, vmem, vmem, hbm, vmem, vmem, vmem],
        out_specs=[hbm] * 7 + [vmem] + [hbm] * 2,
        out_shape=[
            flat,
            flat,
            flat,
            flat,
            flat,
            flat,
            shape((tokens, width), F32),
            shape((PAIRS, 2, tokens), F32),
            shape((tokens, tokens), F32),
            flat,
        ],
        scratch_shapes=[
            pltpu.VMEM((tokens, width), BF),
            pltpu.VMEM((tokens, width), BF),
            pltpu.VMEM((tokens, width), BF),
            pltpu.VMEM((tokens, width), BF),
            pltpu.VMEM((tokens, width), BF),
            pltpu.VMEM((tokens, width), BF),
            pltpu.VMEM((tokens, width), F32),
            pltpu.VMEM((tokens, tokens), F32),
            pltpu.VMEM(wqkv.shape, BF),
            pltpu.VMEM(wout.shape, BF),
            pltpu.VMEM((8, tokens), jnp.int32),
            pltpu.VMEM((8, half), jnp.int32),
            pltpu.VMEM((tokens, LANES), F32),
            pltpu.SemaphoreType.DMA((5,)),
            pltpu.SemaphoreType.DMA((7 + tokens // QB,)),
            pltpu.SemaphoreType.DMA((5,)),
            pltpu.SemaphoreType.DMA((5,)),
        ],
        compiler_params=pltpu.CompilerParams(
            collective_id=0, has_side_effects=True, vmem_limit_bytes=56 * MIB
        ),
        name="front",
    )(x, fv, seg, cot, g1, b1, wqkv, bq, bv, wout, bout, g2, b2)


def feed_kernel(
    act2,
    cot,
    mid,
    att,
    g2_ref,
    bproj_ref,
    wout,
    wfc,
    bfc_ref,
    wproj,
    lout,
    gmid,
    gatt,
    dots,
    dwout,
    fc_half,
    proj_half,
    fc_last,
    proj_last,
    dbfc,
    small,
    acc,
    dact,
    act2t,
    hid,
    dpre,
    sel,
    gf,
    gp,
    rf0,
    rp0,
    rf1,
    rp1,
    send_sem,
    recv_sem,
    out_sem,
):
    t = pl.program_id(0)
    last = pl.num_programs(0) - 1
    tokens, width = act2.shape
    tile = hid.shape[1]
    steps = tokens // QB
    _, core, x, _, _ = spot()
    friends = partners()[:2]

    def core_copies(n):
        return [
            push(
                gf.at[n, :, :, 1 - core],
                rf0.at[n],
                send_sem.at[0, n],
                recv_sem.at[0, n],
                friends[0],
            ),
            push(
                gp.at[n, :, 1 - core],
                rp0.at[n],
                send_sem.at[1, n],
                recv_sem.at[1, n],
                friends[0],
            ),
        ]

    def x_copies(n):
        return [
            push(
                gf.at[n, :, 1 - x, core],
                rf1.at[n],
                send_sem.at[2, n],
                recv_sem.at[2, n],
                friends[1],
            ),
            push(
                gp.at[n, 1 - x, core],
                rp1.at[n],
                send_sem.at[3, n],
                recv_sem.at[3, n],
                friends[1],
            ),
        ]

    def core_done(n):
        for copy in core_copies(n):
            copy.wait()
        for b in range(2):
            add_into(gp.at[n, b, core], rp0.at[n, b])
            for a in range(4):
                add_into(gf.at[n, a, b, core], rf0.at[n, a, b])
        for copy in x_copies(n):
            copy.start()

    def out_copies(n):
        return [
            pltpu.make_async_copy(gp.at[n, x, core], proj_half.at[n], out_sem.at[0, n]),
            pltpu.make_async_copy(
                gf.at[n, :, x, core],
                fc_half.at[:, :, pl.ds(pl.multiple_of(n * tile, tile), tile)],
                out_sem.at[1, n],
            ),
        ]

    def x_done(n):
        for copy in x_copies(n):
            copy.wait()
        add_into(gp.at[n, x, core], rp1.at[n])
        for a in range(4):
            add_into(gf.at[n, a, x, core], rf1.at[n, a])
        for copy in out_copies(n):
            copy.start()

    @pl.when(t == 0)
    def _():
        greet(friends)
        act2t[...] = act2[...].T
        acc[...] = jnp.zeros_like(acc)
        dact[...] = jnp.zeros_like(dact)
        head = lax.broadcasted_iota(jnp.int32, sel.shape, 0)
        feature = lax.broadcasted_iota(jnp.int32, sel.shape, 1)
        inside = (feature >= head * HEAD_DIM) & (feature < (head + 1) * HEAD_DIM)
        sel[...] = jnp.where(inside, 1.0, 0.0).astype(BF)

    total = None
    for c in range(steps):
        rows = slice(c * QB, (c + 1) * QB)
        u = nn(act2[rows, :], wfc[...]) + bfc_ref[...].astype(F32)
        square = u * u
        bend = jnp.tanh(u * (0.7978845608028654 + (0.7978845608028654 * 0.044715) * square))
        halfway = 0.5 + 0.5 * bend
        hidden = (u * halfway).astype(BF)
        hid[rows, :] = hidden
        acc[rows, :] += nn(hidden, wproj[...])
        slope = halfway + (u * (0.5 - 0.5 * bend * bend)) * (
            0.7978845608028654 + (3 * 0.7978845608028654 * 0.044715) * square
        )
        grad = (nt(cot[rows, :], wproj[...]) * slope).astype(BF)
        dpre[rows, :] = grad
        dact[rows, :] += nt(grad, wfc[...])
        part = column_sum(grad.astype(F32))
        total = part if total is None else total + part
        if c == 1:

            @pl.when(t >= 1)
            def _():
                core_done(t - 1)

    dbfc[...] = total

    @pl.when(t >= 2)
    def _():
        x_done(t - 2)

    dproj = tn(hid[...], cot[...]).astype(BF)
    dfc = nn(act2t[...], dpre[...]).astype(BF)

    @pl.when(t < last)
    def _():
        gp[t] = dproj.reshape(gp.shape[1:])
        gf[t] = dfc.reshape(gf.shape[1:])
        for copy in core_copies(t):
            copy.start()

    @pl.when(t == last)
    def _():
        proj_last[...] = dproj.reshape(proj_last.shape)
        fc_last[...] = dfc.reshape(fc_last.shape)
        gain = g2_ref[...].astype(F32)
        sums = [None] * 4
        for c in range(steps):
            rows = slice(c * QB, (c + 1) * QB)
            middle = mid[rows, :]
            upstream = cot[rows, :].astype(F32)
            lout[rows, :] = (middle + acc[rows, :] + bproj_ref[...].astype(F32)).astype(BF)
            xhat, inverse = norm_parts(middle)
            da = dact[rows, :]
            grad_middle = upstream + norm_pull(da, xhat, inverse, gain)
            gmid[rows, :] = grad_middle
            branch = grad_middle.astype(BF)
            hid[rows, :width] = branch
            parts = [
                column_sum(upstream),
                column_sum(da * xhat),
                column_sum(da),
                column_sum(branch.astype(F32)),
            ]
            sums = [b if a is None else a + b for a, b in zip(sums, parts)]
            ga = nt(branch, wout[...]).astype(BF)
            gatt[rows, :] = ga
            product = ga.astype(F32) * att[rows, :].astype(F32)
            big = product.astype(BF)
            rest = (product - big.astype(F32)).astype(BF)
            both = nt(sel[...], big) + nt(sel[...], rest)
            for p in range(PAIRS):
                dots[p, :, rows] = both[2 * p : 2 * p + 2, :]
        small[...] = jnp.concatenate(sums, axis=0)
        dwout[...] = tn(att[...], hid[:, :width]).astype(BF).reshape(dwout.shape)
        x_done(t - 1)
        for n in range(gp.shape[0]):
            for copy in out_copies(n):
                copy.wait()


def feed(act2, cot, mid, att, g2, bproj, wout, wfc, bfc, wproj):
    tokens, width = act2.shape
    ff = wfc.shape[1]
    tiles = 4
    tile = ff // tiles
    owner = width // 16
    owner_ff = ff // 16
    shape = jax.ShapeDtypeStruct
    flat = shape((tokens, width), BF)
    once = pl.Buffered(1)
    hbm = pl.BlockSpec(memory_space=pl.ANY)

    def whole(s):
        return pl.BlockSpec(s, lambda t: (0,) * len(s), pipeline_mode=once)

    rows = whole((tokens, width))
    line = whole((1, width))
    return pl.pallas_call(
        feed_kernel,
        grid=(tiles,),
        in_specs=[
            rows,
            rows,
            rows,
            rows,
            line,
            line,
            whole(wout.shape),
            pl.BlockSpec((width, tile), lambda t: (0, t)),
            pl.BlockSpec((1, tile), lambda t: (0, t)),
            pl.BlockSpec((tile, width), lambda t: (t, 0)),
        ],
        out_specs=[
            rows,
            rows,
            rows,
            whole((PAIRS, 2, tokens)),
            whole((2, 2, 2, 2, owner, width)),
            hbm,
            hbm,
            whole((2, 2, 2, 2, owner, tile)),
            whole((2, 2, owner_ff, width)),
            pl.BlockSpec((1, tile), lambda t: (0, t)),
            whole((4, width)),
        ],
        out_shape=[
            flat,
            shape((tokens, width), F32),
            flat,
            shape((PAIRS, 2, tokens), F32),
            shape((2, 2, 2, 2, owner, width), BF),
            shape((4, owner, ff - tile), BF),
            shape((tiles - 1, owner_ff, width), BF),
            shape((2, 2, 2, 2, owner, tile), BF),
            shape((2, 2, owner_ff, width), BF),
            shape((1, ff), F32),
            shape((4, width), F32),
        ],
        scratch_shapes=[
            pltpu.VMEM((tokens, width), F32),
            pltpu.VMEM((tokens, width), F32),
            pltpu.VMEM((width, tokens), BF),
            pltpu.VMEM((tokens, tile), BF),
            pltpu.VMEM((tokens, tile), BF),
            pltpu.VMEM((16, width), BF),
            pltpu.VMEM((tiles - 1, 4, 2, 2, owner, tile), BF),
            pltpu.VMEM((tiles - 1, 2, 2, owner_ff, width), BF),
            pltpu.VMEM((tiles - 1, 4, 2, owner, tile), BF),
            pltpu.VMEM((tiles - 1, 2, owner_ff, width), BF),
            pltpu.VMEM((tiles - 1, 4, owner, tile), BF),
            pltpu.VMEM((tiles - 1, owner_ff, width), BF),
            pltpu.SemaphoreType.DMA((4, tiles - 1)),
            pltpu.SemaphoreType.DMA((4, tiles - 1)),
            pltpu.SemaphoreType.DMA((2, tiles - 1)),
        ],
        compiler_params=pltpu.CompilerParams(
            collective_id=1, has_side_effects=True, vmem_limit_bytes=60 * MIB
        ),
        name="feed",
    )(act2, cot, mid, att, g2, bproj, wout, wfc, bfc, wproj)


class Sum:
    def __init__(self, held, got, first, send_sem, recv_sem):
        self.held, self.got, self.first = held, got, first
        self.send_sem, self.recv_sem = send_sem, recv_sem

    def places(self, stage):
        _, core, x, near, far = spot()
        own = [far, near, x, core]
        bits = len(self.held.shape) - 2
        own = own[4 - (4 if self.first == 0 else 2) :] if bits == 4 else own[:2]
        return own[:bits]

    def cut(self, stage, keep):
        own = self.places(stage)
        bits = len(own)
        if stage == 4:
            return tuple(own)
        at = (3 - stage) if bits == 4 else (1 - (stage - 2))
        pick = own[at] if keep else 1 - own[at]
        return (slice(None),) * at + (pick,) + tuple(own[at + 1 :])

    def copy(self, stage):
        return push(
            self.held.at[self.cut(stage, False)],
            self.got[stage - self.first],
            self.send_sem.at[stage],
            self.recv_sem.at[stage],
            partners()[stage],
        )

    def start(self, stage):
        self.copy(stage).start()

    def take(self, stage):
        self.copy(stage).wait()
        mine = self.held.at[self.cut(stage, True)]
        came = self.got[stage - self.first]
        lead = came.shape[:-2]
        count = 1
        for size in lead:
            count *= size
        for n in range(count):
            at = []
            for size in reversed(lead):
                at.insert(0, n % size)
                n //= size
            at = tuple(at)
            add_into(mine.at[at] if at else mine, came.at[at] if at else came)
        self.start(stage + 1)

    def result(self):
        self.copy(4).wait()
        return self.held[self.cut(4, True)].astype(F32) + self.got[4 - self.first][...].astype(F32)


def tail_kernel(
    q_in,
    k_in,
    v_in,
    do_in,
    bias_in,
    x_in,
    gmid_in,
    wqkv_in,
    lout_in,
    dwout_in,
    fch_in,
    ph_in,
    fc3_in,
    p3_in,
    lse_ref,
    d_ref,
    g1_ref,
    b1_ref,
    dbfc_ref,
    small_in,
    lout_out,
    gx_out,
    gf_out,
    wqkv_out,
    wout_out,
    wfc_out,
    wproj_out,
    small_out,
    q_ref,
    k_ref,
    v_ref,
    do_ref,
    bias,
    xs,
    gmid,
    wqkv,
    dqk,
    dvs,
    gfs,
    dqa,
    act1,
    act1t,
    gx,
    g_out,
    g_fch,
    g_ph,
    g_fc3,
    g_p3,
    g_q1,
    g_q2,
    o0, o1, o2, o3, o4,
    h2, h3, h4,
    p2, p3, p4,
    f0, f1, f2, f3, f4,
    t0, t1,
    a0, a1, a2, a3, a4,
    b0, b1, b2, b3, b4,
    sums,
    s_got,
    in_sem,
    out_sem,
    back_send,
    back_recv,
    sum_send,
    sum_recv,
):
    tokens, width = q_ref.shape
    half = tokens // 2
    val = gfs.shape[1]
    steps = tokens // QB
    me = lax.axis_index("blk")
    mine = pl.multiple_of(me * half, half)
    theirs = pl.multiple_of((1 - me) * half, half)
    _, core, x, near, far = spot()
    friends = partners()

    loads = [
        pltpu.make_async_copy(src, dst, in_sem.at[n])
        for n, (src, dst) in enumerate(
            [
                (q_in, q_ref),
                (k_in, k_ref),
                (v_in, v_ref),
                (do_in, do_ref),
                (bias_in, bias),
                (p3_in, g_p3),
                (fc3_in, g_fc3),
                (dwout_in, g_out),
                (fch_in, g_fch),
                (ph_in.at[0:2], g_ph.at[0]),
                (ph_in.at[2], g_ph.at[1, 0]),
                (x_in, xs),
                (wqkv_in, wqkv),
                (gmid_in, gmid),
            ]
        )
    ]
    for load in loads:
        load.start()
    greet(friends)

    s_out = Sum(g_out, [o0, o1, o2, o3, o4], 0, sum_send.at[0], sum_recv.at[0])
    s_fch = Sum(g_fch, [h2, h3, h4], 2, sum_send.at[1], sum_recv.at[1])
    s_ph = Sum(g_ph, [p2, p3, p4], 2, sum_send.at[2], sum_recv.at[2])
    s_fc3 = Sum(g_fc3, [f0, f1, f2, f3, f4], 0, sum_send.at[3], sum_recv.at[3])
    s_q1 = Sum(g_q1, [a0, a1, a2, a3, a4], 0, sum_send.at[4], sum_recv.at[4])
    s_q2 = Sum(g_q2, [b0, b1, b2, b3, b4], 0, sum_send.at[5], sum_recv.at[5])

    def p3_copy(stage):
        src = g_p3.at[:, 1 - core] if stage == 0 else g_p3.at[1 - x, core]
        return push(
            src, t0 if stage == 0 else t1, sum_send.at[6, stage], sum_recv.at[6, stage], friends[stage]
        )

    def small_copy(stage):
        return push(
            sums.at[stage], s_got.at[stage], sum_send.at[7, stage], sum_recv.at[7, stage], friends[stage]
        )

    def give_back(n, src, dst):
        return push(src, dst, back_send.at[n], back_recv.at[n], friends[4])

    back_lout = give_back(0, lout_in.at[pl.ds(theirs, half)], lout_out.at[me])
    back_lout.start()
    keep_lout = pltpu.make_async_copy(lout_in.at[pl.ds(mine, half)], lout_out.at[me], out_sem.at[0])
    keep_lout.start()

    for n in (5, 6, 7):
        loads[n].wait()
    p3_copy(0).start()
    s_fc3.start(0)
    s_out.start(0)
    loads[8].wait()
    s_fch.start(2)
    loads[11].wait()
    gain = g1_ref[...].astype(F32)
    shift = b1_ref[...].astype(F32)
    for c in range(steps):
        rows = slice(c * QB, (c + 1) * QB)
        xhat, _ = norm_parts(xs[rows, :].astype(F32))
        act1[rows, :] = (xhat * gain + shift).astype(BF)
    act1t[...] = act1[...].T
    for n in range(5):
        loads[n].wait()

    low = lax.broadcasted_iota(jnp.int32, (1, LANES), 1) < HEAD_DIM
    masks = [low, ~low]
    zero = jnp.zeros((), BF)

    def split(value, store):
        store[...] = value.astype(BF).reshape(store.shape)

    @pl.loop(0, PAIRS)
    def _(p):
        @pl.when(p == 1)
        def _():
            p3_copy(0).wait()
            for b in range(2):
                add_into(g_p3.at[b, core], t0.at[b])
            p3_copy(1).start()
            s_fc3.take(0)
            s_out.take(0)

        @pl.when(p == 3)
        def _():
            s_fch.take(2)
            g1 = g_q1.shape[-1] // 3
            for n, grad in enumerate([dqk[:, 0:g1], dqk[:, width : width + g1], dvs[...]]):
                g_q1[:, :, :, :, :, n * g1 : (n + 1) * g1] = (
                    nn(act1t[...], grad).astype(BF).reshape(g_q1.shape[:-1] + (g1,))
                )
            s_q1.start(0)

        @pl.when(p == 4)
        def _():
            s_q1.take(0)
            p3_copy(1).wait()
            loads[9].wait()
            loads[10].wait()
            g_ph[1, 1] = (g_p3[x, core].astype(F32) + t1[...].astype(F32)).astype(BF)
            s_ph.start(2)

        @pl.when(p == 5)
        def _():
            s_fch.take(3)
            s_fc3.take(1)
            s_out.take(1)

        cols = pl.ds(pl.multiple_of(p * LANES, LANES), LANES)
        kcols = pl.ds(pl.multiple_of(width + p * LANES, LANES), LANES)
        q, k, v, do = q_ref[:, cols], k_ref[:, cols], v_ref[:, cols], do_ref[:, cols]
        qm = [jnp.where(m, q, zero) for m in masks]
        km = [jnp.where(m, k, zero) for m in masks]
        dom = [jnp.where(m, do, zero) for m in masks]
        dvals = []
        for j in range(steps):
            a = j * QB
            keys = slice(a, a + QB)
            dk = dv = dq = None
            for h in range(2):
                s = nt(k[keys], qm[h][a:]) + bias[keys, a:]
                probs = jnp.exp(s - lse_ref[p, h : h + 1, a:])
                dp = nt(v[keys], dom[h][a:])
                ds = (probs * (dp - d_ref[p, h : h + 1, a:])).astype(BF)
                dvh = nn(probs.astype(BF), dom[h][a:])
                dkh = nn(ds, qm[h][a:])
                dqh = tn(ds, km[h][keys])
                dk = dkh if dk is None else dk + dkh
                dv = dvh if dv is None else dv + dvh
                dq = dqh if dq is None else dq + dqh
            dqk[keys, kcols] = dk.astype(BF)
            dvals.append(dv.astype(BF))
            if j == 0:
                dqa[...] = dq
            else:
                dqa[a:, :] += dq
        dqk[:, cols] = (dqa[...] * HEAD_DIM**-0.5).astype(BF)

        @pl.when(p < PAIRS // 2)
        def _():
            for j in range(steps):
                dvs[j * QB : (j + 1) * QB, cols] = dvals[j]

        @pl.when(p >= PAIRS // 2)
        def _():
            late = pl.ds(pl.multiple_of(p * LANES - val, LANES), LANES)
            for j in range(steps):
                gfs[j * QB : (j + 1) * QB, late] = dvals[j]

    g2 = g_q2.shape[-1] // 2
    for n, grad in enumerate([dqk[:, width - g2 : width], dqk[:, 2 * width - g2 :]]):
        g_q2[:, :, :, :, :, n * g2 : (n + 1) * g2] = (
            nn(act1t[...], grad).astype(BF).reshape(g_q2.shape[:-1] + (g2,))
        )
    s_q2.start(0)
    back_gf = give_back(1, gfs.at[pl.ds(theirs, half)], gf_out.at[me])
    back_gf.start()
    keep_gf = pltpu.make_async_copy(gfs.at[pl.ds(mine, half)], gf_out.at[me], out_sem.at[1])
    keep_gf.start()
    loads[12].wait()
    loads[13].wait()
    s_q1.take(1)

    totals = [None] * 4

    def input_grad(start):
        rows = pl.ds(pl.multiple_of(start, QB), QB)
        da = nt(dqk[rows, :], wqkv[:, : 2 * width]) + nt(dvs[rows, :], wqkv[:, 2 * width :])
        xhat, inverse = norm_parts(xs[rows, :].astype(F32))
        gx[rows, :] = (gmid[rows, :] + norm_pull(da, xhat, inverse, gain)).astype(BF)
        bv = column_sum(dvs[rows, :].astype(F32))
        parts = [
            column_sum(da * xhat),
            column_sum(da),
            column_sum(dqk[rows, :width].astype(F32)),
            jnp.concatenate([bv, jnp.zeros((1, width - val), F32)], axis=1),
        ]
        totals[:] = [b if a is None else a + b for a, b in zip(totals, parts)]

    backs = []
    for c in range(half // QB):
        start = pl.multiple_of(theirs + c * QB, QB)
        input_grad(start)
        copy = give_back(2 + c, gx.at[pl.ds(start, QB)], gx_out.at[me, pl.ds(c * QB, QB)])
        copy.start()
        backs.append(copy)
        if c == 0:
            s_q2.take(0)
    for c in range(half // QB):
        input_grad(mine + c * QB)
    keep_gx = pltpu.make_async_copy(gx.at[pl.ds(mine, half)], gx_out.at[me], out_sem.at[2])
    keep_gx.start()
    wide = [dbfc_ref[:, n * width : (n + 1) * width] for n in range(4)]
    sums[0] = jnp.concatenate(
        [small_in[...]] + totals + wide + [jnp.zeros((4, width), F32)], axis=0
    )
    small_copy(0).start()

    s_ph.take(2)
    s_fc3.take(2)
    s_out.take(2)
    s_q1.take(2)

    def small_take(stage):
        small_copy(stage).wait()
        sums[stage + 1] = sums[stage] + s_got[stage]
        if stage < 4:
            small_copy(stage + 1).start()

    small_take(0)
    s_q2.take(1)
    small_take(1)
    s_ph.take(3)
    s_fc3.take(3)
    s_out.take(3)
    s_q1.take(3)
    small_take(2)
    s_q2.take(2)
    small_take(3)
    s_q2.take(3)
    late = wfc_out.shape[1] - g_fc3.shape[-1]
    wfc_out[:, :late] = s_fch.result()
    wproj_out[...] = s_ph.result()
    wfc_out[:, late:] = s_fc3.result()
    wout_out[...] = s_out.result()
    part = s_q1.result()
    for n, at in enumerate([0, width, 2 * width]):
        wqkv_out[:, at : at + g1_size(g_q1)] = part[:, n * g1_size(g_q1) : (n + 1) * g1_size(g_q1)]
    small_take(4)
    small_out[...] = sums[5]
    part = s_q2.result()
    for n, at in enumerate([width - g2, 2 * width - g2]):
        wqkv_out[:, at : at + g2] = part[:, n * g2 : (n + 1) * g2]
    back_lout.wait()
    back_gf.wait()
    for copy in backs:
        copy.wait()
    keep_lout.wait()
    keep_gf.wait()
    keep_gx.wait()


def g1_size(ref):
    return ref.shape[-1] // 3


def tail(q, k, v, do, bias, x, gmid, wqkv, lout, dwout, fch, ph, fc3, p3, lse, dots, g1, b1, dbfc, small):
    tokens, width = q.shape
    half = tokens // 2
    val = wqkv.shape[1] - 2 * width
    owner = width // 16
    owner_ff = dbfc.shape[1] // 16
    ff = dbfc.shape[1]
    shape = jax.ShapeDtypeStruct
    hbm = pl.BlockSpec(memory_space=pl.ANY)
    vmem = pl.BlockSpec(memory_space=pltpu.VMEM)

    def vm(*s):
        return pltpu.VMEM(s, BF)

    def chain(rows, cols):
        return [
            vm(2, 2, 2, rows, cols),
            vm(2, 2, rows, cols),
            vm(2, rows, cols),
            vm(rows, cols),
            vm(rows, cols),
        ]

    flat = vm(tokens, width)
    tile = fc3.shape[-1]
    return pl.pallas_call(
        tail_kernel,
        in_specs=[hbm] * 14 + [vmem] * 6,
        out_specs=[hbm] * 3 + [vmem] * 5,
        out_shape=[
            shape((2, half, width), BF),
            shape((2, half, width), BF),
            shape((2, half, val), BF),
            shape((owner, wqkv.shape[1]), F32),
            shape((owner, width), F32),
            shape((owner, ff), F32),
            shape((owner_ff, width), F32),
            shape((16, width), F32),
        ],
        scratch_shapes=[
            flat,
            flat,
            flat,
            flat,
            pltpu.VMEM((tokens, tokens), F32),
            flat,
            pltpu.VMEM((tokens, width), F32),
            vm(*wqkv.shape),
            vm(tokens, 2 * width),
            vm(tokens, val),
            vm(tokens, val),
            pltpu.VMEM((tokens, LANES), F32),
            flat,
            vm(width, tokens),
            flat,
            vm(*dwout.shape),
            vm(2, 2, owner, ff - tile),
            vm(2, 2, owner_ff, width),
            vm(*fc3.shape),
            vm(*p3.shape),
            vm(2, 2, 2, 2, owner, 3 * val),
            vm(2, 2, 2, 2, owner, 2 * (width - val)),
        ]
        + chain(owner, width)
        + chain(owner, ff - tile)[2:]
        + chain(owner_ff, width)[2:]
        + chain(owner, tile)
        + [vm(2, owner_ff, width), vm(owner_ff, width)]
        + chain(owner, 3 * val)
        + chain(owner, 2 * (width - val))
        + [
            pltpu.VMEM((6, 16, width), F32),
            pltpu.VMEM((5, 16, width), F32),
            pltpu.SemaphoreType.DMA((14,)),
            pltpu.SemaphoreType.DMA((3,)),
            pltpu.SemaphoreType.DMA((4,)),
            pltpu.SemaphoreType.DMA((4,)),
            pltpu.SemaphoreType.DMA((8, 5)),
            pltpu.SemaphoreType.DMA((8, 5)),
        ],
        compiler_params=pltpu.CompilerParams(
            collective_id=2, has_side_effects=True, vmem_limit_bytes=62 * MIB
        ),
        name="tail",
    )(
        q, k, v, do, bias, x, gmid, wqkv, lout, dwout, fch, ph, fc3, p3, lse, dots, g1, b1, dbfc, small
    )


def paired(
    inputs,
    first_values,
    segments,
    ln1_gain,
    first_norm_bias,
    w_qkv,
    b_query,
    b_value,
    w_out,
    b_out,
    ln2_gain,
    second_norm_bias,
    w_fc,
    b_fc,
    w_proj,
    b_proj,
    cotangent,
):
    half, width = inputs.shape[1], inputs.shape[2]
    val = first_values.shape[2]
    line = lambda a: a.reshape(1, -1)
    x, q, k, v, att, act2, mid, lse, bias, cot = front(
        inputs,
        first_values,
        segments,
        cotangent,
        line(ln1_gain),
        line(first_norm_bias),
        w_qkv,
        line(b_query),
        line(b_value),
        w_out,
        line(b_out),
        line(ln2_gain),
        line(second_norm_bias),
    )
    lout, gmid, gatt, dots, dwout, fch, ph, fc3, p3, dbfc, small = feed(
        act2, cot, mid, att, line(ln2_gain), line(b_proj), w_out, w_fc, line(b_fc), w_proj
    )
    owner = width // 16
    layer_out, grad_inputs, grad_first, gwqkv, gwout, gwfc, gwproj, sums = tail(
        q,
        k,
        v,
        gatt,
        bias,
        x,
        gmid,
        w_qkv,
        lout,
        dwout,
        fch.reshape((2, 2) + fch.shape[1:]),
        ph,
        fc3,
        p3,
        lse,
        dots,
        line(ln1_gain),
        line(first_norm_bias),
        dbfc,
        small,
    )
    index = lax.axis_index("batch")

    def share(row, size):
        return lax.dynamic_slice_in_dim(row, index * size, size)

    return (
        layer_out,
        grad_inputs,
        grad_first,
        share(sums[4], owner),
        share(sums[5], owner),
        gwqkv,
        share(sums[6], owner),
        share(sums[7], val // 16),
        gwout,
        share(sums[3], owner),
        share(sums[1], owner),
        share(sums[2], owner),
        gwfc,
        share(sums[8:12].reshape(-1), w_fc.shape[1] // 16),
        gwproj,
        share(sums[0], owner),
    )


MICRO = 2


def as_sent(shard):
    return jax.tree.map(lambda a: a.astype(jnp.bfloat16) if a.dtype == jnp.float32 else a, shard)


def apply_norm(values_in, norm_gain, shift_bias):
    mean_val = jnp.mean(values_in, axis=-1, keepdims=True)
    centred_rows = values_in - mean_val
    inverse_deviation = lax.rsqrt(
        jnp.mean(centred_rows * centred_rows, axis=-1, keepdims=True) + EPS
    )
    standardized = centred_rows * inverse_deviation
    return (standardized * norm_gain + shift_bias, standardized, inverse_deviation)


def apply_norm_backward(upstream_gradient, standardized, inverse_deviation, norm_gain):
    scaled_rows = upstream_gradient * norm_gain
    first_average = jnp.mean(scaled_rows, axis=-1, keepdims=True)
    second_average = jnp.mean(scaled_rows * standardized, axis=-1, keepdims=True)
    incoming_gradient = inverse_deviation * (
        scaled_rows - first_average - standardized * second_average
    )
    return (
        incoming_gradient,
        jnp.sum(upstream_gradient * standardized, axis=(0, 1)),
        jnp.sum(upstream_gradient, axis=(0, 1)),
    )


def gelu_tanh(values_in):
    cubic = values_in + 0.044715 * values_in * values_in * values_in
    return 0.5 * values_in * (1.0 + jnp.tanh(0.7978845608028654 * cubic))


def heads_of(values_in):
    return values_in.reshape(values_in.shape[0], values_in.shape[1], HEADS, HEAD_DIM)


def visible(seg_query, seg_key, query_pos, key_pos):
    same = seg_query[:, :, None] == seg_key[:, None, :]
    causal = key_pos[None, :] <= query_pos[:, None]
    live = seg_query[:, :, None] >= 0
    diagonal = key_pos[None, :] == query_pos[:, None]
    return (same & causal[None] & live | diagonal[None])[:, :, None, :]


def score_block(query4, key4, mask):
    raw = jnp.einsum("rqhd,rkhd->rqhk", query4, key4, preferred_element_type=jnp.float32)
    return jnp.where(mask, raw * HEAD_DIM ** (-0.5), NEG)


def grad_block(query4, key4, value4, dout4, log_total, out_dot, mask):
    probs = jnp.where(mask, jnp.exp(score_block(query4, key4, mask) - log_total[..., None]), 0.0)
    probs_low = probs.astype(jnp.bfloat16)
    grad_probs = jnp.einsum("rqhd,rkhd->rqhk", dout4, value4, preferred_element_type=jnp.float32)
    grad_scores = (probs * (grad_probs - out_dot[..., None]) * HEAD_DIM ** (-0.5)).astype(
        jnp.bfloat16
    )
    return (probs_low, grad_scores)


def spread(
    inputs,
    first_values,
    segments,
    ln1_gain,
    first_norm_bias,
    w_qkv,
    b_query,
    b_value,
    w_out,
    b_out,
    ln2_gain,
    second_norm_bias,
    w_fc,
    b_fc,
    w_proj,
    b_proj,
    cotangent,
):
    all_seg = lax.all_gather(segments, "blk", axis=1, tiled=True)
    block_len = inputs.shape[1]
    model_width = inputs.shape[2]
    val_width = first_values.shape[2]
    rows_mb = inputs.shape[0] // MICRO
    own_pos = lax.axis_index("blk") * block_len + jnp.arange(block_len)
    first_gain = ln1_gain.astype(jnp.float32)
    second_gain = ln2_gain.astype(jnp.float32)
    outputs = []
    input_grads = []
    first_grads = []
    totals = None
    for micro_step in range(MICRO):
        first_row = micro_step * rows_mb
        last_row = first_row + rows_mb
        residual_stream = inputs[first_row:last_row].astype(jnp.float32)
        first_part = first_values[first_row:last_row]
        seg_local = segments[first_row:last_row]
        seg_row = all_seg[first_row:last_row]
        cot_part = cotangent[first_row:last_row]
        first_normed_rows, first_standardized, first_inverse_deviation = apply_norm(
            residual_stream, first_gain, first_norm_bias.astype(jnp.float32)
        )
        act1 = first_normed_rows.astype(jnp.bfloat16)
        projected = jnp.einsum("rbd,de->rbe", act1, w_qkv, preferred_element_type=jnp.float32)
        queries = (projected[..., :model_width] + b_query.astype(jnp.float32)).astype(jnp.bfloat16)
        keys_low = projected[..., model_width : 2 * model_width].astype(jnp.bfloat16)
        fresh = (projected[..., 2 * model_width :] + b_value.astype(jnp.float32)).astype(
            jnp.bfloat16
        )
        values_low = jnp.concatenate([fresh, first_part], axis=-1)
        query4 = heads_of(queries)
        key_part = lax.all_gather(keys_low, "blk", axis=1, tiled=True)
        value_part = lax.all_gather(values_low, "blk", axis=1, tiled=True)
        span = key_part.shape[1]
        key_pos = jnp.arange(span)
        mask = visible(seg_local, seg_row, own_pos, key_pos)
        scores = score_block(query4, heads_of(key_part), mask)
        old_max = jnp.full((rows_mb, block_len, HEADS), NEG, jnp.float32)
        new_max = jnp.maximum(old_max, jnp.max(scores, axis=-1))
        weights = jnp.where(mask, jnp.exp(scores - new_max[..., None]), 0.0)
        new_sum = jnp.sum(weights, axis=-1)
        new_acc = jnp.einsum(
            "rqhk,rkhd->rqhd",
            weights.astype(jnp.bfloat16),
            heads_of(value_part),
            preferred_element_type=jnp.float32,
        )
        attention4 = new_acc / new_sum[..., None]
        log_total = new_max + jnp.log(new_sum)
        attention_low = attention4.reshape(rows_mb, block_len, model_width).astype(jnp.bfloat16)
        branch = jnp.einsum("rbd,de->rbe", attention_low, w_out, preferred_element_type=jnp.float32)
        middle_state = residual_stream + branch + b_out.astype(jnp.float32)
        second_normed_rows, second_standardized, second_inverse_deviation = apply_norm(
            middle_state, second_gain, second_norm_bias.astype(jnp.float32)
        )
        act2 = second_normed_rows.astype(jnp.bfloat16)
        pre_gelu = jnp.einsum(
            "rbd,df->rbf", act2, w_fc, preferred_element_type=jnp.float32
        ) + b_fc.astype(jnp.float32)
        hidden = gelu_tanh(pre_gelu).astype(jnp.bfloat16)
        result = middle_state + jnp.einsum(
            "rbf,fd->rbd", hidden, w_proj, preferred_element_type=jnp.float32
        )
        result = result + b_proj.astype(jnp.float32)
        outputs.append(result.astype(jnp.bfloat16))
        upstream_gradient = cot_part.astype(jnp.float32)
        grad_wproj = jnp.einsum("rbf,rbd->fd", hidden, cot_part, preferred_element_type=jnp.float32)
        grad_bproj = jnp.sum(upstream_gradient, axis=(0, 1))
        grad_hidden = jnp.einsum(
            "rbd,fd->rbf", cot_part, w_proj, preferred_element_type=jnp.float32
        )
        gelu_value, gelu_pull = jax.vjp(gelu_tanh, pre_gelu)
        grad_pre = gelu_pull(grad_hidden)[0].astype(jnp.bfloat16)
        grad_wfc = jnp.einsum("rbd,rbf->df", act2, grad_pre, preferred_element_type=jnp.float32)
        grad_bfc = jnp.sum(grad_pre.astype(jnp.float32), axis=(0, 1))
        second_activation_gradient = jnp.einsum(
            "rbf,df->rbd", grad_pre, w_fc, preferred_element_type=jnp.float32
        )
        second_norm_gradient, second_gain_gradient, second_bias_gradient = apply_norm_backward(
            second_activation_gradient, second_standardized, second_inverse_deviation, second_gain
        )
        grad_middle = upstream_gradient + second_norm_gradient
        grad_branch = grad_middle.astype(jnp.bfloat16)
        grad_wout = jnp.einsum(
            "rbd,rbe->de", attention_low, grad_branch, preferred_element_type=jnp.float32
        )
        grad_bout = jnp.sum(grad_branch.astype(jnp.float32), axis=(0, 1))
        grad_attention = jnp.einsum(
            "rbe,de->rbd", grad_branch, w_out, preferred_element_type=jnp.float32
        ).astype(jnp.bfloat16)
        dout4 = heads_of(grad_attention)
        out_dot = jnp.sum(dout4.astype(jnp.float32) * attention4, axis=-1)
        back_key_part = lax.all_gather(keys_low, "blk", axis=1, tiled=True)
        back_value_part = lax.all_gather(values_low, "blk", axis=1, tiled=True)
        back_span = back_key_part.shape[1]
        back_key_pos = jnp.arange(back_span)
        back_mask = visible(seg_local, seg_row, own_pos, back_key_pos)
        part_key4 = heads_of(back_key_part)
        probs_low, grad_scores = grad_block(
            query4, part_key4, heads_of(back_value_part), dout4, log_total, out_dot, back_mask
        )
        query_acc = jnp.einsum(
            "rqhk,rkhd->rqhd", grad_scores, part_key4, preferred_element_type=jnp.float32
        )
        key_piece = jnp.einsum(
            "rqhk,rqhd->rkhd", grad_scores, query4, preferred_element_type=jnp.float32
        ).reshape(rows_mb, back_span, model_width)
        value_piece = jnp.einsum(
            "rqhk,rqhd->rkhd", probs_low, dout4, preferred_element_type=jnp.float32
        ).reshape(rows_mb, back_span, model_width)
        query_acc, key_acc, value_acc = (query_acc, key_piece, value_piece)
        grad_keys, grad_values = (
            lax.psum_scatter(
                key_acc.astype(jnp.bfloat16), "blk", scatter_dimension=1, tiled=True
            ).astype(jnp.float32),
            lax.psum_scatter(
                value_acc.astype(jnp.bfloat16), "blk", scatter_dimension=1, tiled=True
            ).astype(jnp.float32),
        )
        grad_query = query_acc.reshape(rows_mb, block_len, model_width)
        grad_qkv = jnp.concatenate(
            [
                grad_query.astype(jnp.bfloat16),
                grad_keys.astype(jnp.bfloat16),
                grad_values[..., :val_width].astype(jnp.bfloat16),
            ],
            axis=-1,
        )
        first_grads.append(grad_values[..., val_width:].astype(jnp.bfloat16))
        grad_wqkv = jnp.einsum("rbd,rbe->de", act1, grad_qkv, preferred_element_type=jnp.float32)
        grad_bquery = jnp.sum(grad_qkv[..., :model_width].astype(jnp.float32), axis=(0, 1))
        grad_bvalue = jnp.sum(grad_qkv[..., 2 * model_width :].astype(jnp.float32), axis=(0, 1))
        first_activation_gradient = jnp.einsum(
            "rbe,de->rbd", grad_qkv, w_qkv, preferred_element_type=jnp.float32
        )
        first_norm_gradient, first_gain_gradient, first_bias_gradient = apply_norm_backward(
            first_activation_gradient, first_standardized, first_inverse_deviation, first_gain
        )
        input_grads.append((grad_middle + first_norm_gradient).astype(jnp.bfloat16))
        gradient_set = (
            first_gain_gradient,
            first_bias_gradient,
            grad_wqkv,
            grad_bquery,
            grad_bvalue,
            grad_wout,
            grad_bout,
            second_gain_gradient,
            second_bias_gradient,
            grad_wfc,
            grad_bfc,
            grad_wproj,
            grad_bproj,
        )
        if totals is None:
            totals = gradient_set
        else:
            totals = tuple((older + newer for older, newer in zip(totals, gradient_set)))
    totals = jax.tree.map(
        lambda part: part.astype(jnp.float32),
        lax.psum_scatter(as_sent(totals), "batch", scatter_dimension=0, tiled=True),
    )
    totals = jax.tree.map(lambda part: part.astype(jnp.float32), lax.psum(as_sent(totals), "blk"))
    return (
        jnp.concatenate(outputs, axis=0),
        jnp.concatenate(input_grads, axis=0),
        jnp.concatenate(first_grads, axis=0),
    ) + tuple(totals)


def layer(inputs, *rest):
    whole_rows = lax.axis_size("blk") == inputs.shape[0] == 2 and inputs.shape[1] == 2 * QB
    whole_rows = whole_rows and lax.axis_size("batch") == 16
    return (paired if whole_rows else spread)(inputs, *rest)


def solution(mesh):
    rows = P("batch", "blk", None)
    flat = P("batch")
    wide = P("batch", None)
    return jax.shard_map(
        layer,
        mesh=mesh,
        in_specs=(rows, rows, P("batch", "blk")) + (P(),) * 13 + (rows,),
        out_specs=(rows, rows, rows)
        + (flat, flat, wide, flat, flat, wide, flat, flat, flat, wide, flat, wide, flat),
        check_vma=False,
    )
```

```python
import functools

import jax
import jax.numpy as jnp
from jax import lax
from jax.experimental import pallas as pl
from jax.experimental.pallas import tpu as pltpu
from jax.sharding import PartitionSpec as P

HEADS = 12
HEAD_DIM = 64
PAIRS = HEADS // 2
LANES = 2 * HEAD_DIM
EPS = 1e-05
NEG = -1e30
QB = 256
F32 = jnp.float32
BF = jnp.bfloat16
MIB = 2**20
MESH = pl.DeviceIdType.MESH


def nn(a, b):
    return lax.dot_general(a, b, (((1,), (0,)), ((), ())), preferred_element_type=F32)


def nt(a, b):
    return lax.dot_general(a, b, (((1,), (1,)), ((), ())), preferred_element_type=F32)


def tn(a, b):
    return lax.dot_general(a, b, (((0,), (0,)), ((), ())), preferred_element_type=F32)


def norm_parts(rows):
    mean = jnp.mean(rows, axis=-1, keepdims=True)
    centred = rows - mean
    inverse = lax.rsqrt(jnp.mean(centred * centred, axis=-1, keepdims=True) + EPS)
    return centred * inverse, inverse


def norm_pull(grad, xhat, inverse, gain):
    scaled = grad * gain
    first = jnp.mean(scaled, axis=-1, keepdims=True)
    second = jnp.mean(scaled * xhat, axis=-1, keepdims=True)
    return inverse * (scaled - first - xhat * second)


def row(ref):
    return ref[...].astype(F32).reshape(1, -1)


def column_sum(rows):
    return jnp.sum(rows, axis=0, keepdims=True)


def spot():
    b = lax.axis_index("batch")
    core = lax.rem(b, 2)
    x = lax.rem(lax.div(b, 2), 2)
    near = lax.rem(lax.div(b, 4), 2)
    far = lax.div(b, 8)
    return b, core, x, near, far


def partners():
    b, core, x, near, far = spot()
    return [
        {"batch": b + 1 - 2 * core},
        {"batch": b + 2 - 4 * x},
        {"batch": b + 4 - 8 * near},
        {"batch": b + 8 - 16 * far},
        {"blk": 1 - lax.axis_index("blk")},
    ]


def greet(friends):
    barrier = pltpu.get_barrier_semaphore()
    for friend in friends:
        pl.semaphore_signal(barrier, inc=1, device_id=friend, device_id_type=MESH)
    pl.semaphore_wait(barrier, len(friends))


def push(src, dst, send_sem, recv_sem, friend):
    copy = pltpu.make_async_remote_copy(
        src_ref=src,
        dst_ref=dst,
        send_sem=send_sem,
        recv_sem=recv_sem,
        device_id=friend,
        device_id_type=MESH,
    )
    return copy


def add_into(dst, src):
    dst[...] = (dst[...].astype(F32) + src[...].astype(F32)).astype(dst.dtype)


PLACES = ("core", "x", "near", "far")


class Sum:
    def __init__(self, held, got, dims, order, send_sem, recv_sem, cut_columns=True):
        self.held, self.got, self.dims, self.order = held, got, dims, order
        self.send_sem, self.recv_sem, self.cut_columns = send_sem, recv_sem, cut_columns

    def cut(self, stage, keep):
        name = self.order[stage]
        done = self.order[:stage]
        _, core, x, near, far = spot()
        own = {"core": core, "x": x, "near": near, "far": far}
        at = []
        for dim in self.dims:
            if dim == name:
                at.append(own[dim] if keep else 1 - own[dim])
            else:
                at.append(own[dim] if dim in done else slice(None))
        if self.cut_columns and (name == "half" or "half" in done):
            me = lax.axis_index("blk")
            size = self.held.shape[-1] // 2
            side = 1 - me if name == "half" and not keep else me
            at += [slice(None), pl.ds(pl.multiple_of(side * size, size), size)]
        return tuple(at)

    def copy(self, stage):
        name = self.order[stage]
        return push(
            self.held.at[self.cut(stage, False)],
            self.got[stage],
            self.send_sem.at[stage],
            self.recv_sem.at[stage],
            partners()[PLACES.index(name) if name in PLACES else 4],
        )

    def start(self, stage):
        self.copy(stage).start()

    def take(self, stage):
        self.copy(stage).wait()
        mine = self.held.at[self.cut(stage, True)]
        came = self.got[stage]
        lead = came.shape[:-2]
        count = 1
        for size in lead:
            count *= size
        for n in range(count):
            at = []
            for size in reversed(lead):
                at.insert(0, n % size)
                n //= size
            at = tuple(at)
            add_into(mine.at[at] if at else mine, came.at[at] if at else came)
        if stage + 1 < len(self.order):
            self.start(stage + 1)

    def last(self):
        stage = len(self.order) - 1
        self.copy(stage).wait()
        return self.held[self.cut(stage, True)].astype(F32), self.got[stage][...].astype(F32)


def front_kernel(
    x_in,
    fv_in,
    seg_in,
    cot_in,
    g1_ref,
    b1_ref,
    wqkv_in,
    bq_ref,
    bv_ref,
    wout_in,
    bout_ref,
    g2_ref,
    b2_ref,
    x_out,
    q_out,
    k_out,
    v_out,
    att_out,
    act2_out,
    mid_out,
    lse_ref,
    bias_out,
    cot_out,
    xs,
    qs,
    ks,
    vs,
    atts,
    act2s,
    mids,
    bias,
    wqkv,
    wout,
    segrow,
    segsend,
    segcol,
    cots,
    in_sem,
    out_sem,
    send_sem,
    recv_sem,
):
    half = x_in.shape[1]
    tokens = 2 * half
    width = x_in.shape[2]
    val = fv_in.shape[2]
    steps = tokens // QB
    me = lax.axis_index("blk")
    other = 1 - me
    mine = pl.multiple_of(me * half, half)
    theirs = pl.multiple_of(other * half, half)

    def local_in(i, src, dst):
        copy = pltpu.make_async_copy(src, dst, in_sem.at[i])
        copy.start()
        return copy

    own_x = local_in(0, x_in.at[me], xs.at[pl.ds(mine, half)])
    own_fv = local_in(1, fv_in.at[me], vs.at[pl.ds(mine, half), pl.ds(val, val)])
    own_w = local_in(2, wqkv_in, wqkv)
    own_wo = local_in(3, wout_in, wout)
    own_cot = local_in(4, cot_in.at[me], cots)
    first, second = seg_in[0:1, :], seg_in[1:2, :]
    segsend[...] = jnp.broadcast_to(jnp.where(me == 0, second, first), segsend.shape)

    barrier = pltpu.get_barrier_semaphore()
    pl.semaphore_signal(barrier, inc=1, device_id={"blk": other}, device_id_type=MESH)
    pl.semaphore_wait(barrier, 1)

    def remote(i, src, dst):
        copy = pltpu.make_async_remote_copy(
            src_ref=src,
            dst_ref=dst,
            send_sem=send_sem.at[i],
            recv_sem=recv_sem.at[i],
            device_id={"blk": other},
            device_id_type=MESH,
        )
        copy.start()
        return copy

    part = half // 2
    far_x = [
        remote(
            c,
            x_in.at[other, pl.ds(c * part, part)],
            xs.at[pl.ds(pl.multiple_of(mine + c * part, part), part)],
        )
        for c in range(2)
    ]
    far_seg = remote(2, segsend, segrow.at[:, pl.ds(mine, half)])
    far_fv = remote(3, fv_in.at[other], vs.at[pl.ds(mine, half), pl.ds(val, val)])
    far_cot = remote(4, cot_in.at[other], cot_out.at[pl.ds(mine, half)])

    own_row = jnp.broadcast_to(jnp.where(me == 0, first, second), (8, half))
    segrow[:, pl.ds(mine, half)] = own_row

    def project(start):
        rows = pl.ds(pl.multiple_of(start, QB), QB)
        xhat, _ = norm_parts(xs[rows, :].astype(F32))
        act1 = (xhat * row(g1_ref) + row(b1_ref)).astype(BF)
        out = nn(act1, wqkv[...])
        query = (out[:, :width] + row(bq_ref)).astype(BF)
        qs[rows, :] = query * jnp.asarray(HEAD_DIM**-0.5, BF)
        ks[rows, :] = out[:, width : 2 * width].astype(BF)
        vs[rows, pl.ds(0, val)] = (out[:, 2 * width :] + row(bv_ref)).astype(BF)

    own_x.wait()
    own_w.wait()
    for c in range(2):
        project(mine + c * QB)
    for c in range(2):
        far_x[c].wait()
        project(theirs + c * part)

    outs = []

    def local_out(src, dst):
        copy = pltpu.make_async_copy(src, dst, out_sem.at[len(outs)])
        copy.start()
        outs.append(copy)

    own_cot.wait()
    local_out(cots, cot_out.at[pl.ds(mine, half)])
    local_out(xs, x_out)
    local_out(qs, q_out)
    local_out(ks, k_out)

    far_seg.wait()
    for c in range(tokens // LANES):
        line = segrow[0:1, c * LANES : (c + 1) * LANES].astype(F32)
        segcol[c * LANES : (c + 1) * LANES, :] = jnp.broadcast_to(line, (LANES, LANES)).T
    for j in range(steps):
        key = segcol[j * QB : (j + 1) * QB, :]
        key = jnp.concatenate([key] * (QB // LANES), axis=1)
        for i in range(j, steps):
            query = segrow[0:1, i * QB : (i + 1) * QB].astype(F32)
            seen = (key == query) & (query >= 0.0)
            if i == j:
                down = lax.broadcasted_iota(jnp.int32, (QB, QB), 0)
                across = lax.broadcasted_iota(jnp.int32, (QB, QB), 1)
                seen = (seen & (down <= across)) | (down == across)
            bias[j * QB : (j + 1) * QB, i * QB : (i + 1) * QB] = jnp.where(seen, 0.0, NEG)
        cut = (pl.ds(j * QB, QB), pl.ds(j * QB, tokens - j * QB))
        local_out(bias.at[cut], bias_out.at[cut])
    low = lax.broadcasted_iota(jnp.int32, (1, LANES), 1) < HEAD_DIM

    @pl.loop(0, PAIRS)
    def _(p):
        @pl.when(p == PAIRS // 2)
        def _():
            own_fv.wait()
            far_fv.wait()

        cols = pl.ds(pl.multiple_of(p * LANES, LANES), LANES)
        k = ks[:, cols]
        v = vs[:, cols]

        def score(i, h):
            q = qs[i * QB : (i + 1) * QB, cols]
            q = jnp.where(low if h == 0 else ~low, q, jnp.zeros_like(q))
            span = (i + 1) * QB
            return nt(k[:span], q) + bias[:span, i * QB : span]

        done = {}

        def finish(i, h, s):
            span = (i + 1) * QB
            top = jnp.max(s, axis=0, keepdims=True)
            e = jnp.exp(s - top)
            total = jnp.sum(e, axis=0, keepdims=True)
            done[h] = tn((e * (1.0 / total)).astype(BF), v[:span])
            lse_ref[p, h : h + 1, i * QB : span] = top + jnp.log(total)
            if h == 1:
                atts[i * QB : span, cols] = jnp.where(low, done[0], done[1]).astype(BF)

        waiting = []
        for i in range(steps):
            for h in range(2):
                waiting.append((i, h, score(i, h)))
                if len(waiting) > 2:
                    finish(*waiting.pop(0))
        for item in waiting:
            finish(*item)

    local_out(atts, att_out)
    local_out(vs, v_out)
    own_wo.wait()
    for c in range(steps):
        rows = slice(c * QB, (c + 1) * QB)
        middle = xs[rows, :].astype(F32) + nn(atts[rows, :], wout[...]) + row(bout_ref)
        mids[rows, :] = middle
        xhat, _ = norm_parts(middle)
        act2s[rows, :] = (xhat * row(g2_ref) + row(b2_ref)).astype(BF)
    local_out(mids, mid_out)
    local_out(act2s, act2_out)
    for copy in outs:
        copy.wait()
    far_cot.wait()


def front(x, fv, seg, cot, g1, b1, wqkv, bq, bv, wout, bout, g2, b2):
    half, width, val = x.shape[1], x.shape[2], fv.shape[2]
    tokens = 2 * half
    hbm = pl.BlockSpec(memory_space=pl.ANY)
    vmem = pl.BlockSpec(memory_space=pltpu.VMEM)
    flat = jax.ShapeDtypeStruct((tokens, width), BF)
    shape = jax.ShapeDtypeStruct
    return pl.pallas_call(
        front_kernel,
        in_specs=[hbm, hbm, vmem, hbm, vmem, vmem, hbm, vmem, vmem, hbm, vmem, vmem, vmem],
        out_specs=[hbm] * 7 + [vmem] + [hbm] * 2,
        out_shape=[
            flat,
            flat,
            flat,
            flat,
            flat,
            flat,
            shape((tokens, width), F32),
            shape((PAIRS, 2, tokens), F32),
            shape((tokens, tokens), F32),
            flat,
        ],
        scratch_shapes=[
            pltpu.VMEM((tokens, width), BF),
            pltpu.VMEM((tokens, width), BF),
            pltpu.VMEM((tokens, width), BF),
            pltpu.VMEM((tokens, width), BF),
            pltpu.VMEM((tokens, width), BF),
            pltpu.VMEM((tokens, width), BF),
            pltpu.VMEM((tokens, width), F32),
            pltpu.VMEM((tokens, tokens), F32),
            pltpu.VMEM(wqkv.shape, BF),
            pltpu.VMEM(wout.shape, BF),
            pltpu.VMEM((8, tokens), jnp.int32),
            pltpu.VMEM((8, half), jnp.int32),
            pltpu.VMEM((tokens, LANES), F32),
            pltpu.VMEM((half, width), BF),
            pltpu.SemaphoreType.DMA((5,)),
            pltpu.SemaphoreType.DMA((8 + tokens // QB,)),
            pltpu.SemaphoreType.DMA((5,)),
            pltpu.SemaphoreType.DMA((5,)),
        ],
        compiler_params=pltpu.CompilerParams(
            collective_id=0, has_side_effects=True, vmem_limit_bytes=56 * MIB
        ),
        name="front",
    )(x, fv, seg, cot, g1, b1, wqkv, bq, bv, wout, bout, g2, b2)


def feed_kernel(
    act2,
    cot,
    mid,
    att,
    g2_ref,
    bproj_ref,
    wout,
    wfc,
    bfc_ref,
    wproj,
    lout,
    gmid,
    gatt,
    dots,
    dwout,
    fc_done,
    fc_half,
    proj_half,
    fc_last,
    proj_last,
    dbfc,
    small,
    acc,
    dact,
    act2t,
    hid,
    dpre,
    sel,
    bias,
    gf,
    gp,
    rf0,
    rp0,
    rfh,
    rp1,
    rf1,
    send_sem,
    recv_sem,
    out_sem,
):
    t = pl.program_id(0)
    last = pl.num_programs(0) - 1
    tokens, width = act2.shape
    tile = hid.shape[1]
    steps = tokens // QB
    _, core, x, _, _ = spot()
    me = lax.axis_index("blk")
    both = partners()
    friends = [both[0], both[1], both[4]]
    side = pl.ds(pl.multiple_of(me * (tile // 2), tile // 2), tile // 2)

    fcs = []
    projs = []
    for n in range(3):
        order = ("core", "half", "x") if n < 2 else ("core", "half")
        fcs.append(
            Sum(
                gf.at[n],
                [rf0.at[n], rfh.at[n]] + ([rf1.at[n]] if n < 2 else []),
                ("far", "near", "x", "core"),
                order,
                send_sem.at[n],
                recv_sem.at[n],
            )
        )
        projs.append(
            Sum(
                gp.at[n],
                [rp0.at[n], rp1.at[n]],
                ("x", "core"),
                ("core", "x"),
                send_sem.at[3 + n],
                recv_sem.at[3 + n],
            )
        )

    def proj_out(n):
        return pltpu.make_async_copy(gp.at[n, x, core], proj_half.at[n], out_sem.at[n])

    def fc_out(n):
        if n < 2:
            src = gf.at[n, :, :, x, core, :, side]
            return pltpu.make_async_copy(src, fc_done.at[n], out_sem.at[3 + n])
        return pltpu.make_async_copy(gf.at[n, :, :, :, core, :, side], fc_half, out_sem.at[3 + n])

    def at_step(k, *actions):
        @pl.when(t == k)
        def _():
            for action in actions:
                action()

    def first_stage(n):
        projs[n].take(0)
        fcs[n].take(0)

    def second_stage(n):
        fcs[n].take(1)
        projs[n].take(1)
        proj_out(n).start()
        if n == 2:
            fc_out(n).start()

    def third_stage(n):
        fcs[n].take(2)
        fc_out(n).start()

    @pl.when(t == 0)
    def _():
        greet(friends)
        act2t[...] = act2[...].T
        for n in range(bias.shape[0]):
            bias[n] = row(bfc_ref)[:, n * tile : (n + 1) * tile]
        acc[...] = jnp.zeros_like(acc)
        dact[...] = jnp.zeros_like(dact)
        head = lax.broadcasted_iota(jnp.int32, sel.shape, 0)
        feature = lax.broadcasted_iota(jnp.int32, sel.shape, 1)
        inside = (feature >= head * HEAD_DIM) & (feature < (head + 1) * HEAD_DIM)
        sel[...] = jnp.where(inside, 1.0, 0.0).astype(BF)

    total = None
    for c in range(steps):
        rows = slice(c * QB, (c + 1) * QB)
        u = nn(act2[rows, :], wfc[...]) + bias[t]
        square = u * u
        bend = jnp.tanh(u * (0.7978845608028654 + (0.7978845608028654 * 0.044715) * square))
        halfway = 0.5 + 0.5 * bend
        hidden = (u * halfway).astype(BF)
        hid[rows, :] = hidden
        acc[rows, :] += nn(hidden, wproj[...])
        slope = halfway + (u * (0.5 - 0.5 * bend * bend)) * (
            0.7978845608028654 + (3 * 0.7978845608028654 * 0.044715) * square
        )
        grad = (nt(cot[rows, :], wproj[...]) * slope).astype(BF)
        dpre[rows, :] = grad
        dact[rows, :] += nt(grad, wfc[...])
        part = column_sum(grad.astype(F32))
        total = part if total is None else total + part
        for n in range(3):
            if c == 0 and n < 2:
                at_step(n + 2, lambda n=n: second_stage(n))
            if c == 1:
                at_step(n + 1, lambda n=n: first_stage(n))

    dbfc[...] = total
    for n in range(2):
        at_step(n + 2, lambda n=n: third_stage(n))
    dproj = tn(hid[...], cot[...]).astype(BF)
    dfc = nn(act2t[...], dpre[...]).astype(BF)

    @pl.when(t < last)
    def _():
        gp[t] = dproj.reshape(gp.shape[1:])
        gf[t] = dfc.reshape(gf.shape[1:])

    for n in range(3):
        at_step(n, lambda n=n: projs[n].start(0), lambda n=n: fcs[n].start(0))

    @pl.when(t == last)
    def _():
        proj_last[...] = dproj.reshape(proj_last.shape)
        fc_last[...] = dfc.reshape(fc_last.shape)
        gain = row(g2_ref)
        sums = [None] * 4
        for c in range(steps):
            rows = slice(c * QB, (c + 1) * QB)
            middle = mid[rows, :]
            upstream = cot[rows, :].astype(F32)
            lout[rows, :] = (middle + acc[rows, :] + row(bproj_ref)).astype(BF)
            xhat, inverse = norm_parts(middle)
            da = dact[rows, :]
            grad_middle = upstream + norm_pull(da, xhat, inverse, gain)
            gmid[rows, :] = grad_middle
            branch = grad_middle.astype(BF)
            hid[rows, :width] = branch
            parts = [
                column_sum(upstream),
                column_sum(da * xhat),
                column_sum(da),
                column_sum(branch.astype(F32)),
            ]
            sums = [b if a is None else a + b for a, b in zip(sums, parts)]
            ga = nt(branch, wout[...]).astype(BF)
            gatt[rows, :] = ga
            product = ga.astype(F32) * att[rows, :].astype(F32)
            big = product.astype(BF)
            rest = (product - big.astype(F32)).astype(BF)
            dot = nt(sel[...], big) + nt(sel[...], rest)
            for p in range(PAIRS):
                dots[p, :, rows] = dot[2 * p : 2 * p + 2, :]
        small[...] = jnp.concatenate(sums, axis=0)
        dwout[...] = tn(att[...], hid[:, :width]).astype(BF).reshape(dwout.shape)
        second_stage(2)
        for n in range(3):
            proj_out(n).wait()
            fc_out(n).wait()


def feed(act2, cot, mid, att, g2, bproj, wout, wfc, bfc, wproj):
    tokens, width = act2.shape
    ff = wfc.shape[1]
    tiles = 4
    tile = ff // tiles
    owner = width // 16
    owner_ff = ff // 16
    shape = jax.ShapeDtypeStruct
    flat = shape((tokens, width), BF)
    once = pl.Buffered(1)
    hbm = pl.BlockSpec(memory_space=pl.ANY)

    def whole(s):
        return pl.BlockSpec(s, lambda t: (0,) * len(s), pipeline_mode=once)

    rows = whole((tokens, width))
    line = whole((width,))
    return pl.pallas_call(
        feed_kernel,
        grid=(tiles,),
        in_specs=[
            rows,
            rows,
            rows,
            rows,
            line,
            line,
            whole(wout.shape),
            pl.BlockSpec((width, tile), lambda t: (0, t)),
            whole((ff,)),
            pl.BlockSpec((tile, width), lambda t: (t, 0)),
        ],
        out_specs=[
            rows,
            rows,
            rows,
            whole((PAIRS, 2, tokens)),
            whole((2, 2, 2, 2, owner, width)),
            hbm,
            hbm,
            hbm,
            whole((2, 2, 2, 2, owner, tile)),
            whole((2, 2, owner_ff, width)),
            pl.BlockSpec((1, tile), lambda t: (0, t)),
            whole((4, width)),
        ],
        out_shape=[
            flat,
            shape((tokens, width), F32),
            flat,
            shape((PAIRS, 2, tokens), F32),
            shape((2, 2, 2, 2, owner, width), BF),
            shape((2, 2, 2, owner, tile // 2), BF),
            shape((2, 2, 2, owner, tile // 2), BF),
            shape((tiles - 1, owner_ff, width), BF),
            shape((2, 2, 2, 2, owner, tile), BF),
            shape((2, 2, owner_ff, width), BF),
            shape((1, ff), F32),
            shape((4, width), F32),
        ],
        scratch_shapes=[
            pltpu.VMEM((tokens, width), F32),
            pltpu.VMEM((tokens, width), F32),
            pltpu.VMEM((width, tokens), BF),
            pltpu.VMEM((tokens, tile), BF),
            pltpu.VMEM((tokens, tile), BF),
            pltpu.VMEM((16, width), BF),
            pltpu.VMEM((tiles, 1, tile), F32),
            pltpu.VMEM((tiles - 1, 2, 2, 2, 2, owner, tile), BF),
            pltpu.VMEM((tiles - 1, 2, 2, owner_ff, width), BF),
            pltpu.VMEM((tiles - 1, 2, 2, 2, owner, tile), BF),
            pltpu.VMEM((tiles - 1, 2, owner_ff, width), BF),
            pltpu.VMEM((tiles - 1, 2, 2, 2, owner, tile // 2), BF),
            pltpu.VMEM((tiles - 1, owner_ff, width), BF),
            pltpu.VMEM((tiles - 2, 2, 2, owner, tile // 2), BF),
            pltpu.SemaphoreType.DMA((6, 3)),
            pltpu.SemaphoreType.DMA((6, 3)),
            pltpu.SemaphoreType.DMA((6,)),
        ],
        compiler_params=pltpu.CompilerParams(
            collective_id=1, has_side_effects=True, vmem_limit_bytes=60 * MIB
        ),
        name="feed",
    )(act2, cot, mid, att, g2, bproj, wout, wfc, bfc, wproj)


FIRST_PAIR = PAIRS // 2


def pieces(width, val):
    lanes = LANES
    return [
        (2, [(3 * lanes, 2 * lanes), (width + 3 * lanes, 2 * lanes)]),
        (
            4,
            [
                (5 * lanes, lanes),
                (0, lanes),
                (width + 5 * lanes, lanes),
                (width, lanes),
                (2 * width, lanes),
            ],
        ),
        (
            6,
            [(lanes, 2 * lanes), (width + lanes, 2 * lanes), (2 * width + lanes, 2 * lanes)],
        ),
    ]


def tail_kernel(
    q_in,
    k_in,
    v_in,
    do_in,
    bias_in,
    x_in,
    gmid_in,
    wqkv_in,
    lout_in,
    dwout_in,
    fd_in,
    f2_in,
    ph_in,
    fc3_in,
    p3_in,
    lse_ref,
    d_ref,
    g1_ref,
    b1_ref,
    dbfc_ref,
    small_in,
    lout_out,
    gx_out,
    gf_out,
    wqkv_out,
    wout_out,
    wfc_out,
    wproj_out,
    small_out,
    q_ref,
    k_ref,
    v_ref,
    do_ref,
    bias,
    xs,
    gmid,
    wqkv,
    dqk,
    dvs,
    gfs,
    dqa,
    act1,
    act1t,
    gx,
    louts,
    g_out,
    g_fd,
    g_f2,
    g_ph,
    g_fc3,
    g_p3,
    g_q,
    r_out,
    r_fd,
    r_f2,
    r_ph,
    r_fc3,
    r_p3,
    r_q,
    sums,
    s_got,
    in_sem,
    out_sem,
    back_send,
    back_recv,
    sum_send,
    sum_recv,
):
    tokens, width = q_ref.shape
    half = tokens // 2
    val = gfs.shape[1]
    steps = tokens // QB
    me = lax.axis_index("blk")
    mine = pl.multiple_of(me * half, half)
    theirs = pl.multiple_of((1 - me) * half, half)
    _, core, x, near, far = spot()
    friends = partners()
    parts = pieces(width, val)

    sources = {
        "p3": (p3_in, g_p3),
        "fc3": (fc3_in, g_fc3),
        "out": (dwout_in, g_out),
        "f2": (f2_in, g_f2),
        "fd0": (fd_in.at[0], g_fd.at[:, :, :, 0 : fd_in.shape[-1]]),
        "fd1": (fd_in.at[1], g_fd.at[:, :, :, fd_in.shape[-1] :]),
        "ph0": (ph_in.at[0:2], g_ph.at[0]),
        "ph1": (ph_in.at[2], g_ph.at[1, 0]),
        "q": (q_in, q_ref),
        "k": (k_in, k_ref),
        "v": (v_in, v_ref),
        "do": (do_in, do_ref),
        "bias": (bias_in, bias),
        "x": (x_in, xs),
        "wqkv": (wqkv_in, wqkv),
        "gmid": (gmid_in, gmid),
        "lout": (lout_in.at[pl.ds(mine, half)], louts),
    }
    loads = {
        name: pltpu.make_async_copy(src, dst, in_sem.at[n])
        for n, (name, (src, dst)) in enumerate(sources.items())
    }
    for load in loads.values():
        load.start()
    greet(friends)

    full = ("far", "near", "x", "core")
    down = ("core", "x", "near", "far", "pair")
    sems = iter(range(16))

    def chain(held, got, dims, order, cut_columns=True):
        n = next(sems)
        return Sum(held, got, dims, order, sum_send.at[n], sum_recv.at[n], cut_columns)

    s_out = chain(g_out, r_out, full, down)
    s_fc3 = chain(g_fc3, r_fc3, full, down)
    s_p3 = chain(g_p3, r_p3, ("x", "core"), ("core", "x"))
    s_fd = chain(g_fd, r_fd, full[:2], ("near", "far", "gather"), False)
    s_f2 = chain(g_f2, r_f2, full[:3], ("x", "near", "far", "gather"), False)
    s_pa = chain(g_ph.at[0], r_ph[0:1], ("near",), ("near",))
    s_pb = chain(g_ph.at[1], r_ph[1:2], ("near",), ("near",))
    s_ph = chain(g_ph, [None] + list(r_ph[2:]), full[:2], ("near", "far", "pair"))
    s_q = [chain(g, r, full, down) for g, r in zip(g_q, r_q)]
    s_small = next(sems)

    def small_copy(stage):
        return push(
            sums.at[stage],
            s_got.at[stage],
            sum_send.at[s_small, stage],
            sum_recv.at[s_small, stage],
            friends[stage],
        )

    def give_back(n, src, dst):
        return push(src, dst, back_send.at[n], back_recv.at[n], friends[4])

    back_lout = give_back(0, lout_in.at[pl.ds(theirs, half)], lout_out.at[me])
    back_lout.start()
    keep_lout = pltpu.make_async_copy(louts, lout_out.at[me], out_sem.at[0])

    for name, begin in (("p3", s_p3), ("fc3", s_fc3), ("out", s_out), ("f2", s_f2)):
        loads[name].wait()
        begin.start(0)
    loads["fd0"].wait()
    loads["fd1"].wait()
    s_fd.start(0)
    loads["ph0"].wait()
    s_pa.start(0)
    for name in ("q", "k", "v", "do", "bias"):
        loads[name].wait()

    low = lax.broadcasted_iota(jnp.int32, (1, LANES), 1) < HEAD_DIM
    masks = [low, ~low]
    zero = jnp.zeros((), BF)
    gain = row(g1_ref)
    shift = row(b1_ref)

    def columns(at, size):
        return dqk[:, at : at + size] if at < 2 * width else dvs[:, at - 2 * width : at - 2 * width + size]

    def project_grad(n):
        at = 0
        for start, size in parts[n][1]:
            block = nn(act1t[...], columns(start, size)).astype(BF)
            g_q[n][:, :, :, :, :, at : at + size] = block.reshape(g_q[n].shape[:-1] + (size,))
            at += size
        s_q[n].start(0)

    def normed():
        loads["x"].wait()
        for c in range(steps):
            rows = slice(c * QB, (c + 1) * QB)
            xhat, _ = norm_parts(xs[rows, :].astype(F32))
            act1[rows, :] = (xhat * gain + shift).astype(BF)
        act1t[...] = act1[...].T

    def third_tile():
        s_p3.take(1)
        loads["ph1"].wait()
        g_ph[1, 1] = g_p3[x, core]
        s_pb.start(0)

    back_gf = give_back(1, gfs.at[pl.ds(theirs, half)], gf_out.at[me])
    keep_gf = pltpu.make_async_copy(gfs.at[pl.ds(mine, half)], gf_out.at[me], out_sem.at[1])

    plan = {
        1: [
            lambda: s_p3.take(0),
            lambda: s_fc3.take(0),
            lambda: s_out.take(0),
            lambda: s_f2.take(0),
            lambda: s_fd.take(0),
            normed,
        ],
        2: [lambda: project_grad(0), lambda: s_pa.take(0)],
        3: [
            back_gf.start,
            keep_gf.start,
            third_tile,
            lambda: s_q[0].take(0),
            lambda: s_fd.take(1),
            lambda: s_f2.take(1),
        ],
        4: [lambda: project_grad(1), lambda: s_fc3.take(1)],
        5: [
            lambda: s_q[1].take(0),
            lambda: s_out.take(1),
            lambda: s_f2.take(2),
            lambda: s_pb.take(0),
            lambda: s_ph.start(1),
        ],
    }

    @pl.loop(0, PAIRS)
    def _(step):
        for k, actions in plan.items():

            @pl.when(step == k)
            def _():
                for action in actions:
                    action()

        p = lax.rem(step + FIRST_PAIR, PAIRS)
        cols = pl.ds(pl.multiple_of(p * LANES, LANES), LANES)
        kcols = pl.ds(pl.multiple_of(width + p * LANES, LANES), LANES)
        q, k, v, do = q_ref[:, cols], k_ref[:, cols], v_ref[:, cols], do_ref[:, cols]
        qm = [jnp.where(m, q, zero) for m in masks]
        km = [jnp.where(m, k, zero) for m in masks]
        dom = [jnp.where(m, do, zero) for m in masks]
        dvals = []
        for j in range(steps):
            a = j * QB
            keys = slice(a, a + QB)
            dk = dv = dq = None
            for h in range(2):
                s = nt(k[keys], qm[h][a:]) + bias[keys, a:]
                probs = jnp.exp(s - lse_ref[p, h : h + 1, a:])
                dp = nt(v[keys], dom[h][a:])
                ds = (probs * (dp - d_ref[p, h : h + 1, a:])).astype(BF)
                dvh = nn(probs.astype(BF), dom[h][a:])
                dkh = nn(ds, qm[h][a:])
                dqh = tn(ds, km[h][keys])
                dk = dkh if dk is None else dk + dkh
                dv = dvh if dv is None else dv + dvh
                dq = dqh if dq is None else dq + dqh
            dqk[keys, kcols] = dk.astype(BF)
            dvals.append(dv.astype(BF))
            if j == 0:
                dqa[...] = dq
            else:
                dqa[a:, :] += dq
        dqk[:, cols] = (dqa[...] * HEAD_DIM**-0.5).astype(BF)

        @pl.when(p < PAIRS // 2)
        def _():
            for j in range(steps):
                dvs[j * QB : (j + 1) * QB, cols] = dvals[j]

        @pl.when(p >= PAIRS // 2)
        def _():
            late = pl.ds(pl.multiple_of(p * LANES - val, LANES), LANES)
            for j in range(steps):
                gfs[j * QB : (j + 1) * QB, late] = dvals[j]

    project_grad(2)
    s_q[0].take(1)
    loads["wqkv"].wait()
    loads["gmid"].wait()
    loads["lout"].wait()
    keep_lout.start()

    totals = [None] * 4

    def input_grad(start):
        rows = pl.ds(pl.multiple_of(start, QB), QB)
        da = nt(dqk[rows, :], wqkv[:, : 2 * width]) + nt(dvs[rows, :], wqkv[:, 2 * width :])
        xhat, inverse = norm_parts(xs[rows, :].astype(F32))
        gx[rows, :] = (gmid[rows, :] + norm_pull(da, xhat, inverse, gain)).astype(BF)
        bv = column_sum(dvs[rows, :].astype(F32))
        found = [
            column_sum(da * xhat),
            column_sum(da),
            column_sum(dqk[rows, :width].astype(F32)),
            jnp.concatenate([bv, jnp.zeros((1, width - val), F32)], axis=1),
        ]
        totals[:] = [b if a is None else a + b for a, b in zip(totals, found)]

    backs = []
    for c in range(half // QB):
        start = pl.multiple_of(theirs + c * QB, QB)
        input_grad(start)
        copy = give_back(2 + c, gx.at[pl.ds(start, QB)], gx_out.at[me, pl.ds(c * QB, QB)])
        copy.start()
        backs.append(copy)
        if c == 0:
            s_q[2].take(0)
        else:
            s_q[1].take(1)
            s_fc3.take(2)
    for c in range(half // QB):
        input_grad(mine + c * QB)
    keep_gx = pltpu.make_async_copy(gx.at[pl.ds(mine, half)], gx_out.at[me], out_sem.at[2])
    keep_gx.start()
    wide = [dbfc_ref[:, n * width : (n + 1) * width] for n in range(4)]
    sums[0] = jnp.concatenate(
        [small_in[...]] + totals + wide + [jnp.zeros((4, width), F32)], axis=0
    )
    small_copy(0).start()

    def small_take(stage):
        small_copy(stage).wait()
        sums[stage + 1] = sums[stage] + s_got[stage]
        if stage < 4:
            small_copy(stage + 1).start()

    s_out.take(2)
    s_q[0].take(2)
    s_ph.take(1)
    small_take(0)
    s_q[2].take(1)
    s_q[1].take(2)
    small_take(1)
    s_fc3.take(3)
    s_out.take(3)
    s_q[0].take(3)
    small_take(2)
    s_q[2].take(2)
    s_q[1].take(3)
    small_take(3)
    s_q[2].take(3)

    tile = g_fc3.shape[-1]
    side = tile // 2
    for sum_, tiles in ((s_fd, (0, 1)), (s_f2, (2,))):
        for part, who in zip(sum_.last(), (me, 1 - me)):
            for n, t in enumerate(tiles):
                at = pl.ds(pl.multiple_of(t * tile + who * side, side), side)
                wfc_out[:, at] = part[:, n * side : (n + 1) * side]
    own, came = s_fc3.last()
    wfc_out[:, 3 * tile :] = own + came
    own, came = s_ph.last()
    wproj_out[...] = own + came
    own, came = s_out.last()
    wout_out[...] = own + came
    for n in range(3):
        own, came = s_q[n].last()
        part = own + came
        at = 0
        for start, size in parts[n][1]:
            wqkv_out[:, start : start + size] = part[:, at : at + size]
            at += size
        if n == 1:
            small_take(4)
            small_out[...] = sums[5]
    back_lout.wait()
    back_gf.wait()
    for copy in backs:
        copy.wait()
    keep_lout.wait()
    keep_gf.wait()
    keep_gx.wait()


def tail(q, k, v, do, bias, x, gmid, wqkv, lout, dwout, fd, f2, ph, fc3, p3, lse, dots, g1, b1, dbfc, small):
    tokens, width = q.shape
    half = tokens // 2
    val = wqkv.shape[1] - 2 * width
    owner = width // 16
    owner_ff = dbfc.shape[1] // 16
    ff = dbfc.shape[1]
    tile = fc3.shape[-1]
    shape = jax.ShapeDtypeStruct
    hbm = pl.BlockSpec(memory_space=pl.ANY)
    vmem = pl.BlockSpec(memory_space=pltpu.VMEM)

    def vm(*s):
        return pltpu.VMEM(s, BF)

    def chain(rows, cols):
        return [
            vm(2, 2, 2, rows, cols),
            vm(2, 2, rows, cols),
            vm(2, rows, cols),
            vm(rows, cols),
            vm(rows, cols),
        ]

    flat = vm(tokens, width)
    sizes = [sum(size for _, size in columns) for _, columns in pieces(width, val)]
    return pl.pallas_call(
        tail_kernel,
        in_specs=[hbm] * 15 + [vmem] * 6,
        out_specs=[hbm] * 3 + [vmem] * 5,
        out_shape=[
            shape((2, half, width), BF),
            shape((2, half, width), BF),
            shape((2, half, val), BF),
            shape((owner, wqkv.shape[1]), F32),
            shape((owner, width), F32),
            shape((owner, ff), F32),
            shape((owner_ff, width), F32),
            shape((16, width), F32),
        ],
        scratch_shapes=[
            flat,
            flat,
            flat,
            flat,
            pltpu.VMEM((tokens, tokens), F32),
            flat,
            pltpu.VMEM((tokens, width), F32),
            vm(*wqkv.shape),
            vm(tokens, 2 * width),
            vm(tokens, val),
            vm(tokens, val),
            pltpu.VMEM((tokens, LANES), F32),
            flat,
            vm(width, tokens),
            flat,
            vm(half, width),
            vm(*dwout.shape),
            vm(2, 2, owner, tile),
            vm(2, 2, 2, owner, tile // 2),
            vm(2, 2, owner_ff, width),
            vm(*fc3.shape),
            vm(*p3.shape),
            [vm(2, 2, 2, 2, owner, size) for size in sizes],
            chain(owner, width),
            chain(owner, tile)[2:],
            chain(owner, tile // 2)[1:],
            [vm(owner_ff, width)] * 4,
            chain(owner, tile),
            [vm(2, owner_ff, width), vm(owner_ff, width)],
            [chain(owner, size) for size in sizes],
            pltpu.VMEM((6, 16, width), F32),
            pltpu.VMEM((5, 16, width), F32),
            pltpu.SemaphoreType.DMA((17,)),
            pltpu.SemaphoreType.DMA((3,)),
            pltpu.SemaphoreType.DMA((4,)),
            pltpu.SemaphoreType.DMA((4,)),
            pltpu.SemaphoreType.DMA((12, 5)),
            pltpu.SemaphoreType.DMA((12, 5)),
        ],
        compiler_params=pltpu.CompilerParams(
            collective_id=2, has_side_effects=True, vmem_limit_bytes=62 * MIB
        ),
        name="tail",
    )(
        q,
        k,
        v,
        do,
        bias,
        x,
        gmid,
        wqkv,
        lout,
        dwout,
        fd,
        f2,
        ph,
        fc3,
        p3,
        lse,
        dots,
        g1,
        b1,
        dbfc,
        small,
    )


def finish_kernel(*refs):
    wide_in, sums = refs[:7], refs[7]
    wide_out, small_out, held, sem = refs[8:15], refs[15:24], refs[24], refs[25]
    loads = [pltpu.make_async_copy(src, dst, sem.at[0, n]) for n, (src, dst) in enumerate(zip(wide_in, held))]
    stores = [pltpu.make_async_copy(src, dst, sem.at[1, n]) for n, (src, dst) in enumerate(zip(held, wide_out))]
    for load in loads:
        load.start()
    b = lax.axis_index("batch")
    rows = sums[0:8, :]
    width = rows.shape[1]
    long = jnp.concatenate([sums[8 + n : 9 + n, :] for n in range(4)], axis=1)
    long = jnp.broadcast_to(long, (8, 4 * width))
    for at, ref in zip((4, 5, 6, 7, 3, 1, 2, None, 0), small_out):
        size = ref.shape[0]
        source = long if at is None else rows
        line = 0 if at is None else at
        length = source.shape[1]
        turned = pltpu.roll(source, lax.rem(length - b * size, length), 1)
        ref[...] = turned[line, :size]
    for load, store in zip(loads, stores):
        load.wait()
        store.start()
    for store in stores:
        store.wait()


def finish(wide, sums, sizes):
    hbm = pl.BlockSpec(memory_space=pl.ANY)
    vmem = pl.BlockSpec(memory_space=pltpu.VMEM)
    shape = jax.ShapeDtypeStruct
    return pl.pallas_call(
        finish_kernel,
        in_specs=[hbm] * 7 + [vmem],
        out_specs=[hbm] * 7 + [vmem] * 9,
        out_shape=[shape(a.shape, a.dtype) for a in wide] + [shape((n,), F32) for n in sizes],
        scratch_shapes=[
            [pltpu.VMEM(a.shape, a.dtype) for a in wide],
            pltpu.SemaphoreType.DMA((2, 7)),
        ],
        compiler_params=pltpu.CompilerParams(vmem_limit_bytes=60 * MIB),
        name="finish",
    )(*wide, sums)


def paired(
    inputs,
    first_values,
    segments,
    ln1_gain,
    first_norm_bias,
    w_qkv,
    b_query,
    b_value,
    w_out,
    b_out,
    ln2_gain,
    second_norm_bias,
    w_fc,
    b_fc,
    w_proj,
    b_proj,
    cotangent,
):
    half, width = inputs.shape[1], inputs.shape[2]
    val = first_values.shape[2]
    x, q, k, v, att, act2, mid, lse, bias, cot = front(
        inputs,
        first_values,
        segments,
        cotangent,
        ln1_gain,
        first_norm_bias,
        w_qkv,
        b_query,
        b_value,
        w_out,
        b_out,
        ln2_gain,
        second_norm_bias,
    )
    lout, gmid, gatt, dots, dwout, fd, f2, ph, fc3, p3, dbfc, small = feed(
        act2, cot, mid, att, ln2_gain, b_proj, w_out, w_fc, b_fc, w_proj
    )
    owner = width // 16
    *wide, sums = tail(
        q,
        k,
        v,
        gatt,
        bias,
        x,
        gmid,
        w_qkv,
        lout,
        dwout,
        fd,
        f2,
        ph,
        fc3,
        p3,
        lse,
        dots,
        ln1_gain,
        first_norm_bias,
        dbfc,
        small,
    )
    sizes = [owner, owner, owner, val // 16, owner, owner, owner, w_fc.shape[1] // 16, owner]
    out = finish(wide, sums, sizes)
    layer_out, grad_inputs, grad_first, gwqkv, gwout, gwfc, gwproj = out[:7]
    g1, b1, bq, bv, bo, g2, b2, bf, bp = out[7:]
    return (
        layer_out,
        grad_inputs,
        grad_first,
        g1,
        b1,
        gwqkv,
        bq,
        bv,
        gwout,
        bo,
        g2,
        b2,
        gwfc,
        bf,
        gwproj,
        bp,
    )


MICRO = 2


def as_sent(shard):
    return jax.tree.map(lambda a: a.astype(jnp.bfloat16) if a.dtype == jnp.float32 else a, shard)


def apply_norm(values_in, norm_gain, shift_bias):
    mean_val = jnp.mean(values_in, axis=-1, keepdims=True)
    centred_rows = values_in - mean_val
    inverse_deviation = lax.rsqrt(
        jnp.mean(centred_rows * centred_rows, axis=-1, keepdims=True) + EPS
    )
    standardized = centred_rows * inverse_deviation
    return (standardized * norm_gain + shift_bias, standardized, inverse_deviation)


def apply_norm_backward(upstream_gradient, standardized, inverse_deviation, norm_gain):
    scaled_rows = upstream_gradient * norm_gain
    first_average = jnp.mean(scaled_rows, axis=-1, keepdims=True)
    second_average = jnp.mean(scaled_rows * standardized, axis=-1, keepdims=True)
    incoming_gradient = inverse_deviation * (
        scaled_rows - first_average - standardized * second_average
    )
    return (
        incoming_gradient,
        jnp.sum(upstream_gradient * standardized, axis=(0, 1)),
        jnp.sum(upstream_gradient, axis=(0, 1)),
    )


def gelu_tanh(values_in):
    cubic = values_in + 0.044715 * values_in * values_in * values_in
    return 0.5 * values_in * (1.0 + jnp.tanh(0.7978845608028654 * cubic))


def heads_of(values_in):
    return values_in.reshape(values_in.shape[0], values_in.shape[1], HEADS, HEAD_DIM)


def visible(seg_query, seg_key, query_pos, key_pos):
    same = seg_query[:, :, None] == seg_key[:, None, :]
    causal = key_pos[None, :] <= query_pos[:, None]
    live = seg_query[:, :, None] >= 0
    diagonal = key_pos[None, :] == query_pos[:, None]
    return (same & causal[None] & live | diagonal[None])[:, :, None, :]


def score_block(query4, key4, mask):
    raw = jnp.einsum("rqhd,rkhd->rqhk", query4, key4, preferred_element_type=jnp.float32)
    return jnp.where(mask, raw * HEAD_DIM ** (-0.5), NEG)


def grad_block(query4, key4, value4, dout4, log_total, out_dot, mask):
    probs = jnp.where(mask, jnp.exp(score_block(query4, key4, mask) - log_total[..., None]), 0.0)
    probs_low = probs.astype(jnp.bfloat16)
    grad_probs = jnp.einsum("rqhd,rkhd->rqhk", dout4, value4, preferred_element_type=jnp.float32)
    grad_scores = (probs * (grad_probs - out_dot[..., None]) * HEAD_DIM ** (-0.5)).astype(
        jnp.bfloat16
    )
    return (probs_low, grad_scores)


def spread(
    inputs,
    first_values,
    segments,
    ln1_gain,
    first_norm_bias,
    w_qkv,
    b_query,
    b_value,
    w_out,
    b_out,
    ln2_gain,
    second_norm_bias,
    w_fc,
    b_fc,
    w_proj,
    b_proj,
    cotangent,
):
    all_seg = lax.all_gather(segments, "blk", axis=1, tiled=True)
    block_len = inputs.shape[1]
    model_width = inputs.shape[2]
    val_width = first_values.shape[2]
    rows_mb = inputs.shape[0] // MICRO
    own_pos = lax.axis_index("blk") * block_len + jnp.arange(block_len)
    first_gain = ln1_gain.astype(jnp.float32)
    second_gain = ln2_gain.astype(jnp.float32)
    outputs = []
    input_grads = []
    first_grads = []
    totals = None
    for micro_step in range(MICRO):
        first_row = micro_step * rows_mb
        last_row = first_row + rows_mb
        residual_stream = inputs[first_row:last_row].astype(jnp.float32)
        first_part = first_values[first_row:last_row]
        seg_local = segments[first_row:last_row]
        seg_row = all_seg[first_row:last_row]
        cot_part = cotangent[first_row:last_row]
        first_normed_rows, first_standardized, first_inverse_deviation = apply_norm(
            residual_stream, first_gain, first_norm_bias.astype(jnp.float32)
        )
        act1 = first_normed_rows.astype(jnp.bfloat16)
        projected = jnp.einsum("rbd,de->rbe", act1, w_qkv, preferred_element_type=jnp.float32)
        queries = (projected[..., :model_width] + b_query.astype(jnp.float32)).astype(jnp.bfloat16)
        keys_low = projected[..., model_width : 2 * model_width].astype(jnp.bfloat16)
        fresh = (projected[..., 2 * model_width :] + b_value.astype(jnp.float32)).astype(
            jnp.bfloat16
        )
        values_low = jnp.concatenate([fresh, first_part], axis=-1)
        query4 = heads_of(queries)
        key_part = lax.all_gather(keys_low, "blk", axis=1, tiled=True)
        value_part = lax.all_gather(values_low, "blk", axis=1, tiled=True)
        span = key_part.shape[1]
        key_pos = jnp.arange(span)
        mask = visible(seg_local, seg_row, own_pos, key_pos)
        scores = score_block(query4, heads_of(key_part), mask)
        old_max = jnp.full((rows_mb, block_len, HEADS), NEG, jnp.float32)
        new_max = jnp.maximum(old_max, jnp.max(scores, axis=-1))
        weights = jnp.where(mask, jnp.exp(scores - new_max[..., None]), 0.0)
        new_sum = jnp.sum(weights, axis=-1)
        new_acc = jnp.einsum(
            "rqhk,rkhd->rqhd",
            weights.astype(jnp.bfloat16),
            heads_of(value_part),
            preferred_element_type=jnp.float32,
        )
        attention4 = new_acc / new_sum[..., None]
        log_total = new_max + jnp.log(new_sum)
        attention_low = attention4.reshape(rows_mb, block_len, model_width).astype(jnp.bfloat16)
        branch = jnp.einsum("rbd,de->rbe", attention_low, w_out, preferred_element_type=jnp.float32)
        middle_state = residual_stream + branch + b_out.astype(jnp.float32)
        second_normed_rows, second_standardized, second_inverse_deviation = apply_norm(
            middle_state, second_gain, second_norm_bias.astype(jnp.float32)
        )
        act2 = second_normed_rows.astype(jnp.bfloat16)
        pre_gelu = jnp.einsum(
            "rbd,df->rbf", act2, w_fc, preferred_element_type=jnp.float32
        ) + b_fc.astype(jnp.float32)
        hidden = gelu_tanh(pre_gelu).astype(jnp.bfloat16)
        result = middle_state + jnp.einsum(
            "rbf,fd->rbd", hidden, w_proj, preferred_element_type=jnp.float32
        )
        result = result + b_proj.astype(jnp.float32)
        outputs.append(result.astype(jnp.bfloat16))
        upstream_gradient = cot_part.astype(jnp.float32)
        grad_wproj = jnp.einsum("rbf,rbd->fd", hidden, cot_part, preferred_element_type=jnp.float32)
        grad_bproj = jnp.sum(upstream_gradient, axis=(0, 1))
        grad_hidden = jnp.einsum(
            "rbd,fd->rbf", cot_part, w_proj, preferred_element_type=jnp.float32
        )
        gelu_value, gelu_pull = jax.vjp(gelu_tanh, pre_gelu)
        grad_pre = gelu_pull(grad_hidden)[0].astype(jnp.bfloat16)
        grad_wfc = jnp.einsum("rbd,rbf->df", act2, grad_pre, preferred_element_type=jnp.float32)
        grad_bfc = jnp.sum(grad_pre.astype(jnp.float32), axis=(0, 1))
        second_activation_gradient = jnp.einsum(
            "rbf,df->rbd", grad_pre, w_fc, preferred_element_type=jnp.float32
        )
        second_norm_gradient, second_gain_gradient, second_bias_gradient = apply_norm_backward(
            second_activation_gradient, second_standardized, second_inverse_deviation, second_gain
        )
        grad_middle = upstream_gradient + second_norm_gradient
        grad_branch = grad_middle.astype(jnp.bfloat16)
        grad_wout = jnp.einsum(
            "rbd,rbe->de", attention_low, grad_branch, preferred_element_type=jnp.float32
        )
        grad_bout = jnp.sum(grad_branch.astype(jnp.float32), axis=(0, 1))
        grad_attention = jnp.einsum(
            "rbe,de->rbd", grad_branch, w_out, preferred_element_type=jnp.float32
        ).astype(jnp.bfloat16)
        dout4 = heads_of(grad_attention)
        out_dot = jnp.sum(dout4.astype(jnp.float32) * attention4, axis=-1)
        back_key_part = lax.all_gather(keys_low, "blk", axis=1, tiled=True)
        back_value_part = lax.all_gather(values_low, "blk", axis=1, tiled=True)
        back_span = back_key_part.shape[1]
        back_key_pos = jnp.arange(back_span)
        back_mask = visible(seg_local, seg_row, own_pos, back_key_pos)
        part_key4 = heads_of(back_key_part)
        probs_low, grad_scores = grad_block(
            query4, part_key4, heads_of(back_value_part), dout4, log_total, out_dot, back_mask
        )
        query_acc = jnp.einsum(
            "rqhk,rkhd->rqhd", grad_scores, part_key4, preferred_element_type=jnp.float32
        )
        key_piece = jnp.einsum(
            "rqhk,rqhd->rkhd", grad_scores, query4, preferred_element_type=jnp.float32
        ).reshape(rows_mb, back_span, model_width)
        value_piece = jnp.einsum(
            "rqhk,rqhd->rkhd", probs_low, dout4, preferred_element_type=jnp.float32
        ).reshape(rows_mb, back_span, model_width)
        query_acc, key_acc, value_acc = (query_acc, key_piece, value_piece)
        grad_keys, grad_values = (
            lax.psum_scatter(
                key_acc.astype(jnp.bfloat16), "blk", scatter_dimension=1, tiled=True
            ).astype(jnp.float32),
            lax.psum_scatter(
                value_acc.astype(jnp.bfloat16), "blk", scatter_dimension=1, tiled=True
            ).astype(jnp.float32),
        )
        grad_query = query_acc.reshape(rows_mb, block_len, model_width)
        grad_qkv = jnp.concatenate(
            [
                grad_query.astype(jnp.bfloat16),
                grad_keys.astype(jnp.bfloat16),
                grad_values[..., :val_width].astype(jnp.bfloat16),
            ],
            axis=-1,
        )
        first_grads.append(grad_values[..., val_width:].astype(jnp.bfloat16))
        grad_wqkv = jnp.einsum("rbd,rbe->de", act1, grad_qkv, preferred_element_type=jnp.float32)
        grad_bquery = jnp.sum(grad_qkv[..., :model_width].astype(jnp.float32), axis=(0, 1))
        grad_bvalue = jnp.sum(grad_qkv[..., 2 * model_width :].astype(jnp.float32), axis=(0, 1))
        first_activation_gradient = jnp.einsum(
            "rbe,de->rbd", grad_qkv, w_qkv, preferred_element_type=jnp.float32
        )
        first_norm_gradient, first_gain_gradient, first_bias_gradient = apply_norm_backward(
            first_activation_gradient, first_standardized, first_inverse_deviation, first_gain
        )
        input_grads.append((grad_middle + first_norm_gradient).astype(jnp.bfloat16))
        gradient_set = (
            first_gain_gradient,
            first_bias_gradient,
            grad_wqkv,
            grad_bquery,
            grad_bvalue,
            grad_wout,
            grad_bout,
            second_gain_gradient,
            second_bias_gradient,
            grad_wfc,
            grad_bfc,
            grad_wproj,
            grad_bproj,
        )
        if totals is None:
            totals = gradient_set
        else:
            totals = tuple((older + newer for older, newer in zip(totals, gradient_set)))
    totals = jax.tree.map(
        lambda part: part.astype(jnp.float32),
        lax.psum_scatter(as_sent(totals), "batch", scatter_dimension=0, tiled=True),
    )
    totals = jax.tree.map(lambda part: part.astype(jnp.float32), lax.psum(as_sent(totals), "blk"))
    return (
        jnp.concatenate(outputs, axis=0),
        jnp.concatenate(input_grads, axis=0),
        jnp.concatenate(first_grads, axis=0),
    ) + tuple(totals)


def layer(inputs, *rest):
    whole_rows = lax.axis_size("blk") == inputs.shape[0] == 2 and inputs.shape[1] == 2 * QB
    whole_rows = whole_rows and lax.axis_size("batch") == 16
    return (paired if whole_rows else spread)(inputs, *rest)


def solution(mesh):
    rows = P("batch", "blk", None)
    flat = P("batch")
    wide = P("batch", None)
    return jax.shard_map(
        layer,
        mesh=mesh,
        in_specs=(rows, rows, P("batch", "blk")) + (P(),) * 13 + (rows,),
        out_specs=(rows, rows, rows)
        + (flat, flat, wide, flat, flat, wide, flat, flat, flat, wide, flat, wide, flat),
        check_vma=False,
    )
```

```python
import functools

import jax
import jax.numpy as jnp
from jax import lax
from jax.experimental import pallas as pl
from jax.experimental.pallas import tpu as pltpu
from jax.sharding import PartitionSpec as P

HEADS = 12
HEAD_DIM = 64
PAIRS = HEADS // 2
LANES = 2 * HEAD_DIM
EPS = 1e-05
NEG = -1e30
QB = 256
F32 = jnp.float32
BF = jnp.bfloat16
MIB = 2**20
MESH = pl.DeviceIdType.MESH


def nn(a, b):
    return lax.dot_general(a, b, (((1,), (0,)), ((), ())), preferred_element_type=F32)


def nt(a, b):
    return lax.dot_general(a, b, (((1,), (1,)), ((), ())), preferred_element_type=F32)


def tn(a, b):
    return lax.dot_general(a, b, (((0,), (0,)), ((), ())), preferred_element_type=F32)


def norm_parts(rows):
    mean = jnp.mean(rows, axis=-1, keepdims=True)
    centred = rows - mean
    inverse = lax.rsqrt(jnp.mean(centred * centred, axis=-1, keepdims=True) + EPS)
    return centred * inverse, inverse


def norm_pull(grad, xhat, inverse, gain):
    scaled = grad * gain
    first = jnp.mean(scaled, axis=-1, keepdims=True)
    second = jnp.mean(scaled * xhat, axis=-1, keepdims=True)
    return inverse * (scaled - first - xhat * second)


def row(ref):
    return ref[...].astype(F32).reshape(1, -1)


def column_sum(rows):
    return jnp.sum(rows, axis=0, keepdims=True)


def spot():
    b = lax.axis_index("batch")
    core = lax.rem(b, 2)
    x = lax.rem(lax.div(b, 2), 2)
    near = lax.rem(lax.div(b, 4), 2)
    far = lax.div(b, 8)
    return b, core, x, near, far


def partners():
    b, core, x, near, far = spot()
    return [
        {"batch": b + 1 - 2 * core},
        {"batch": b + 2 - 4 * x},
        {"batch": b + 4 - 8 * near},
        {"batch": b + 8 - 16 * far},
        {"blk": 1 - lax.axis_index("blk")},
    ]


def greet(friends):
    barrier = pltpu.get_barrier_semaphore()
    for friend in friends:
        pl.semaphore_signal(barrier, inc=1, device_id=friend, device_id_type=MESH)
    pl.semaphore_wait(barrier, len(friends))


def push(src, dst, send_sem, recv_sem, friend):
    copy = pltpu.make_async_remote_copy(
        src_ref=src,
        dst_ref=dst,
        send_sem=send_sem,
        recv_sem=recv_sem,
        device_id=friend,
        device_id_type=MESH,
    )
    return copy


def add_into(dst, src):
    dst[...] = dst[...] + src[...]


PLACES = ("core", "x", "near", "far")


class Sum:
    def __init__(self, held, got, dims, order, send_sem, recv_sem, cut_columns=True):
        self.held, self.got, self.dims, self.order = held, got, dims, order
        self.send_sem, self.recv_sem, self.cut_columns = send_sem, recv_sem, cut_columns

    def cut(self, stage, keep):
        name = self.order[stage]
        done = self.order[:stage]
        _, core, x, near, far = spot()
        own = {"core": core, "x": x, "near": near, "far": far}
        at = []
        for dim in self.dims:
            if dim == name:
                at.append(own[dim] if keep else 1 - own[dim])
            else:
                at.append(own[dim] if dim in done else slice(None))
        if self.cut_columns and (name == "half" or "half" in done):
            me = lax.axis_index("blk")
            size = self.held.shape[-1] // 2
            side = 1 - me if name == "half" and not keep else me
            at += [slice(None), pl.ds(pl.multiple_of(side * size, size), size)]
        return tuple(at)

    def copy(self, stage):
        name = self.order[stage]
        return push(
            self.held.at[self.cut(stage, False)],
            self.got[stage],
            self.send_sem.at[stage],
            self.recv_sem.at[stage],
            partners()[PLACES.index(name) if name in PLACES else 4],
        )

    def start(self, stage):
        self.copy(stage).start()

    def take(self, stage):
        self.copy(stage).wait()
        mine = self.held.at[self.cut(stage, True)]
        came = self.got[stage]
        lead = came.shape[:-2]
        count = 1
        for size in lead:
            count *= size
        for n in range(count):
            at = []
            for size in reversed(lead):
                at.insert(0, n % size)
                n //= size
            at = tuple(at)
            add_into(mine.at[at] if at else mine, came.at[at] if at else came)
        if stage + 1 < len(self.order):
            self.start(stage + 1)

    def last(self):
        stage = len(self.order) - 1
        self.copy(stage).wait()
        return self.held[self.cut(stage, True)].astype(F32), self.got[stage][...].astype(F32)


def front_kernel(
    x_in,
    fv_in,
    seg_in,
    cot_in,
    g1_ref,
    b1_ref,
    wqkv_in,
    bq_ref,
    bv_ref,
    wout_in,
    bout_ref,
    g2_ref,
    b2_ref,
    x_out,
    q_out,
    k_out,
    v_out,
    att_out,
    act2_out,
    mid_out,
    lse_ref,
    bias_out,
    act1t_out,
    cot_out,
    xs,
    qs,
    ks,
    vs,
    atts,
    act2s,
    mids,
    bias,
    wqkv,
    wout,
    segrow,
    segsend,
    segcol,
    act1ts,
    in_sem,
    out_sem,
    send_sem,
    recv_sem,
):
    half = x_in.shape[1]
    tokens = 2 * half
    width = x_in.shape[2]
    val = fv_in.shape[2]
    steps = tokens // QB
    me = lax.axis_index("blk")
    other = 1 - me
    mine = pl.multiple_of(me * half, half)
    theirs = pl.multiple_of(other * half, half)

    def local_in(i, src, dst):
        copy = pltpu.make_async_copy(src, dst, in_sem.at[i])
        copy.start()
        return copy

    own_x = local_in(0, x_in.at[me], xs.at[pl.ds(mine, half)])
    own_fv = local_in(1, fv_in.at[me], vs.at[pl.ds(mine, half), pl.ds(val, val)])
    own_w = local_in(2, wqkv_in, wqkv)
    own_wo = local_in(3, wout_in, wout)
    first, second = seg_in[0:1, :], seg_in[1:2, :]
    segsend[...] = jnp.broadcast_to(jnp.where(me == 0, second, first), segsend.shape)

    barrier = pltpu.get_barrier_semaphore()
    pl.semaphore_signal(barrier, inc=1, device_id={"blk": other}, device_id_type=MESH)
    pl.semaphore_wait(barrier, 1)

    def remote(i, src, dst):
        copy = pltpu.make_async_remote_copy(
            src_ref=src,
            dst_ref=dst,
            send_sem=send_sem.at[i],
            recv_sem=recv_sem.at[i],
            device_id={"blk": other},
            device_id_type=MESH,
        )
        copy.start()
        return copy

    part = half // 2
    far_x = [
        remote(
            c,
            x_in.at[other, pl.ds(c * part, part)],
            xs.at[pl.ds(pl.multiple_of(mine + c * part, part), part)],
        )
        for c in range(2)
    ]
    far_seg = remote(2, segsend, segrow.at[:, pl.ds(mine, half)])
    far_fv = remote(3, fv_in.at[other], vs.at[pl.ds(mine, half), pl.ds(val, val)])
    far_cot = remote(4, cot_in.at[other, pl.ds(0, part)], cot_out)

    own_row = jnp.broadcast_to(jnp.where(me == 0, first, second), (8, half))
    segrow[:, pl.ds(mine, half)] = own_row

    def project(start):
        rows = pl.ds(pl.multiple_of(start, QB), QB)
        xhat, _ = norm_parts(xs[rows, :].astype(F32))
        act1 = (xhat * row(g1_ref) + row(b1_ref)).astype(BF)
        act1ts[:, rows] = act1.T
        out = nn(act1, wqkv[...])
        query = (out[:, :width] + row(bq_ref)).astype(BF)
        qs[rows, :] = query * jnp.asarray(HEAD_DIM**-0.5, BF)
        ks[rows, :] = out[:, width : 2 * width].astype(BF)
        vs[rows, pl.ds(0, val)] = (out[:, 2 * width :] + row(bv_ref)).astype(BF)

    own_x.wait()
    own_w.wait()
    for c in range(2):
        project(mine + c * QB)
    for c in range(2):
        far_x[c].wait()
        project(theirs + c * part)

    outs = []

    def local_out(src, dst):
        copy = pltpu.make_async_copy(src, dst, out_sem.at[len(outs)])
        copy.start()
        outs.append(copy)

    local_out(act1ts, act1t_out)
    local_out(xs, x_out)
    local_out(qs, q_out)
    local_out(ks, k_out)

    far_seg.wait()
    for c in range(tokens // LANES):
        line = segrow[0:1, c * LANES : (c + 1) * LANES].astype(F32)
        segcol[c * LANES : (c + 1) * LANES, :] = jnp.broadcast_to(line, (LANES, LANES)).T
    for j in range(steps):
        key = segcol[j * QB : (j + 1) * QB, :]
        key = jnp.concatenate([key] * (QB // LANES), axis=1)
        for i in range(j, steps):
            query = segrow[0:1, i * QB : (i + 1) * QB].astype(F32)
            seen = (key == query) & (query >= 0.0)
            if i == j:
                down = lax.broadcasted_iota(jnp.int32, (QB, QB), 0)
                across = lax.broadcasted_iota(jnp.int32, (QB, QB), 1)
                seen = (seen & (down <= across)) | (down == across)
            bias[j * QB : (j + 1) * QB, i * QB : (i + 1) * QB] = jnp.where(seen, 0.0, NEG)
        cut = (pl.ds(j * QB, QB), pl.ds(j * QB, tokens - j * QB))
        local_out(bias.at[cut], bias_out.at[cut])
    low = lax.broadcasted_iota(jnp.int32, (1, LANES), 1) < HEAD_DIM

    @pl.loop(0, PAIRS)
    def _(p):
        @pl.when(p == PAIRS // 2)
        def _():
            own_fv.wait()
            far_fv.wait()

        cols = pl.ds(pl.multiple_of(p * LANES, LANES), LANES)
        k = ks[:, cols]
        v = vs[:, cols]

        def score(i, h):
            q = qs[i * QB : (i + 1) * QB, cols]
            q = jnp.where(low if h == 0 else ~low, q, jnp.zeros_like(q))
            span = (i + 1) * QB
            return nt(k[:span], q) + bias[:span, i * QB : span]

        done = {}

        def finish(i, h, s):
            span = (i + 1) * QB
            top = jnp.max(s, axis=0, keepdims=True)
            e = jnp.exp(s - top)
            total = jnp.sum(e, axis=0, keepdims=True)
            done[h] = tn((e * (1.0 / total)).astype(BF), v[:span])
            lse_ref[p, h : h + 1, i * QB : span] = top + jnp.log(total)
            if h == 1:
                atts[i * QB : span, cols] = jnp.where(low, done[0], done[1]).astype(BF)

        waiting = []
        for i in range(steps):
            for h in range(2):
                waiting.append((i, h, score(i, h)))
                if len(waiting) > 2:
                    finish(*waiting.pop(0))
        for item in waiting:
            finish(*item)

    local_out(atts, att_out)
    local_out(vs, v_out)
    own_wo.wait()
    for c in range(steps):
        rows = slice(c * QB, (c + 1) * QB)
        middle = xs[rows, :].astype(F32) + nn(atts[rows, :], wout[...]) + row(bout_ref)
        mids[rows, :] = middle
        xhat, _ = norm_parts(middle)
        act2s[rows, :] = (xhat * row(g2_ref) + row(b2_ref)).astype(BF)
    local_out(mids, mid_out)
    local_out(act2s, act2_out)
    for copy in outs:
        copy.wait()
    far_cot.wait()


def front(x, fv, seg, cot, g1, b1, wqkv, bq, bv, wout, bout, g2, b2):
    half, width, val = x.shape[1], x.shape[2], fv.shape[2]
    tokens = 2 * half
    hbm = pl.BlockSpec(memory_space=pl.ANY)
    vmem = pl.BlockSpec(memory_space=pltpu.VMEM)
    flat = jax.ShapeDtypeStruct((tokens, width), BF)
    shape = jax.ShapeDtypeStruct
    return pl.pallas_call(
        front_kernel,
        in_specs=[hbm, hbm, vmem, hbm, vmem, vmem, hbm, vmem, vmem, hbm, vmem, vmem, vmem],
        out_specs=[hbm] * 7 + [vmem] + [hbm] * 3,
        out_shape=[
            flat,
            flat,
            flat,
            flat,
            flat,
            flat,
            shape((tokens, width), F32),
            shape((PAIRS, 2, tokens), F32),
            shape((tokens, tokens), F32),
            shape((width, tokens), BF),
            shape((half // 2, width), BF),
        ],
        scratch_shapes=[
            pltpu.VMEM((tokens, width), BF),
            pltpu.VMEM((tokens, width), BF),
            pltpu.VMEM((tokens, width), BF),
            pltpu.VMEM((tokens, width), BF),
            pltpu.VMEM((tokens, width), BF),
            pltpu.VMEM((tokens, width), BF),
            pltpu.VMEM((tokens, width), F32),
            pltpu.VMEM((tokens, tokens), F32),
            pltpu.VMEM(wqkv.shape, BF),
            pltpu.VMEM(wout.shape, BF),
            pltpu.VMEM((8, tokens), jnp.int32),
            pltpu.VMEM((8, half), jnp.int32),
            pltpu.VMEM((tokens, LANES), F32),
            pltpu.VMEM((width, tokens), BF),
            pltpu.SemaphoreType.DMA((5,)),
            pltpu.SemaphoreType.DMA((8 + tokens // QB,)),
            pltpu.SemaphoreType.DMA((5,)),
            pltpu.SemaphoreType.DMA((5,)),
        ],
        compiler_params=pltpu.CompilerParams(
            collective_id=0, has_side_effects=True, vmem_limit_bytes=56 * MIB
        ),
        name="front",
    )(x, fv, seg, cot, g1, b1, wqkv, bq, bv, wout, bout, g2, b2)


def feed_kernel(
    act2,
    g2_ref,
    bproj_ref,
    bfc_ref,
    wfc,
    wproj,
    cot_in,
    cot_far,
    mid_in,
    att_in,
    wout_in,
    lout_out,
    gmid_out,
    gatt_out,
    dwout_out,
    f0_out,
    f12_out,
    f3_out,
    p01_out,
    p2_out,
    p3_out,
    dots,
    dbfc,
    small,
    cots,
    mids,
    atts,
    wout,
    acc,
    act2t,
    hid,
    slope,
    dpre,
    louts,
    gatts,
    dwouts,
    sel,
    bias,
    gf,
    gp,
    rf0,
    rp0,
    rf1,
    rp1,
    rfh,
    in_sem,
    out_sem,
    send_sem,
    recv_sem,
):
    t = pl.program_id(0)
    tiles = pl.num_programs(0) // 2
    tokens, width = act2.shape
    half = tokens // 2
    tile = dpre.shape[1]
    steps = tokens // QB
    count = gf.shape[0]
    _, core, x, _, _ = spot()
    me = lax.axis_index("blk")
    mine = pl.multiple_of(me * half, half)
    theirs = pl.multiple_of((1 - me) * half, half)
    both = partners()
    friends = [both[0], both[1], both[4]]
    side = pl.ds(pl.multiple_of(me * (tile // 2), tile // 2), tile // 2)

    def chain(held, got, dims, order, n):
        return Sum(held, got, dims, order, send_sem.at[n], recv_sem.at[n])

    full = ("far", "near", "x", "core")
    fcs = [
        chain(gf.at[0], [rf0.at[0], rf1], full, ("core", "x"), 0),
        chain(gf.at[1], [rf0.at[1], rfh.at[0]], full, ("core", "half"), 1),
        chain(gf.at[2], [rf0.at[2], rfh.at[1]], full, ("core", "half"), 2),
    ]
    projs = [
        chain(gp.at[0], [rp0.at[0], rp1.at[0]], full[2:], ("core", "x"), 3),
        chain(gp.at[1], [rp0.at[1], rp1.at[1]], full[2:], ("core", "x"), 4),
        chain(gp.at[2], [rp0.at[2]], full[2:], ("core",), 5),
    ]

    def load(n):
        src, dst = [
            (cot_in.at[me], cots.at[pl.ds(mine, half)]),
            (cot_far, cots.at[pl.ds(theirs, half // 2)]),
            (mid_in, mids),
            (att_in, atts),
            (wout_in, wout),
        ][n]
        return pltpu.make_async_copy(src, dst, in_sem.at[n])

    far_cot = push(
        cot_in.at[1 - me, pl.ds(half // 2, half // 2)],
        cots.at[pl.ds(pl.multiple_of(mine + half // 2, half // 2), half // 2)],
        send_sem.at[6, 0],
        recv_sem.at[6, 0],
        friends[2],
    )
    back = push(
        louts.at[pl.ds(theirs, half)], lout_out.at[me], send_sem.at[6, 1], recv_sem.at[6, 1], friends[2]
    )

    stores = [
        (louts.at[pl.ds(mine, half)], lout_out.at[me]),
        (acc, gmid_out),
        (gatts, gatt_out),
        (dwouts, dwout_out),
        (gf.at[0, :, :, x, core], f0_out),
        (gf.at[1, :, :, :, core, :, side], f12_out.at[:, :, :, :, 0 : tile // 2]),
        (gf.at[2, :, :, :, core, :, side], f12_out.at[:, :, :, :, tile // 2 : tile]),
        (gf.at[3], f3_out),
        (gp.at[0, x, core], p01_out.at[0]),
        (gp.at[1, x, core], p01_out.at[1]),
        (gp.at[2, :, core], p2_out),
        (gp.at[3], p3_out),
    ]

    def store(n):
        return pltpu.make_async_copy(stores[n][0], stores[n][1], out_sem.at[n])

    def at_step(k, *actions):
        @pl.when(t == k)
        def _():
            for action in actions:
                action()

    @pl.when(t == 0)
    def _():
        for n in range(5):
            load(n).start()
        greet(friends)
        far_cot.start()
        act2t[...] = act2[...].T
        for n in range(count):
            bias[n] = row(bfc_ref)[:, n * tile : (n + 1) * tile]
        acc[...] = jnp.zeros_like(acc)
        head = lax.broadcasted_iota(jnp.int32, sel.shape, 0)
        feature = lax.broadcasted_iota(jnp.int32, sel.shape, 1)
        inside = (feature >= head * HEAD_DIM) & (feature < (head + 1) * HEAD_DIM)
        sel[...] = jnp.where(inside, 1.0, 0.0).astype(BF)

    @pl.when(t < tiles)
    def _():
        for c in range(steps):
            rows = slice(c * QB, (c + 1) * QB)
            u = nn(act2[rows, :], wfc[...]) + bias[t]
            square = u * u
            bend = jnp.tanh(u * (0.7978845608028654 + (0.7978845608028654 * 0.044715) * square))
            halfway = 0.5 + 0.5 * bend
            hidden = (u * halfway).astype(BF)
            hid[t, rows, :] = hidden
            slope[t, rows, :] = (
                halfway
                + (u * (0.5 - 0.5 * bend * bend))
                * (0.7978845608028654 + (3 * 0.7978845608028654 * 0.044715) * square)
            ).astype(BF)
            acc[rows, :] += nn(hidden, wproj[...])

    @pl.when(t == tiles - 1)
    def _():
        load(2).wait()
        for c in range(steps):
            rows = slice(c * QB, (c + 1) * QB)
            louts[rows, :] = (mids[rows, :] + acc[rows, :] + row(bproj_ref)).astype(BF)
        back.start()
        store(0).start()
        acc[...] = jnp.zeros_like(acc)
        load(0).wait()
        load(1).wait()
        far_cot.wait()

    @pl.when(t >= tiles)
    def _():
        n = t - tiles
        total = None
        for c in range(steps):
            rows = slice(c * QB, (c + 1) * QB)
            grad = (nt(cots[rows, :], wproj[...]) * slope[n, rows, :].astype(F32)).astype(BF)
            dpre[rows, :] = grad
            acc[rows, :] += nt(grad, wfc[...])
            part = column_sum(grad.astype(F32))
            total = part if total is None else total + part
            if c == 2:
                for k in range(3):
                    at_step(tiles + k + 1, lambda k=k: projs[k].take(0), lambda k=k: fcs[k].take(0))
        dbfc[...] = total
        gp[n] = tn(hid[n], cots[...]).astype(BF).reshape(gp.shape[1:])
        gf[n] = nn(act2t[...], dpre[...]).astype(BF).reshape(gf.shape[1:])

    for k in range(3):
        at_step(tiles + k, lambda k=k: projs[k].start(0), lambda k=k: fcs[k].start(0))

    @pl.when(t == 2 * tiles - 1)
    def _():
        for n in (7, 10, 11):
            store(n).start()
        load(3).wait()
        load(4).wait()
        projs[0].take(1)
        store(8).start()
        gain = row(g2_ref)
        sums = [None] * 4
        for c in range(steps):
            rows = slice(c * QB, (c + 1) * QB)
            middle = mids[rows, :]
            upstream = cots[rows, :].astype(F32)
            xhat, inverse = norm_parts(middle)
            da = acc[rows, :]
            grad_middle = upstream + norm_pull(da, xhat, inverse, gain)
            acc[rows, :] = grad_middle
            branch = grad_middle.astype(BF)
            dpre[rows, :] = branch
            parts = [
                column_sum(upstream),
                column_sum(da * xhat),
                column_sum(da),
                column_sum(branch.astype(F32)),
            ]
            sums = [b if a is None else a + b for a, b in zip(sums, parts)]
            ga = nt(branch, wout[...]).astype(BF)
            gatts[rows, :] = ga
            product = ga.astype(F32) * atts[rows, :].astype(F32)
            big = product.astype(BF)
            rest = (product - big.astype(F32)).astype(BF)
            dot = nt(sel[...], big) + nt(sel[...], rest)
            for p in range(PAIRS):
                dots[p, :, rows] = dot[2 * p : 2 * p + 2, :]
        store(1).start()
        store(2).start()
        small[...] = jnp.concatenate(sums, axis=0)
        dwouts[...] = tn(atts[...], dpre[...]).astype(BF).reshape(dwouts.shape)
        store(3).start()
        fcs[0].take(1)
        store(4).start()
        fcs[1].take(1)
        store(5).start()
        projs[1].take(1)
        store(9).start()
        fcs[2].take(1)
        store(6).start()
        for n in range(len(stores)):
            store(n).wait()
        back.wait()


def feed(act2, cotangent, cot_far, mid, att, g2, bproj, wout, wfc, bfc, wproj):
    tokens, width = act2.shape
    half = tokens // 2
    ff = wfc.shape[1]
    tiles = 4
    tile = ff // tiles
    owner = width // 16
    owner_ff = ff // 16
    shape = jax.ShapeDtypeStruct
    flat = shape((tokens, width), BF)
    once = pl.Buffered(1)
    hbm = pl.BlockSpec(memory_space=pl.ANY)

    def whole(s):
        return pl.BlockSpec(s, lambda t: (0,) * len(s), pipeline_mode=once)

    def vm(*s):
        return pltpu.VMEM(s, BF)

    line = whole((width,))
    return pl.pallas_call(
        feed_kernel,
        grid=(2 * tiles,),
        in_specs=[
            whole((tokens, width)),
            line,
            line,
            whole((ff,)),
            pl.BlockSpec((width, tile), lambda t: (0, lax.rem(t, tiles))),
            pl.BlockSpec((tile, width), lambda t: (lax.rem(t, tiles), 0)),
        ]
        + [hbm] * 5,
        out_specs=[hbm] * 10
        + [
            whole((PAIRS, 2, tokens)),
            pl.BlockSpec((1, tile), lambda t: (0, jnp.maximum(t - tiles, 0))),
            whole((4, width)),
        ],
        out_shape=[
            shape((2, half, width), BF),
            shape((tokens, width), F32),
            flat,
            shape((2, 2, 2, 2, owner, width), BF),
            shape((2, 2, owner, tile), BF),
            shape((2, 2, 2, owner, tile), BF),
            shape((2, 2, 2, 2, owner, tile), BF),
            shape((2, owner_ff, width), BF),
            shape((2, owner_ff, width), BF),
            shape((2, 2, owner_ff, width), BF),
            shape((PAIRS, 2, tokens), F32),
            shape((1, ff), F32),
            shape((4, width), F32),
        ],
        scratch_shapes=[
            vm(tokens, width),
            pltpu.VMEM((tokens, width), F32),
            vm(tokens, width),
            vm(width, width),
            pltpu.VMEM((tokens, width), F32),
            vm(width, tokens),
            vm(tiles, tokens, tile),
            vm(tiles, tokens, tile),
            vm(tokens, tile),
            vm(tokens, width),
            vm(tokens, width),
            vm(2, 2, 2, 2, owner, width),
            vm(16, width),
            pltpu.VMEM((tiles, 1, tile), F32),
            vm(tiles, 2, 2, 2, 2, owner, tile),
            vm(tiles, 2, 2, owner_ff, width),
            vm(3, 2, 2, 2, owner, tile),
            vm(3, 2, owner_ff, width),
            vm(2, 2, owner, tile),
            vm(2, owner_ff, width),
            vm(2, 2, 2, 2, owner, tile // 2),
            pltpu.SemaphoreType.DMA((5,)),
            pltpu.SemaphoreType.DMA((12,)),
            pltpu.SemaphoreType.DMA((7, 2)),
            pltpu.SemaphoreType.DMA((7, 2)),
        ],
        compiler_params=pltpu.CompilerParams(
            collective_id=1, has_side_effects=True, vmem_limit_bytes=62 * MIB
        ),
        name="feed",
    )(act2, g2, bproj, bfc, wfc, wproj, cotangent, cot_far, mid, att, wout)


FIRST_PAIR = PAIRS // 2


def pieces(width, val):
    lanes = LANES
    return [
        (3, [(3 * lanes, 3 * lanes), (width + 3 * lanes, 3 * lanes)]),
        (5, [(0, 2 * lanes), (width, 2 * lanes), (2 * width, 2 * lanes)]),
        (6, [(2 * lanes, lanes), (width + 2 * lanes, lanes), (2 * width + 2 * lanes, lanes)]),
    ]


def tail_kernel(
    q_in,
    k_in,
    v_in,
    do_in,
    bias_in,
    x_in,
    act1t_in,
    gmid_in,
    wqkv_in,
    dwout_in,
    f0_in,
    f12_in,
    f3_in,
    p01_in,
    p2_in,
    p3_in,
    lse_ref,
    d_ref,
    g1_ref,
    dbfc_ref,
    small_in,
    gx_out,
    gf_out,
    wqkv_out,
    wout_out,
    wfc_out,
    wproj_out,
    small_out,
    q_ref,
    k_ref,
    v_ref,
    do_ref,
    bias,
    xs,
    gmid,
    wqkv,
    dqk,
    dvs,
    gfs,
    dqa,
    act1t,
    gx,
    g_out,
    g_f0,
    g_f12,
    g_f3,
    g_ph,
    g_p2,
    g_p3,
    g_q,
    r_out,
    r_f0,
    r_f12,
    r_f3,
    r_ph,
    r_p2,
    r_p3,
    r_q,
    sums,
    s_got,
    in_sem,
    out_sem,
    back_send,
    back_recv,
    sum_send,
    sum_recv,
):
    tokens, width = q_ref.shape
    half = tokens // 2
    val = gfs.shape[1]
    steps = tokens // QB
    me = lax.axis_index("blk")
    mine = pl.multiple_of(me * half, half)
    theirs = pl.multiple_of((1 - me) * half, half)
    _, core, x, near, far = spot()
    friends = partners()
    parts = pieces(width, val)

    sources = {
        "p3": (p3_in, g_p3),
        "f3": (f3_in, g_f3),
        "out": (dwout_in, g_out),
        "p2": (p2_in, g_p2),
        "f12": (f12_in, g_f12),
        "p01": (p01_in, g_ph.at[0]),
        "f0": (f0_in, g_f0),
        "q": (q_in, q_ref),
        "k": (k_in, k_ref),
        "bias": (bias_in, bias),
        "v": (v_in, v_ref),
        "do": (do_in, do_ref),
        "act1t": (act1t_in, act1t),
        "x": (x_in, xs),
        "wqkv": (wqkv_in, wqkv),
        "gmid": (gmid_in, gmid),
    }
    loads = {
        name: pltpu.make_async_copy(src, dst, in_sem.at[n])
        for n, (name, (src, dst)) in enumerate(sources.items())
    }
    for load in loads.values():
        load.start()
    greet(friends)

    full = ("far", "near", "x", "core")
    down = ("core", "x", "near", "far", "pair")
    sems = iter(range(16))

    def chain(held, got, dims, order, cut_columns=True):
        n = next(sems)
        return Sum(held, got, dims, order, sum_send.at[n], sum_recv.at[n], cut_columns)

    across = ("core", "half", "x", "near", "far", "gather")
    s_out = chain(g_out, r_out, full, across)
    s_f3 = chain(g_f3, r_f3, full, across)
    s_f0 = chain(g_f0, r_f0, full[:2], ("near", "far", "pair"))
    s_f12 = chain(g_f12, r_f12, full[:3], ("x", "near", "far", "gather"), False)
    s_p2 = chain(g_p2, r_p2, full[2:3], ("x",))
    s_p3 = chain(g_p3, r_p3, full[2:], ("core", "x"))
    s_pa = chain(g_ph.at[0], r_ph[0:1], full[1:2], ("near",))
    s_pb = chain(g_ph.at[1], r_ph[1:2], full[1:2], ("near",))
    s_ph = chain(g_ph, [None] + list(r_ph[2:]), full[:2], ("near", "far", "pair"))
    s_q = [chain(g, r, full, down) for g, r in zip(g_q, r_q)]
    s_small = next(sems)

    def small_copy(stage):
        return push(
            sums.at[stage],
            s_got.at[stage],
            sum_send.at[s_small, stage],
            sum_recv.at[s_small, stage],
            friends[stage],
        )

    def give_back(n, src, dst):
        return push(src, dst, back_send.at[n], back_recv.at[n], friends[4])

    for name, begin in (
        ("p3", s_p3),
        ("f3", s_f3),
        ("out", s_out),
        ("p2", s_p2),
        ("f12", s_f12),
        ("p01", s_pa),
        ("f0", s_f0),
    ):
        loads[name].wait()
        begin.start(0)
    for name in ("q", "k", "bias", "v", "do"):
        loads[name].wait()

    low = lax.broadcasted_iota(jnp.int32, (1, LANES), 1) < HEAD_DIM
    masks = [low, ~low]
    zero = jnp.zeros((), BF)
    gain = row(g1_ref)

    def columns(at, size):
        return dqk[:, at : at + size] if at < 2 * width else dvs[:, at - 2 * width : at - 2 * width + size]

    def project_grad(n):
        at = 0
        for start, size in parts[n][1]:
            block = nn(act1t[...], columns(start, size)).astype(BF)
            g_q[n][:, :, :, :, :, at : at + size] = block.reshape(g_q[n].shape[:-1] + (size,))
            at += size
        s_q[n].start(0)

    def second_tile():
        s_p2.take(0)
        g_ph[1, 0] = g_p2[x]

    def third_tile():
        s_p3.take(1)
        g_ph[1, 1] = g_p3[x, core]
        s_pb.start(0)

    back_gf = give_back(1, gfs.at[pl.ds(theirs, half)], gf_out.at[me])
    keep_gf = pltpu.make_async_copy(gfs.at[pl.ds(mine, half)], gf_out.at[me], out_sem.at[1])

    plan = {
        (1, 0): [
            lambda: s_p3.take(0),
            lambda: s_f3.take(0),
            lambda: s_out.take(0),
            lambda: s_f0.take(0),
        ],
        (2, 0): [second_tile, lambda: s_pa.take(0), loads["act1t"].wait],
        (3, 0): [
            lambda: project_grad(0),
            back_gf.start,
            keep_gf.start,
            lambda: s_f12.take(0),
            lambda: s_f3.take(1),
            lambda: s_f0.take(1),
        ],
        (3, 1): [lambda: s_q[0].take(0)],
        (4, 0): [third_tile, lambda: s_out.take(1), lambda: s_f12.take(1)],
        (5, 0): [
            lambda: project_grad(1),
            lambda: s_f3.take(2),
            lambda: s_f12.take(2),
        ],
        (5, 1): [
            lambda: s_q[1].take(0),
            lambda: s_pb.take(0),
            lambda: s_ph.start(1),
            lambda: s_out.take(2),
        ],
    }

    def act(step, middle):
        for (k, when), actions in plan.items():
            if when == middle:

                @pl.when(step == k)
                def _():
                    for action in actions:
                        action()

    @pl.loop(0, PAIRS)
    def _(step):
        act(step, 0)
        p = lax.rem(step + FIRST_PAIR, PAIRS)
        cols = pl.ds(pl.multiple_of(p * LANES, LANES), LANES)
        kcols = pl.ds(pl.multiple_of(width + p * LANES, LANES), LANES)
        q, k, v, do = q_ref[:, cols], k_ref[:, cols], v_ref[:, cols], do_ref[:, cols]
        qm = [jnp.where(m, q, zero) for m in masks]
        km = [jnp.where(m, k, zero) for m in masks]
        dom = [jnp.where(m, do, zero) for m in masks]
        dvals = []
        for j in range(steps):
            a = j * QB
            keys = slice(a, a + QB)
            dk = dv = dq = None
            for h in range(2):
                s = nt(k[keys], qm[h][a:]) + bias[keys, a:]
                probs = jnp.exp(s - lse_ref[p, h : h + 1, a:])
                dp = nt(v[keys], dom[h][a:])
                ds = (probs * (dp - d_ref[p, h : h + 1, a:])).astype(BF)
                dvh = nn(probs.astype(BF), dom[h][a:])
                dkh = nn(ds, qm[h][a:])
                dqh = tn(ds, km[h][keys])
                dk = dkh if dk is None else dk + dkh
                dv = dvh if dv is None else dv + dvh
                dq = dqh if dq is None else dq + dqh
            dqk[keys, kcols] = dk.astype(BF)
            dvals.append(dv.astype(BF))
            if j == 1:
                act(step, 1)
            if j == 0:
                dqa[...] = dq
            else:
                dqa[a:, :] += dq
        dqk[:, cols] = (dqa[...] * HEAD_DIM**-0.5).astype(BF)

        @pl.when(p < PAIRS // 2)
        def _():
            for j in range(steps):
                dvs[j * QB : (j + 1) * QB, cols] = dvals[j]

        @pl.when(p >= PAIRS // 2)
        def _():
            late = pl.ds(pl.multiple_of(p * LANES - val, LANES), LANES)
            for j in range(steps):
                gfs[j * QB : (j + 1) * QB, late] = dvals[j]

    project_grad(2)
    s_q[0].take(1)
    for name in ("x", "wqkv", "gmid"):
        loads[name].wait()

    totals = [None] * 4

    def input_grad(start):
        rows = pl.ds(pl.multiple_of(start, QB), QB)
        da = nt(dqk[rows, :], wqkv[:, : 2 * width]) + nt(dvs[rows, :], wqkv[:, 2 * width :])
        xhat, inverse = norm_parts(xs[rows, :].astype(F32))
        gx[rows, :] = (gmid[rows, :] + norm_pull(da, xhat, inverse, gain)).astype(BF)
        bv = column_sum(dvs[rows, :].astype(F32))
        found = [
            column_sum(da * xhat),
            column_sum(da),
            column_sum(dqk[rows, :width].astype(F32)),
            jnp.concatenate([bv, jnp.zeros((1, width - val), F32)], axis=1),
        ]
        totals[:] = [b if a is None else a + b for a, b in zip(totals, found)]

    backs = []
    for c in range(half // QB):
        start = pl.multiple_of(theirs + c * QB, QB)
        input_grad(start)
        copy = give_back(2 + c, gx.at[pl.ds(start, QB)], gx_out.at[me, pl.ds(c * QB, QB)])
        copy.start()
        backs.append(copy)
        if c == 0:
            s_q[2].take(0)
            s_f3.take(3)
        else:
            s_q[1].take(1)
            s_out.take(3)
            s_q[0].take(2)
    for c in range(half // QB):
        input_grad(mine + c * QB)
        if c == 0:
            s_f3.take(4)
    keep_gx = pltpu.make_async_copy(gx.at[pl.ds(mine, half)], gx_out.at[me], out_sem.at[2])
    keep_gx.start()
    wide = [dbfc_ref[:, n * width : (n + 1) * width] for n in range(4)]
    sums[0] = jnp.concatenate(
        [small_in[...]] + totals + wide + [jnp.zeros((4, width), F32)], axis=0
    )
    small_copy(0).start()

    def small_take(stage):
        small_copy(stage).wait()
        sums[stage + 1] = sums[stage] + s_got[stage]
        if stage < 4:
            small_copy(stage + 1).start()

    s_q[2].take(1)
    s_out.take(4)
    s_q[0].take(3)
    s_q[1].take(2)
    small_take(0)
    s_ph.take(1)
    s_q[2].take(2)
    small_take(1)
    s_q[1].take(3)
    s_q[2].take(3)
    small_take(2)

    tile = g_f3.shape[-1]
    side = tile // 2
    own, came = s_f0.last()
    wfc_out[:, :tile] = own + came
    for sum_, tiles in ((s_f12, (1, 2)), (s_f3, (3,))):
        for part, who in zip(sum_.last(), (me, 1 - me)):
            for n, t in enumerate(tiles):
                at = pl.ds(pl.multiple_of(t * tile + who * side, side), side)
                wfc_out[:, at] = part[:, n * side : (n + 1) * side]
    small_take(3)
    side = width // 2
    for part, who in zip(s_out.last(), (me, 1 - me)):
        wout_out[:, pl.ds(pl.multiple_of(who * side, side), side)] = part
    own, came = s_ph.last()
    wproj_out[...] = own + came
    for n in range(3):
        own, came = s_q[n].last()
        part = own + came
        at = 0
        for start, size in parts[n][1]:
            wqkv_out[:, start : start + size] = part[:, at : at + size]
            at += size
        if n == 1:
            small_take(4)
            small_out[...] = sums[5]
    back_gf.wait()
    for copy in backs:
        copy.wait()
    keep_gf.wait()
    keep_gx.wait()


def tail(
    q, k, v, do, bias, x, act1t, gmid, wqkv, dwout, f0, f12, f3, p01, p2, p3, lse, dots, g1, dbfc, small
):
    tokens, width = q.shape
    half = tokens // 2
    val = wqkv.shape[1] - 2 * width
    owner = width // 16
    owner_ff = dbfc.shape[1] // 16
    ff = dbfc.shape[1]
    tile = f3.shape[-1]
    shape = jax.ShapeDtypeStruct
    hbm = pl.BlockSpec(memory_space=pl.ANY)
    vmem = pl.BlockSpec(memory_space=pltpu.VMEM)

    def vm(*s):
        return pltpu.VMEM(s, BF)

    def chain(rows, cols):
        return [
            vm(2, 2, 2, rows, cols),
            vm(2, 2, rows, cols),
            vm(2, rows, cols),
            vm(rows, cols),
            vm(rows, cols),
        ]

    def cut_chain(rows, cols):
        side = chain(rows, cols // 2)
        return [vm(2, 2, 2, rows, cols)] + side[:1] + side[1:4] + side[3:4]

    flat = vm(tokens, width)
    sizes = [sum(size for _, size in columns) for _, columns in pieces(width, val)]
    return pl.pallas_call(
        tail_kernel,
        in_specs=[hbm] * 16 + [vmem] * 5,
        out_specs=[hbm] * 2 + [vmem] * 5,
        out_shape=[
            shape((2, half, width), BF),
            shape((2, half, val), BF),
            shape((owner, wqkv.shape[1]), F32),
            shape((owner, width), F32),
            shape((owner, ff), F32),
            shape((owner_ff, width), F32),
            shape((16, width), F32),
        ],
        scratch_shapes=[
            flat,
            flat,
            flat,
            flat,
            pltpu.VMEM((tokens, tokens), F32),
            flat,
            pltpu.VMEM((tokens, width), F32),
            vm(*wqkv.shape),
            vm(tokens, 2 * width),
            vm(tokens, val),
            vm(tokens, val),
            pltpu.VMEM((tokens, LANES), F32),
            vm(width, tokens),
            flat,
            vm(*dwout.shape),
            vm(*f0.shape),
            vm(*f12.shape),
            vm(*f3.shape),
            vm(2, 2, owner_ff, width),
            vm(*p2.shape),
            vm(*p3.shape),
            [vm(2, 2, 2, 2, owner, size) for size in sizes],
            cut_chain(owner, width),
            chain(owner, tile)[2:],
            chain(owner, tile)[1:],
            cut_chain(owner, tile),
            [vm(owner_ff, width)] * 4,
            [vm(owner_ff, width)],
            [vm(2, owner_ff, width), vm(owner_ff, width)],
            [chain(owner, size) for size in sizes],
            pltpu.VMEM((6, 16, width), F32),
            pltpu.VMEM((5, 16, width), F32),
            pltpu.SemaphoreType.DMA((16,)),
            pltpu.SemaphoreType.DMA((3,)),
            pltpu.SemaphoreType.DMA((4,)),
            pltpu.SemaphoreType.DMA((4,)),
            pltpu.SemaphoreType.DMA((13, 6)),
            pltpu.SemaphoreType.DMA((13, 6)),
        ],
        compiler_params=pltpu.CompilerParams(
            collective_id=2, has_side_effects=True, vmem_limit_bytes=62 * MIB
        ),
        name="tail",
    )(q, k, v, do, bias, x, act1t, gmid, wqkv, dwout, f0, f12, f3, p01, p2, p3, lse, dots, g1, dbfc, small)


def finish_kernel(*refs):
    wide_in, sums = refs[:7], refs[7]
    wide_out, small_out, held, sem = refs[8:15], refs[15:24], refs[24], refs[25]
    loads = [pltpu.make_async_copy(src, dst, sem.at[0, n]) for n, (src, dst) in enumerate(zip(wide_in, held))]
    stores = [pltpu.make_async_copy(src, dst, sem.at[1, n]) for n, (src, dst) in enumerate(zip(held, wide_out))]
    for load in loads:
        load.start()
    b = lax.axis_index("batch")
    rows = sums[0:8, :]
    width = rows.shape[1]
    long = jnp.concatenate([sums[8 + n : 9 + n, :] for n in range(4)], axis=1)
    long = jnp.broadcast_to(long, (8, 4 * width))
    for at, ref in zip((4, 5, 6, 7, 3, 1, 2, None, 0), small_out):
        size = ref.shape[0]
        source = long if at is None else rows
        line = 0 if at is None else at
        length = source.shape[1]
        turned = pltpu.roll(source, lax.rem(length - b * size, length), 1)
        ref[...] = turned[line, :size]
    for load, store in zip(loads, stores):
        load.wait()
        store.start()
    for store in stores:
        store.wait()


def finish(wide, sums, sizes):
    hbm = pl.BlockSpec(memory_space=pl.ANY)
    vmem = pl.BlockSpec(memory_space=pltpu.VMEM)
    shape = jax.ShapeDtypeStruct
    return pl.pallas_call(
        finish_kernel,
        in_specs=[hbm] * 7 + [vmem],
        out_specs=[hbm] * 7 + [vmem] * 9,
        out_shape=[shape(a.shape, a.dtype) for a in wide] + [shape((n,), F32) for n in sizes],
        scratch_shapes=[
            [pltpu.VMEM(a.shape, a.dtype) for a in wide],
            pltpu.SemaphoreType.DMA((2, 7)),
        ],
        compiler_params=pltpu.CompilerParams(vmem_limit_bytes=60 * MIB),
        name="finish",
    )(*wide, sums)


def paired(
    inputs,
    first_values,
    segments,
    ln1_gain,
    first_norm_bias,
    w_qkv,
    b_query,
    b_value,
    w_out,
    b_out,
    ln2_gain,
    second_norm_bias,
    w_fc,
    b_fc,
    w_proj,
    b_proj,
    cotangent,
):
    half, width = inputs.shape[1], inputs.shape[2]
    val = first_values.shape[2]
    x, q, k, v, att, act2, mid, lse, bias, act1t, cot_far = front(
        inputs,
        first_values,
        segments,
        cotangent,
        ln1_gain,
        first_norm_bias,
        w_qkv,
        b_query,
        b_value,
        w_out,
        b_out,
        ln2_gain,
        second_norm_bias,
    )
    layer_out, gmid, gatt, dwout, f0, f12, f3, p01, p2, p3, dots, dbfc, small = feed(
        act2, cotangent, cot_far, mid, att, ln2_gain, b_proj, w_out, w_fc, b_fc, w_proj
    )
    owner = width // 16
    *wide, sums = tail(
        q,
        k,
        v,
        gatt,
        bias,
        x,
        act1t,
        gmid,
        w_qkv,
        dwout,
        f0,
        f12,
        f3,
        p01,
        p2,
        p3,
        lse,
        dots,
        ln1_gain,
        dbfc,
        small,
    )
    sizes = [owner, owner, owner, val // 16, owner, owner, owner, w_fc.shape[1] // 16, owner]
    out = finish([layer_out] + wide, sums, sizes)
    layer_out, grad_inputs, grad_first, gwqkv, gwout, gwfc, gwproj = out[:7]
    g1, b1, bq, bv, bo, g2, b2, bf, bp = out[7:]
    return (
        layer_out,
        grad_inputs,
        grad_first,
        g1,
        b1,
        gwqkv,
        bq,
        bv,
        gwout,
        bo,
        g2,
        b2,
        gwfc,
        bf,
        gwproj,
        bp,
    )


MICRO = 2


def as_sent(shard):
    return jax.tree.map(lambda a: a.astype(jnp.bfloat16) if a.dtype == jnp.float32 else a, shard)


def apply_norm(values_in, norm_gain, shift_bias):
    mean_val = jnp.mean(values_in, axis=-1, keepdims=True)
    centred_rows = values_in - mean_val
    inverse_deviation = lax.rsqrt(
        jnp.mean(centred_rows * centred_rows, axis=-1, keepdims=True) + EPS
    )
    standardized = centred_rows * inverse_deviation
    return (standardized * norm_gain + shift_bias, standardized, inverse_deviation)


def apply_norm_backward(upstream_gradient, standardized, inverse_deviation, norm_gain):
    scaled_rows = upstream_gradient * norm_gain
    first_average = jnp.mean(scaled_rows, axis=-1, keepdims=True)
    second_average = jnp.mean(scaled_rows * standardized, axis=-1, keepdims=True)
    incoming_gradient = inverse_deviation * (
        scaled_rows - first_average - standardized * second_average
    )
    return (
        incoming_gradient,
        jnp.sum(upstream_gradient * standardized, axis=(0, 1)),
        jnp.sum(upstream_gradient, axis=(0, 1)),
    )


def gelu_tanh(values_in):
    cubic = values_in + 0.044715 * values_in * values_in * values_in
    return 0.5 * values_in * (1.0 + jnp.tanh(0.7978845608028654 * cubic))


def heads_of(values_in):
    return values_in.reshape(values_in.shape[0], values_in.shape[1], HEADS, HEAD_DIM)


def visible(seg_query, seg_key, query_pos, key_pos):
    same = seg_query[:, :, None] == seg_key[:, None, :]
    causal = key_pos[None, :] <= query_pos[:, None]
    live = seg_query[:, :, None] >= 0
    diagonal = key_pos[None, :] == query_pos[:, None]
    return (same & causal[None] & live | diagonal[None])[:, :, None, :]


def score_block(query4, key4, mask):
    raw = jnp.einsum("rqhd,rkhd->rqhk", query4, key4, preferred_element_type=jnp.float32)
    return jnp.where(mask, raw * HEAD_DIM ** (-0.5), NEG)


def grad_block(query4, key4, value4, dout4, log_total, out_dot, mask):
    probs = jnp.where(mask, jnp.exp(score_block(query4, key4, mask) - log_total[..., None]), 0.0)
    probs_low = probs.astype(jnp.bfloat16)
    grad_probs = jnp.einsum("rqhd,rkhd->rqhk", dout4, value4, preferred_element_type=jnp.float32)
    grad_scores = (probs * (grad_probs - out_dot[..., None]) * HEAD_DIM ** (-0.5)).astype(
        jnp.bfloat16
    )
    return (probs_low, grad_scores)


def spread(
    inputs,
    first_values,
    segments,
    ln1_gain,
    first_norm_bias,
    w_qkv,
    b_query,
    b_value,
    w_out,
    b_out,
    ln2_gain,
    second_norm_bias,
    w_fc,
    b_fc,
    w_proj,
    b_proj,
    cotangent,
):
    all_seg = lax.all_gather(segments, "blk", axis=1, tiled=True)
    block_len = inputs.shape[1]
    model_width = inputs.shape[2]
    val_width = first_values.shape[2]
    rows_mb = inputs.shape[0] // MICRO
    own_pos = lax.axis_index("blk") * block_len + jnp.arange(block_len)
    first_gain = ln1_gain.astype(jnp.float32)
    second_gain = ln2_gain.astype(jnp.float32)
    outputs = []
    input_grads = []
    first_grads = []
    totals = None
    for micro_step in range(MICRO):
        first_row = micro_step * rows_mb
        last_row = first_row + rows_mb
        residual_stream = inputs[first_row:last_row].astype(jnp.float32)
        first_part = first_values[first_row:last_row]
        seg_local = segments[first_row:last_row]
        seg_row = all_seg[first_row:last_row]
        cot_part = cotangent[first_row:last_row]
        first_normed_rows, first_standardized, first_inverse_deviation = apply_norm(
            residual_stream, first_gain, first_norm_bias.astype(jnp.float32)
        )
        act1 = first_normed_rows.astype(jnp.bfloat16)
        projected = jnp.einsum("rbd,de->rbe", act1, w_qkv, preferred_element_type=jnp.float32)
        queries = (projected[..., :model_width] + b_query.astype(jnp.float32)).astype(jnp.bfloat16)
        keys_low = projected[..., model_width : 2 * model_width].astype(jnp.bfloat16)
        fresh = (projected[..., 2 * model_width :] + b_value.astype(jnp.float32)).astype(
            jnp.bfloat16
        )
        values_low = jnp.concatenate([fresh, first_part], axis=-1)
        query4 = heads_of(queries)
        key_part = lax.all_gather(keys_low, "blk", axis=1, tiled=True)
        value_part = lax.all_gather(values_low, "blk", axis=1, tiled=True)
        span = key_part.shape[1]
        key_pos = jnp.arange(span)
        mask = visible(seg_local, seg_row, own_pos, key_pos)
        scores = score_block(query4, heads_of(key_part), mask)
        old_max = jnp.full((rows_mb, block_len, HEADS), NEG, jnp.float32)
        new_max = jnp.maximum(old_max, jnp.max(scores, axis=-1))
        weights = jnp.where(mask, jnp.exp(scores - new_max[..., None]), 0.0)
        new_sum = jnp.sum(weights, axis=-1)
        new_acc = jnp.einsum(
            "rqhk,rkhd->rqhd",
            weights.astype(jnp.bfloat16),
            heads_of(value_part),
            preferred_element_type=jnp.float32,
        )
        attention4 = new_acc / new_sum[..., None]
        log_total = new_max + jnp.log(new_sum)
        attention_low = attention4.reshape(rows_mb, block_len, model_width).astype(jnp.bfloat16)
        branch = jnp.einsum("rbd,de->rbe", attention_low, w_out, preferred_element_type=jnp.float32)
        middle_state = residual_stream + branch + b_out.astype(jnp.float32)
        second_normed_rows, second_standardized, second_inverse_deviation = apply_norm(
            middle_state, second_gain, second_norm_bias.astype(jnp.float32)
        )
        act2 = second_normed_rows.astype(jnp.bfloat16)
        pre_gelu = jnp.einsum(
            "rbd,df->rbf", act2, w_fc, preferred_element_type=jnp.float32
        ) + b_fc.astype(jnp.float32)
        hidden = gelu_tanh(pre_gelu).astype(jnp.bfloat16)
        result = middle_state + jnp.einsum(
            "rbf,fd->rbd", hidden, w_proj, preferred_element_type=jnp.float32
        )
        result = result + b_proj.astype(jnp.float32)
        outputs.append(result.astype(jnp.bfloat16))
        upstream_gradient = cot_part.astype(jnp.float32)
        grad_wproj = jnp.einsum("rbf,rbd->fd", hidden, cot_part, preferred_element_type=jnp.float32)
        grad_bproj = jnp.sum(upstream_gradient, axis=(0, 1))
        grad_hidden = jnp.einsum(
            "rbd,fd->rbf", cot_part, w_proj, preferred_element_type=jnp.float32
        )
        gelu_value, gelu_pull = jax.vjp(gelu_tanh, pre_gelu)
        grad_pre = gelu_pull(grad_hidden)[0].astype(jnp.bfloat16)
        grad_wfc = jnp.einsum("rbd,rbf->df", act2, grad_pre, preferred_element_type=jnp.float32)
        grad_bfc = jnp.sum(grad_pre.astype(jnp.float32), axis=(0, 1))
        second_activation_gradient = jnp.einsum(
            "rbf,df->rbd", grad_pre, w_fc, preferred_element_type=jnp.float32
        )
        second_norm_gradient, second_gain_gradient, second_bias_gradient = apply_norm_backward(
            second_activation_gradient, second_standardized, second_inverse_deviation, second_gain
        )
        grad_middle = upstream_gradient + second_norm_gradient
        grad_branch = grad_middle.astype(jnp.bfloat16)
        grad_wout = jnp.einsum(
            "rbd,rbe->de", attention_low, grad_branch, preferred_element_type=jnp.float32
        )
        grad_bout = jnp.sum(grad_branch.astype(jnp.float32), axis=(0, 1))
        grad_attention = jnp.einsum(
            "rbe,de->rbd", grad_branch, w_out, preferred_element_type=jnp.float32
        ).astype(jnp.bfloat16)
        dout4 = heads_of(grad_attention)
        out_dot = jnp.sum(dout4.astype(jnp.float32) * attention4, axis=-1)
        back_key_part = lax.all_gather(keys_low, "blk", axis=1, tiled=True)
        back_value_part = lax.all_gather(values_low, "blk", axis=1, tiled=True)
        back_span = back_key_part.shape[1]
        back_key_pos = jnp.arange(back_span)
        back_mask = visible(seg_local, seg_row, own_pos, back_key_pos)
        part_key4 = heads_of(back_key_part)
        probs_low, grad_scores = grad_block(
            query4, part_key4, heads_of(back_value_part), dout4, log_total, out_dot, back_mask
        )
        query_acc = jnp.einsum(
            "rqhk,rkhd->rqhd", grad_scores, part_key4, preferred_element_type=jnp.float32
        )
        key_piece = jnp.einsum(
            "rqhk,rqhd->rkhd", grad_scores, query4, preferred_element_type=jnp.float32
        ).reshape(rows_mb, back_span, model_width)
        value_piece = jnp.einsum(
            "rqhk,rqhd->rkhd", probs_low, dout4, preferred_element_type=jnp.float32
        ).reshape(rows_mb, back_span, model_width)
        query_acc, key_acc, value_acc = (query_acc, key_piece, value_piece)
        grad_keys, grad_values = (
            lax.psum_scatter(
                key_acc.astype(jnp.bfloat16), "blk", scatter_dimension=1, tiled=True
            ).astype(jnp.float32),
            lax.psum_scatter(
                value_acc.astype(jnp.bfloat16), "blk", scatter_dimension=1, tiled=True
            ).astype(jnp.float32),
        )
        grad_query = query_acc.reshape(rows_mb, block_len, model_width)
        grad_qkv = jnp.concatenate(
            [
                grad_query.astype(jnp.bfloat16),
                grad_keys.astype(jnp.bfloat16),
                grad_values[..., :val_width].astype(jnp.bfloat16),
            ],
            axis=-1,
        )
        first_grads.append(grad_values[..., val_width:].astype(jnp.bfloat16))
        grad_wqkv = jnp.einsum("rbd,rbe->de", act1, grad_qkv, preferred_element_type=jnp.float32)
        grad_bquery = jnp.sum(grad_qkv[..., :model_width].astype(jnp.float32), axis=(0, 1))
        grad_bvalue = jnp.sum(grad_qkv[..., 2 * model_width :].astype(jnp.float32), axis=(0, 1))
        first_activation_gradient = jnp.einsum(
            "rbe,de->rbd", grad_qkv, w_qkv, preferred_element_type=jnp.float32
        )
        first_norm_gradient, first_gain_gradient, first_bias_gradient = apply_norm_backward(
            first_activation_gradient, first_standardized, first_inverse_deviation, first_gain
        )
        input_grads.append((grad_middle + first_norm_gradient).astype(jnp.bfloat16))
        gradient_set = (
            first_gain_gradient,
            first_bias_gradient,
            grad_wqkv,
            grad_bquery,
            grad_bvalue,
            grad_wout,
            grad_bout,
            second_gain_gradient,
            second_bias_gradient,
            grad_wfc,
            grad_bfc,
            grad_wproj,
            grad_bproj,
        )
        if totals is None:
            totals = gradient_set
        else:
            totals = tuple((older + newer for older, newer in zip(totals, gradient_set)))
    totals = jax.tree.map(
        lambda part: part.astype(jnp.float32),
        lax.psum_scatter(as_sent(totals), "batch", scatter_dimension=0, tiled=True),
    )
    totals = jax.tree.map(lambda part: part.astype(jnp.float32), lax.psum(as_sent(totals), "blk"))
    return (
        jnp.concatenate(outputs, axis=0),
        jnp.concatenate(input_grads, axis=0),
        jnp.concatenate(first_grads, axis=0),
    ) + tuple(totals)


def layer(inputs, *rest):
    whole_rows = lax.axis_size("blk") == inputs.shape[0] == 2 and inputs.shape[1] == 2 * QB
    whole_rows = whole_rows and lax.axis_size("batch") == 16
    return (paired if whole_rows else spread)(inputs, *rest)


def solution(mesh):
    rows = P("batch", "blk", None)
    flat = P("batch")
    wide = P("batch", None)
    return jax.shard_map(
        layer,
        mesh=mesh,
        in_specs=(rows, rows, P("batch", "blk")) + (P(),) * 13 + (rows,),
        out_specs=(rows, rows, rows)
        + (flat, flat, wide, flat, flat, wide, flat, flat, flat, wide, flat, wide, flat),
        check_vma=False,
    )
```

```python
import functools

import jax
import jax.numpy as jnp
from jax import lax
from jax.experimental import pallas as pl
from jax.experimental.pallas import tpu as pltpu
from jax.sharding import PartitionSpec as P

HEADS = 12
HEAD_DIM = 64
PAIRS = HEADS // 2
LANES = 2 * HEAD_DIM
EPS = 1e-05
NEG = -1e30
QB = 256
F32 = jnp.float32
BF = jnp.bfloat16
MIB = 2**20
MESH = pl.DeviceIdType.MESH


def nn(a, b):
    return lax.dot_general(a, b, (((1,), (0,)), ((), ())), preferred_element_type=F32)


def nt(a, b):
    return lax.dot_general(a, b, (((1,), (1,)), ((), ())), preferred_element_type=F32)


def tn(a, b):
    return lax.dot_general(a, b, (((0,), (0,)), ((), ())), preferred_element_type=F32)


def norm_parts(rows):
    mean = jnp.mean(rows, axis=-1, keepdims=True)
    centred = rows - mean
    inverse = lax.rsqrt(jnp.mean(centred * centred, axis=-1, keepdims=True) + EPS)
    return centred * inverse, inverse


def norm_pull(grad, xhat, inverse, gain):
    scaled = grad * gain
    first = jnp.mean(scaled, axis=-1, keepdims=True)
    second = jnp.mean(scaled * xhat, axis=-1, keepdims=True)
    return inverse * (scaled - first - xhat * second)


def row(ref):
    return ref[...].astype(F32).reshape(1, -1)


def column_sum(rows):
    return jnp.sum(rows, axis=0, keepdims=True)


def spot():
    b = lax.axis_index("batch")
    core = lax.rem(b, 2)
    x = lax.rem(lax.div(b, 2), 2)
    near = lax.rem(lax.div(b, 4), 2)
    far = lax.div(b, 8)
    return b, core, x, near, far


def partners():
    b, core, x, near, far = spot()
    return [
        {"batch": b + 1 - 2 * core},
        {"batch": b + 2 - 4 * x},
        {"batch": b + 4 - 8 * near},
        {"batch": b + 8 - 16 * far},
        {"blk": 1 - lax.axis_index("blk")},
    ]


FLIPS = [(f, n, x) for f in range(2) for n in range(2) for x in range(2) if f + n + x]


def flipped(flip):
    _, core, x, near, far = spot()
    at = [own + turn * (1 - 2 * own) for own, turn in zip((far, near, x), flip)]
    return tuple(at) + (core,), {"batch": ((at[0] * 2 + at[1]) * 2 + at[2]) * 2 + core}


def greet(friends):
    barrier = pltpu.get_barrier_semaphore()
    for friend in friends:
        pl.semaphore_signal(barrier, inc=1, device_id=friend, device_id_type=MESH)
    pl.semaphore_wait(barrier, len(friends))


def push(src, dst, send_sem, recv_sem, friend):
    copy = pltpu.make_async_remote_copy(
        src_ref=src,
        dst_ref=dst,
        send_sem=send_sem,
        recv_sem=recv_sem,
        device_id=friend,
        device_id_type=MESH,
    )
    return copy


def add_into(dst, src):
    dst[...] = dst[...] + src[...]


PLACES = ("core", "x", "near", "far")


class Sum:
    def __init__(self, held, got, dims, order, send_sem, recv_sem, cut_columns=True):
        self.held, self.got, self.dims, self.order = held, got, dims, order
        self.send_sem, self.recv_sem, self.cut_columns = send_sem, recv_sem, cut_columns

    def cut(self, stage, keep):
        name = self.order[stage]
        done = self.order[:stage]
        _, core, x, near, far = spot()
        own = {"core": core, "x": x, "near": near, "far": far}
        at = []
        for dim in self.dims:
            if dim == name:
                at.append(own[dim] if keep else 1 - own[dim])
            else:
                at.append(own[dim] if dim in done else slice(None))
        if self.cut_columns and (name == "half" or "half" in done):
            me = lax.axis_index("blk")
            size = self.held.shape[-1] // 2
            side = 1 - me if name == "half" and not keep else me
            at += [slice(None), pl.ds(pl.multiple_of(side * size, size), size)]
        return tuple(at)

    def copy(self, stage):
        name = self.order[stage]
        return push(
            self.held.at[self.cut(stage, False)],
            self.got[stage],
            self.send_sem.at[stage],
            self.recv_sem.at[stage],
            partners()[PLACES.index(name) if name in PLACES else 4],
        )

    def start(self, stage):
        self.copy(stage).start()

    def take(self, stage):
        self.copy(stage).wait()
        mine = self.held.at[self.cut(stage, True)]
        came = self.got[stage]
        lead = came.shape[:-2]
        count = 1
        for size in lead:
            count *= size
        for n in range(count):
            at = []
            for size in reversed(lead):
                at.insert(0, n % size)
                n //= size
            at = tuple(at)
            add_into(mine.at[at] if at else mine, came.at[at] if at else came)
        if stage + 1 < len(self.order):
            self.start(stage + 1)

    def last(self):
        stage = len(self.order) - 1
        self.copy(stage).wait()
        return self.held[self.cut(stage, True)].astype(F32), self.got[stage][...].astype(F32)


class Vectors:
    def __init__(self, held, got, place, sems, far_sems):
        self.held, self.got, self.place = held, got, place
        self.sems, self.far_sems = sems, far_sems

    def copies(self, stage):
        src = self.held.at[stage]
        if stage == 1:
            return [
                push(
                    src,
                    self.got[1].at[n],
                    self.far_sems[0].at[self.place, n],
                    self.far_sems[1].at[self.place, n],
                    flipped(flip)[1],
                )
                for n, flip in enumerate(FLIPS)
            ]
        friend = partners()[stage * 2]
        return [push(src, self.got[stage], self.sems[0].at[stage], self.sems[1].at[stage], friend)]

    def start(self, stage):
        for copy in self.copies(stage):
            copy.start()

    def take(self, stage):
        for copy in self.copies(stage):
            copy.wait()
        if stage == 1:
            total = self.held[1]
            for n in range(len(FLIPS)):
                total = total + self.got[1][n]
        else:
            total = self.held[stage] + self.got[stage][...]
        self.held[stage + 1] = total
        if stage < 2:
            self.start(stage + 1)


def front_kernel(
    x_in,
    fv_in,
    seg_in,
    cot_in,
    g1_ref,
    b1_ref,
    wqkv_in,
    bq_ref,
    bv_ref,
    wout_in,
    bout_ref,
    g2_ref,
    b2_ref,
    x_out,
    q_out,
    k_out,
    v_out,
    att_out,
    act2_out,
    mid_out,
    lse_ref,
    bias_out,
    act1t_out,
    cot_out,
    xs,
    qs,
    ks,
    vs,
    atts,
    act2s,
    mids,
    bias,
    wqkv,
    wout,
    segrow,
    segsend,
    segcol,
    act1ts,
    in_sem,
    out_sem,
    send_sem,
    recv_sem,
):
    half = x_in.shape[1]
    tokens = 2 * half
    width = x_in.shape[2]
    val = fv_in.shape[2]
    steps = tokens // QB
    me = lax.axis_index("blk")
    other = 1 - me
    mine = pl.multiple_of(me * half, half)
    theirs = pl.multiple_of(other * half, half)

    def local_in(i, src, dst):
        copy = pltpu.make_async_copy(src, dst, in_sem.at[i])
        copy.start()
        return copy

    own_x = local_in(0, x_in.at[me], xs.at[pl.ds(mine, half)])
    own_fv = local_in(1, fv_in.at[me], vs.at[pl.ds(mine, half), pl.ds(val, val)])
    own_w = local_in(2, wqkv_in, wqkv)
    own_wo = local_in(3, wout_in, wout)
    first, second = seg_in[0:1, :], seg_in[1:2, :]
    segsend[...] = jnp.broadcast_to(jnp.where(me == 0, second, first), segsend.shape)

    barrier = pltpu.get_barrier_semaphore()
    pl.semaphore_signal(barrier, inc=1, device_id={"blk": other}, device_id_type=MESH)
    pl.semaphore_wait(barrier, 1)

    def remote(i, src, dst):
        copy = pltpu.make_async_remote_copy(
            src_ref=src,
            dst_ref=dst,
            send_sem=send_sem.at[i],
            recv_sem=recv_sem.at[i],
            device_id={"blk": other},
            device_id_type=MESH,
        )
        copy.start()
        return copy

    part = half // 2
    far_x = [
        remote(
            c,
            x_in.at[other, pl.ds(c * part, part)],
            xs.at[pl.ds(pl.multiple_of(mine + c * part, part), part)],
        )
        for c in range(2)
    ]
    far_seg = remote(2, segsend, segrow.at[:, pl.ds(mine, half)])
    far_fv = remote(3, fv_in.at[other], vs.at[pl.ds(mine, half), pl.ds(val, val)])
    far_cot = remote(4, cot_in.at[other, pl.ds(0, part)], cot_out)

    own_row = jnp.broadcast_to(jnp.where(me == 0, first, second), (8, half))
    segrow[:, pl.ds(mine, half)] = own_row

    def project(start):
        rows = pl.ds(pl.multiple_of(start, QB), QB)
        xhat, _ = norm_parts(xs[rows, :].astype(F32))
        act1 = (xhat * row(g1_ref) + row(b1_ref)).astype(BF)
        act1ts[:, rows] = act1.T
        out = nn(act1, wqkv[...])
        query = (out[:, :width] + row(bq_ref)).astype(BF)
        qs[rows, :] = query * jnp.asarray(HEAD_DIM**-0.5, BF)
        ks[rows, :] = out[:, width : 2 * width].astype(BF)
        vs[rows, pl.ds(0, val)] = (out[:, 2 * width :] + row(bv_ref)).astype(BF)

    low = lax.broadcasted_iota(jnp.int32, (1, LANES), 1) < HEAD_DIM
    upper = lax.broadcasted_iota(jnp.int32, (LANES, 1), 0) < HEAD_DIM
    count = half // QB

    def at(start):
        return pl.ds(pl.multiple_of(start, QB), QB)

    def turn_segments(start):
        for c in range(half // LANES):
            place = pl.ds(pl.multiple_of(start + c * LANES, LANES), LANES)
            line = segrow[0:1, place].astype(F32)
            segcol[place, :] = jnp.broadcast_to(line, (LANES, LANES)).T

    def mask_block(key_start, query_start, diagonal):
        key = segcol[at(key_start), :]
        key = jnp.concatenate([key] * (QB // LANES), axis=1)
        query = segrow[0:1, at(query_start)].astype(F32)
        seen = (key == query) & (query >= 0.0)
        if diagonal:
            down = lax.broadcasted_iota(jnp.int32, (QB, QB), 0)
            across = lax.broadcasted_iota(jnp.int32, (QB, QB), 1)
            seen = (seen & (down <= across)) | (down == across)
        bias[at(key_start), at(query_start)] = jnp.where(seen, 0.0, NEG)

    def mask_half(start):
        turn_segments(start)
        for i in range(count):
            for j in range(i + 1):
                mask_block(start + j * QB, start + i * QB, i == j)

    def attend(p, items):
        cols = pl.ds(pl.multiple_of(p * LANES, LANES), LANES)
        done = {}

        def score(first, span, query, h, more):
            keys = pl.ds(pl.multiple_of(first, QB), span)
            q = qs[at(query), cols]
            q = jnp.where(low if h == 0 else ~low, q, jnp.zeros_like(q))
            return nt(ks[keys, cols], q) + bias[keys, at(query)]

        def finish(first, span, query, h, more, s):
            keys = pl.ds(pl.multiple_of(first, QB), span)
            rows = at(query)
            top = jnp.max(s, axis=0, keepdims=True)
            if more:
                before = lse_ref[p, h : h + 1, rows]
                top = jnp.maximum(top, before)
            e = jnp.exp(s - top)
            total = jnp.sum(e, axis=0, keepdims=True)
            if more:
                total = total + jnp.exp(before - top)
            log_total = top + jnp.log(total)
            done[h] = tn((e * (1.0 / total)).astype(BF), vs[keys, cols])
            if more:
                done[h + 2] = jnp.exp(before - log_total)
            lse_ref[p, h : h + 1, rows] = log_total
            if h == 1:
                out = jnp.where(low, done[0], done[1])
                if more:
                    share = jnp.where(upper, done[2], done[3]).T
                    out = out + mids[rows, cols] * share
                else:
                    mids[rows, cols] = out
                atts[rows, cols] = out.astype(BF)

        waiting = []
        for item in items:
            waiting.append(item + (score(*item),))
            if len(waiting) > 2:
                finish(*waiting.pop(0))
        for item in waiting:
            finish(*item)

    def half_items(start):
        return [
            (start, (i + 1) * QB, start + i * QB, h, False) for i in range(count) for h in range(2)
        ]

    cross_items = [
        (0, half, half + i * QB, h, True) for i in range(count) for h in range(2)
    ]

    own_x.wait()
    own_w.wait()
    for c in range(count):
        project(mine + c * QB)
    mask_half(mine)
    own_fv.wait()

    @pl.loop(0, PAIRS)
    def _(p):
        attend(p, half_items(mine))

    for c in range(2):
        far_x[c].wait()
        project(theirs + c * part)

    outs = []

    def local_out(src, dst):
        copy = pltpu.make_async_copy(src, dst, out_sem.at[len(outs)])
        copy.start()
        outs.append(copy)

    local_out(act1ts, act1t_out)
    local_out(xs, x_out)
    local_out(qs, q_out)
    local_out(ks, k_out)

    far_seg.wait()
    mask_half(theirs)
    for i in range(count):
        for j in range(count):
            mask_block(j * QB, half + i * QB, False)
    for j in range(steps):
        cut = (pl.ds(j * QB, QB), pl.ds(j * QB, tokens - j * QB))
        local_out(bias.at[cut], bias_out.at[cut])

    @pl.loop(0, PAIRS)
    def _(p):
        @pl.when(p == PAIRS // 2)
        def _():
            far_fv.wait()

        attend(p, half_items(theirs) + cross_items)

    local_out(atts, att_out)
    local_out(vs, v_out)
    own_wo.wait()
    for c in range(steps):
        rows = slice(c * QB, (c + 1) * QB)
        middle = xs[rows, :].astype(F32) + nn(atts[rows, :], wout[...]) + row(bout_ref)
        mids[rows, :] = middle
        xhat, _ = norm_parts(middle)
        act2s[rows, :] = (xhat * row(g2_ref) + row(b2_ref)).astype(BF)
    local_out(mids, mid_out)
    local_out(act2s, act2_out)
    for copy in outs:
        copy.wait()
    far_cot.wait()


def front(x, fv, seg, cot, g1, b1, wqkv, bq, bv, wout, bout, g2, b2):
    half, width, val = x.shape[1], x.shape[2], fv.shape[2]
    tokens = 2 * half
    hbm = pl.BlockSpec(memory_space=pl.ANY)
    vmem = pl.BlockSpec(memory_space=pltpu.VMEM)
    flat = jax.ShapeDtypeStruct((tokens, width), BF)
    shape = jax.ShapeDtypeStruct
    return pl.pallas_call(
        front_kernel,
        in_specs=[hbm, hbm, vmem, hbm, vmem, vmem, hbm, vmem, vmem, hbm, vmem, vmem, vmem],
        out_specs=[hbm] * 7 + [vmem] + [hbm] * 3,
        out_shape=[
            flat,
            flat,
            flat,
            flat,
            flat,
            flat,
            shape((tokens, width), F32),
            shape((PAIRS, 2, tokens), F32),
            shape((tokens, tokens), F32),
            shape((width, tokens), BF),
            shape((half // 2, width), BF),
        ],
        scratch_shapes=[
            pltpu.VMEM((tokens, width), BF),
            pltpu.VMEM((tokens, width), BF),
            pltpu.VMEM((tokens, width), BF),
            pltpu.VMEM((tokens, width), BF),
            pltpu.VMEM((tokens, width), BF),
            pltpu.VMEM((tokens, width), BF),
            pltpu.VMEM((tokens, width), F32),
            pltpu.VMEM((tokens, tokens), F32),
            pltpu.VMEM(wqkv.shape, BF),
            pltpu.VMEM(wout.shape, BF),
            pltpu.VMEM((8, tokens), jnp.int32),
            pltpu.VMEM((8, half), jnp.int32),
            pltpu.VMEM((tokens, LANES), F32),
            pltpu.VMEM((width, tokens), BF),
            pltpu.SemaphoreType.DMA((5,)),
            pltpu.SemaphoreType.DMA((8 + tokens // QB,)),
            pltpu.SemaphoreType.DMA((5,)),
            pltpu.SemaphoreType.DMA((5,)),
        ],
        compiler_params=pltpu.CompilerParams(
            collective_id=0, has_side_effects=True, vmem_limit_bytes=56 * MIB
        ),
        name="front",
    )(x, fv, seg, cot, g1, b1, wqkv, bq, bv, wout, bout, g2, b2)


def feed_kernel(
    act2,
    g2_ref,
    bproj_ref,
    bfc_ref,
    wfc,
    wproj,
    cot_in,
    cot_far,
    mid_in,
    att_in,
    wout_in,
    lout_out,
    gmid_out,
    gatt_out,
    dwout_out,
    f_out,
    f2_out,
    f3_out,
    p_out,
    dots,
    dbfc,
    small,
    cots,
    mids,
    atts,
    wout,
    acc,
    act2t,
    hid,
    slope,
    dpre,
    louts,
    gatts,
    dwouts,
    sel,
    bias,
    gf,
    gp,
    rf0,
    rp0,
    rfh,
    rp1,
    in_sem,
    out_sem,
    send_sem,
    recv_sem,
):
    t = pl.program_id(0)
    tiles = pl.num_programs(0) // 2
    tokens, width = act2.shape
    half = tokens // 2
    tile = dpre.shape[1]
    steps = tokens // QB
    count = gf.shape[0]
    _, core, x, _, _ = spot()
    me = lax.axis_index("blk")
    mine = pl.multiple_of(me * half, half)
    theirs = pl.multiple_of((1 - me) * half, half)
    both = partners()
    friends = [both[0], both[1], both[4]]
    side = pl.ds(pl.multiple_of(me * (tile // 2), tile // 2), tile // 2)

    def chain(held, got, dims, order, n):
        return Sum(held, got, dims, order, send_sem.at[n], recv_sem.at[n])

    full = ("far", "near", "x", "core")
    fcs = [chain(gf.at[n], [rf0.at[n], rfh.at[n]], full, ("core", "half"), n) for n in range(2)]
    fcs.append(chain(gf.at[2], [rf0.at[2]], full, ("core",), 2))
    projs = [chain(gp.at[n], [rp0.at[n], rp1.at[n]], full[2:], ("core", "x"), 3 + n) for n in range(4)]

    def load(n):
        src, dst = [
            (cot_in.at[me], cots.at[pl.ds(mine, half)]),
            (cot_far, cots.at[pl.ds(theirs, half // 2)]),
            (mid_in, mids),
            (att_in, atts),
            (wout_in, wout),
        ][n]
        return pltpu.make_async_copy(src, dst, in_sem.at[n])

    far_cot = push(
        cot_in.at[1 - me, pl.ds(half // 2, half // 2)],
        cots.at[pl.ds(pl.multiple_of(mine + half // 2, half // 2), half // 2)],
        send_sem.at[7, 0],
        recv_sem.at[7, 0],
        friends[2],
    )
    back = push(
        louts.at[pl.ds(theirs, half)], lout_out.at[me], send_sem.at[7, 1], recv_sem.at[7, 1], friends[2]
    )

    stores = [
        (louts.at[pl.ds(mine, half)], lout_out.at[me]),
        (acc, gmid_out),
        (gatts, gatt_out),
        (dwouts, dwout_out),
        (gf.at[3], f3_out),
    ]
    size = tile // 2
    stores += [
        (gf.at[n, :, :, :, core, :, side], f_out.at[:, :, :, :, n * size : (n + 1) * size]) for n in range(2)
    ]
    stores.append((gf.at[2, :, :, :, core], f2_out))
    stores += [(gp.at[n, x, core], p_out.at[n // 2, n % 2]) for n in range(4)]

    def store(n):
        return pltpu.make_async_copy(stores[n][0], stores[n][1], out_sem.at[n])

    def at_step(k, *actions):
        @pl.when(t == k)
        def _():
            for action in actions:
                action()

    @pl.when(t == 0)
    def _():
        for n in range(5):
            load(n).start()
        greet(friends)
        far_cot.start()
        act2t[...] = act2[...].T
        for n in range(count):
            bias[n] = row(bfc_ref)[:, n * tile : (n + 1) * tile]
        acc[...] = jnp.zeros_like(acc)
        head = lax.broadcasted_iota(jnp.int32, sel.shape, 0)
        feature = lax.broadcasted_iota(jnp.int32, sel.shape, 1)
        inside = (feature >= head * HEAD_DIM) & (feature < (head + 1) * HEAD_DIM)
        sel[...] = jnp.where(inside, 1.0, 0.0).astype(BF)

    @pl.when(t < tiles)
    def _():
        for c in range(steps):
            rows = slice(c * QB, (c + 1) * QB)
            u = nn(act2[rows, :], wfc[...]) + bias[t]
            square = u * u
            bend = jnp.tanh(u * (0.7978845608028654 + (0.7978845608028654 * 0.044715) * square))
            halfway = 0.5 + 0.5 * bend
            hidden = (u * halfway).astype(BF)
            hid[t, rows, :] = hidden
            slope[t, rows, :] = (
                halfway
                + (u * (0.5 - 0.5 * bend * bend))
                * (0.7978845608028654 + (3 * 0.7978845608028654 * 0.044715) * square)
            ).astype(BF)
            acc[rows, :] += nn(hidden, wproj[...])

    @pl.when(t == tiles - 1)
    def _():
        load(2).wait()
        for c in range(steps):
            rows = slice(c * QB, (c + 1) * QB)
            louts[rows, :] = (mids[rows, :] + acc[rows, :] + row(bproj_ref)).astype(BF)
        back.start()
        store(0).start()
        acc[...] = jnp.zeros_like(acc)
        load(0).wait()
        load(1).wait()
        far_cot.wait()

    @pl.when(t >= tiles)
    def _():
        n = t - tiles
        total = None
        for c in range(steps):
            rows = slice(c * QB, (c + 1) * QB)
            grad = (nt(cots[rows, :], wproj[...]) * slope[n, rows, :].astype(F32)).astype(BF)
            dpre[rows, :] = grad
            acc[rows, :] += nt(grad, wfc[...])
            part = column_sum(grad.astype(F32))
            total = part if total is None else total + part
            if c == 2:
                for k in range(3):
                    at_step(tiles + k + 1, lambda k=k: projs[k].take(0), lambda k=k: fcs[k].take(0))
        dbfc[...] = total
        gp[n] = tn(hid[n], cots[...]).astype(BF).reshape(gp.shape[1:])
        gf[n] = nn(act2t[...], dpre[...]).astype(BF).reshape(gf.shape[1:])

    for k in range(3):
        at_step(tiles + k, lambda k=k: projs[k].start(0), lambda k=k: fcs[k].start(0))
    at_step(tiles + 3, lambda: projs[3].start(0))

    @pl.when(t == 2 * tiles - 1)
    def _():
        store(4).start()
        store(7).start()
        load(3).wait()
        load(4).wait()
        projs[0].take(1)
        store(8).start()
        gain = row(g2_ref)
        sums = [None] * 4
        for c in range(steps):
            rows = slice(c * QB, (c + 1) * QB)
            middle = mids[rows, :]
            upstream = cots[rows, :].astype(F32)
            xhat, inverse = norm_parts(middle)
            da = acc[rows, :]
            grad_middle = upstream + norm_pull(da, xhat, inverse, gain)
            acc[rows, :] = grad_middle
            branch = grad_middle.astype(BF)
            dpre[rows, :] = branch
            parts = [
                column_sum(upstream),
                column_sum(da * xhat),
                column_sum(da),
                column_sum(branch.astype(F32)),
            ]
            sums = [b if a is None else a + b for a, b in zip(sums, parts)]
            ga = nt(branch, wout[...]).astype(BF)
            gatts[rows, :] = ga
            product = ga.astype(F32) * atts[rows, :].astype(F32)
            big = product.astype(BF)
            rest = (product - big.astype(F32)).astype(BF)
            dot = nt(sel[...], big) + nt(sel[...], rest)
            for p in range(PAIRS):
                dots[p, :, rows] = dot[2 * p : 2 * p + 2, :]
            if c == 1:
                projs[3].take(0)
        store(1).start()
        store(2).start()
        small[...] = jnp.concatenate(sums, axis=0)
        dwouts[...] = tn(atts[...], dpre[...]).astype(BF).reshape(dwouts.shape)
        store(3).start()
        projs[1].take(1)
        store(9).start()
        fcs[0].take(1)
        store(5).start()
        projs[2].take(1)
        store(10).start()
        fcs[1].take(1)
        store(6).start()
        projs[3].take(1)
        store(11).start()
        for n in range(len(stores)):
            store(n).wait()
        back.wait()


def feed(act2, cotangent, cot_far, mid, att, g2, bproj, wout, wfc, bfc, wproj):
    tokens, width = act2.shape
    half = tokens // 2
    ff = wfc.shape[1]
    tiles = 4
    tile = ff // tiles
    owner = width // 16
    owner_ff = ff // 16
    shape = jax.ShapeDtypeStruct
    flat = shape((tokens, width), BF)
    once = pl.Buffered(1)
    hbm = pl.BlockSpec(memory_space=pl.ANY)

    def whole(s):
        return pl.BlockSpec(s, lambda t: (0,) * len(s), pipeline_mode=once)

    def vm(*s):
        return pltpu.VMEM(s, BF)

    line = whole((width,))
    return pl.pallas_call(
        feed_kernel,
        grid=(2 * tiles,),
        in_specs=[
            whole((tokens, width)),
            line,
            line,
            whole((ff,)),
            pl.BlockSpec((width, tile), lambda t: (0, lax.rem(t, tiles))),
            pl.BlockSpec((tile, width), lambda t: (lax.rem(t, tiles), 0)),
        ]
        + [hbm] * 5,
        out_specs=[hbm] * 8
        + [
            whole((PAIRS, 2, tokens)),
            pl.BlockSpec((1, tile), lambda t: (0, jnp.maximum(t - tiles, 0))),
            whole((4, width)),
        ],
        out_shape=[
            shape((2, half, width), BF),
            shape((tokens, width), F32),
            flat,
            shape((2, 2, 2, 2, owner, width), BF),
            shape((2, 2, 2, owner, tile), BF),
            shape((2, 2, 2, owner, tile), BF),
            shape((2, 2, 2, 2, owner, tile), BF),
            shape((2, 2, owner_ff, width), BF),
            shape((PAIRS, 2, tokens), F32),
            shape((1, ff), F32),
            shape((4, width), F32),
        ],
        scratch_shapes=[
            vm(tokens, width),
            pltpu.VMEM((tokens, width), F32),
            vm(tokens, width),
            vm(width, width),
            pltpu.VMEM((tokens, width), F32),
            vm(width, tokens),
            vm(tiles, tokens, tile),
            vm(tiles, tokens, tile),
            vm(tokens, tile),
            vm(tokens, width),
            vm(tokens, width),
            vm(2, 2, 2, 2, owner, width),
            vm(16, width),
            pltpu.VMEM((tiles, 1, tile), F32),
            vm(tiles, 2, 2, 2, 2, owner, tile),
            vm(tiles, 2, 2, owner_ff, width),
            vm(3, 2, 2, 2, owner, tile),
            vm(4, 2, owner_ff, width),
            vm(2, 2, 2, 2, owner, tile // 2),
            vm(4, owner_ff, width),
            pltpu.SemaphoreType.DMA((5,)),
            pltpu.SemaphoreType.DMA((12,)),
            pltpu.SemaphoreType.DMA((8, 2)),
            pltpu.SemaphoreType.DMA((8, 2)),
        ],
        compiler_params=pltpu.CompilerParams(
            collective_id=1, has_side_effects=True, vmem_limit_bytes=62 * MIB
        ),
        name="feed",
    )(act2, g2, bproj, bfc, wfc, wproj, cotangent, cot_far, mid, att, wout)


FIRST_PAIR = PAIRS // 2


def pieces(width, val):
    lanes = LANES
    return [
        (3, [(3 * lanes, 3 * lanes), (width + 3 * lanes, 3 * lanes)]),
        (5, [(0, 2 * lanes), (width, 2 * lanes), (2 * width, 2 * lanes)]),
        (6, [(2 * lanes, lanes), (width + 2 * lanes, lanes), (2 * width + 2 * lanes, lanes)]),
    ]


def tail_kernel(
    q_in,
    k_in,
    v_in,
    do_in,
    bias_in,
    x_in,
    act1t_in,
    gmid_in,
    wqkv_in,
    dwout_in,
    f_in,
    f2_in,
    f3_in,
    p_in,
    lse_ref,
    d_ref,
    g1_ref,
    dbfc_ref,
    small_in,
    gx_out,
    gf_out,
    wqkv_out,
    wout_out,
    wfc_out,
    wproj_out,
    small_out,
    q_ref,
    k_ref,
    v_ref,
    do_ref,
    bias,
    xs,
    gmid,
    wqkv,
    dqk,
    dvs,
    gfs,
    dqa,
    act1t,
    gx,
    g_out,
    g_f,
    g_f2,
    g_f3,
    g_p,
    g_q,
    r_out,
    r_f,
    r_f2,
    r_f3,
    r_p,
    r_q,
    last_sum,
    r_z,
    r_last,
    sums,
    s_got,
    late,
    l_got,
    w_fc,
    w_proj,
    w_out,
    in_sem,
    out_sem,
    back_send,
    back_recv,
    sum_send,
    sum_recv,
    far_send,
    far_recv,
):
    tokens, width = q_ref.shape
    half = tokens // 2
    val = gfs.shape[1]
    steps = tokens // QB
    me = lax.axis_index("blk")
    mine = pl.multiple_of(me * half, half)
    theirs = pl.multiple_of((1 - me) * half, half)
    _, core, x, near, far = spot()
    friends = partners()
    parts = pieces(width, val)

    sources = {
        "f3": (f3_in, g_f3),
        "out": (dwout_in, g_out),
        "p": (p_in, g_p),
        "f": (f_in, g_f),
        "f2": (f2_in, g_f2),
        "q": (q_in, q_ref),
        "k": (k_in, k_ref),
        "bias": (bias_in, bias),
        "v": (v_in, v_ref),
        "do": (do_in, do_ref),
        "act1t": (act1t_in, act1t),
        "x": (x_in, xs),
        "wqkv": (wqkv_in, wqkv),
        "gmid": (gmid_in, gmid),
    }
    loads = {
        name: pltpu.make_async_copy(src, dst, in_sem.at[n])
        for n, (name, (src, dst)) in enumerate(sources.items())
    }
    for load in loads.values():
        load.start()
    greet([flipped(flip)[1] for flip in FLIPS] + [friends[0], friends[4]])

    full = ("far", "near", "x", "core")
    down = ("core", "x", "near", "far", "pair")
    sems = iter(range(16))

    def chain(held, got, dims, order, cut_columns=True):
        n = next(sems)
        return Sum(held, got, dims, order, sum_send.at[n], sum_recv.at[n], cut_columns)

    s_out = chain(g_out, r_out, full, down)
    s_f = chain(g_f, r_f, full[:3], ("x", "near", "far", "gather"), False)
    s_f2 = chain(g_f2, r_f2, full[:3], ("half", "x", "near", "far", "gather"))
    s_f3 = chain(g_f3, r_f3, full, ("core", "half", "x", "near", "far", "gather"))
    s_p = chain(g_p, r_p, full[:2], ("half", "near", "far", "gather"))
    s_q = [chain(g, r, full, down if n < 2 else down[:2]) for n, (g, r) in enumerate(zip(g_q, r_q))]
    n_small, n_last, n_late = next(sems), next(sems), next(sems)

    def vectors(held, got, place, n):
        return Vectors(held, got, place, (sum_send.at[n], sum_recv.at[n]), (far_send, far_recv))

    s_small = vectors(sums, s_got, 0, n_small)
    s_late = vectors(late, l_got, 1, n_late)

    def z_copies():
        found = []
        for n, flip in enumerate([flip for flip in FLIPS if flip[2] == 0]):
            place, friend = flipped(flip)
            src = g_q[2].at[place]
            found.append(push(src, r_z.at[n], far_send.at[2, n], far_recv.at[2, n], friend))
        return found

    def last_x():
        s_q[2].take(1)
        for copy in z_copies():
            copy.start()

    def last_z():
        for copy in z_copies():
            copy.wait()
        total = g_q[2][far, near, x, core].astype(F32)
        for n in range(3):
            total = total + r_z[n].astype(F32)
        last_sum[...] = total.astype(BF)
        last_copy.start()

    last_copy = push(
        last_sum, r_last, sum_send.at[n_last, 0], sum_recv.at[n_last, 0], friends[4]
    )

    def give_back(n, src, dst):
        return push(src, dst, back_send.at[n], back_recv.at[n], friends[4])

    for n in range(4):
        sums[0, n : n + 1, :] = small_in[n : n + 1, :]
        sums[0, 4 + n : 5 + n, :] = dbfc_ref[:, n * width : (n + 1) * width]
    s_small.start(0)
    for name, begin in (("f3", s_f3), ("p", s_p), ("f", s_f), ("f2", s_f2), ("out", s_out)):
        loads[name].wait()
        begin.start(0)
    for name in ("q", "k", "bias", "v", "do"):
        loads[name].wait()

    low = lax.broadcasted_iota(jnp.int32, (1, LANES), 1) < HEAD_DIM
    masks = [low, ~low]
    zero = jnp.zeros((), BF)
    gain = row(g1_ref)

    def columns(at, size):
        return dqk[:, at : at + size] if at < 2 * width else dvs[:, at - 2 * width : at - 2 * width + size]

    def project_grad(n):
        at = 0
        for start, size in parts[n][1]:
            block = nn(act1t[...], columns(start, size)).astype(BF)
            g_q[n][:, :, :, :, :, at : at + size] = block.reshape(g_q[n].shape[:-1] + (size,))
            at += size
        s_q[n].start(0)

    back_gf = give_back(1, gfs.at[pl.ds(theirs, half)], gf_out.at[me])
    keep_gf = pltpu.make_async_copy(gfs.at[pl.ds(mine, half)], gf_out.at[me], out_sem.at[1])

    def take(name, stage):
        return lambda: names[name].take(stage)

    names = {"sm": s_small, "f3": s_f3, "out": s_out, "f": s_f, "p": s_p, "f2": s_f2}
    names.update({"q0": s_q[0], "q1": s_q[1]})
    plan = {
        (0, 0): [take("sm", 0), take("f3", 0), take("out", 0)],
        (1, 1): [take("f", 0)],
        (2, 1): [take("p", 0), take("sm", 1), loads["act1t"].wait],
        (3, 0): [take("f", 1), lambda: project_grad(0), back_gf.start, keep_gf.start],
        (3, 1): [take("q0", 0), take("f2", 0), take("out", 1)],
        (4, 0): [take("p", 1)],
        (4, 1): [take("f3", 1), take("f", 2), take("sm", 2)],
        (5, 0): [take("q0", 1), take("out", 2), lambda: project_grad(1)],
        (5, 1): [take("q1", 0), take("f2", 1), take("p", 2)],
    }

    def act(step, middle):
        for (k, when), actions in plan.items():
            if when == middle:

                @pl.when(step == k)
                def _():
                    for action in actions:
                        action()

    @pl.loop(0, PAIRS)
    def _(step):
        act(step, 0)
        p = lax.rem(step + FIRST_PAIR, PAIRS)
        cols = pl.ds(pl.multiple_of(p * LANES, LANES), LANES)
        kcols = pl.ds(pl.multiple_of(width + p * LANES, LANES), LANES)
        q, k, v, do = q_ref[:, cols], k_ref[:, cols], v_ref[:, cols], do_ref[:, cols]
        qm = [jnp.where(m, q, zero) for m in masks]
        km = [jnp.where(m, k, zero) for m in masks]
        dom = [jnp.where(m, do, zero) for m in masks]
        dvals = []
        for j in range(steps):
            a = j * QB
            keys = slice(a, a + QB)
            dk = dv = dq = None
            for h in range(2):
                s = nt(k[keys], qm[h][a:]) + bias[keys, a:]
                probs = jnp.exp(s - lse_ref[p, h : h + 1, a:])
                dp = nt(v[keys], dom[h][a:])
                ds = (probs * (dp - d_ref[p, h : h + 1, a:])).astype(BF)
                dvh = nn(probs.astype(BF), dom[h][a:])
                dkh = nn(ds, qm[h][a:])
                dqh = tn(ds, km[h][keys])
                dk = dkh if dk is None else dk + dkh
                dv = dvh if dv is None else dv + dvh
                dq = dqh if dq is None else dq + dqh
            dqk[keys, kcols] = dk.astype(BF)
            dvals.append(dv.astype(BF))
            if j == 0:
                act(step, 1)
            if j == 0:
                dqa[...] = dq
            else:
                dqa[a:, :] += dq
        dqk[:, cols] = (dqa[...] * HEAD_DIM**-0.5).astype(BF)

        @pl.when(p < PAIRS // 2)
        def _():
            for j in range(steps):
                dvs[j * QB : (j + 1) * QB, cols] = dvals[j]

        @pl.when(p >= PAIRS // 2)
        def _():
            late = pl.ds(pl.multiple_of(p * LANES - val, LANES), LANES)
            for j in range(steps):
                gfs[j * QB : (j + 1) * QB, late] = dvals[j]

    for name in ("x", "wqkv", "gmid"):
        loads[name].wait()

    totals = [None] * 4

    def input_grad(start, size):
        rows = pl.ds(pl.multiple_of(start, size), size)
        da = nt(dqk[rows, :], wqkv[:, : 2 * width]) + nt(dvs[rows, :], wqkv[:, 2 * width :])
        xhat, inverse = norm_parts(xs[rows, :].astype(F32))
        gx[rows, :] = (gmid[rows, :] + norm_pull(da, xhat, inverse, gain)).astype(BF)
        bv = column_sum(dvs[rows, :].astype(F32))
        found = [
            column_sum(da * xhat),
            column_sum(da),
            column_sum(dqk[rows, :width].astype(F32)),
            jnp.concatenate([bv, jnp.zeros((1, width - val), F32)], axis=1),
        ]
        totals[:] = [b if a is None else a + b for a, b in zip(totals, found)]

    backs = []

    def give_rows(at, size):
        start = pl.multiple_of(theirs + at, size)
        input_grad(start, size)
        copy = give_back(2 + len(backs), gx.at[pl.ds(start, size)], gx_out.at[me, pl.ds(at, size)])
        copy.start()
        backs.append(copy)

    s_q[0].take(2)
    s_f3.take(2)
    give_rows(0, LANES)
    project_grad(2)
    s_out.take(3)
    give_rows(LANES, LANES)
    s_f2.take(2)
    s_q[2].take(0)
    give_rows(QB, LANES)
    s_q[1].take(1)
    s_q[0].take(3)
    give_rows(QB + LANES, LANES)
    s_f3.take(3)
    input_grad(mine, LANES)
    s_f2.take(3)
    input_grad(mine + LANES, LANES)
    last_x()
    input_grad(mine + QB, LANES)
    s_q[1].take(2)
    input_grad(mine + QB + LANES, LANES)
    keep_gx = pltpu.make_async_copy(gx.at[pl.ds(mine, half)], gx_out.at[me], out_sem.at[2])
    keep_gx.start()
    late[0] = jnp.concatenate(totals, axis=0)
    s_late.start(0)
    s_late.take(0)
    s_f3.take(4)
    last_z()
    s_q[1].take(3)
    s_late.take(1)

    def write(n, src, dst):
        copy = pltpu.make_async_copy(src, dst, out_sem.at[3 + n])
        copy.start()
        return copy

    side = width // 2
    for part, who in zip(s_p.last(), (me, 1 - me)):
        w_proj[:, pl.ds(pl.multiple_of(who * side, side), side)] = part
    writes = [write(0, w_proj, wproj_out)]
    tile = g_f3.shape[-1]
    side = tile // 2
    for sum_, tiles in ((s_f, (0, 1)), (s_f2, (2,)), (s_f3, (3,))):
        for part, who in zip(sum_.last(), (me, 1 - me)):
            for n, t in enumerate(tiles):
                at = pl.ds(pl.multiple_of(t * tile + who * side, side), side)
                w_fc[:, at] = part[:, n * side : (n + 1) * side]
    writes.append(write(1, w_fc, wfc_out))
    own, came = s_out.last()
    w_out[...] = own + came
    writes.append(write(2, w_out, wout_out))
    last_copy.wait()
    for n in range(3):
        if n < 2:
            own, came = s_q[n].last()
        else:
            own, came = last_sum[...].astype(F32), r_last[...].astype(F32)
        part = own + came
        at = 0
        for start, size in parts[n][1]:
            wqkv_out[:, start : start + size] = part[:, at : at + size]
            at += size
    s_late.take(2)
    small_out[...] = jnp.concatenate(
        [sums[3, 0:4, :], late[3], sums[3, 4:8, :], jnp.zeros((4, width), F32)], axis=0
    )
    back_gf.wait()
    for copy in backs:
        copy.wait()
    for copy in writes:
        copy.wait()
    keep_gf.wait()
    keep_gx.wait()


def tail(
    q, k, v, do, bias, x, act1t, gmid, wqkv, dwout, f, f2, f3, p, lse, dots, g1, dbfc, small
):
    tokens, width = q.shape
    half = tokens // 2
    val = wqkv.shape[1] - 2 * width
    owner = width // 16
    owner_ff = dbfc.shape[1] // 16
    ff = dbfc.shape[1]
    tile = f3.shape[-1]
    shape = jax.ShapeDtypeStruct
    hbm = pl.BlockSpec(memory_space=pl.ANY)
    vmem = pl.BlockSpec(memory_space=pltpu.VMEM)

    def vm(*s):
        return pltpu.VMEM(s, BF)

    def chain(rows, cols):
        return [
            vm(2, 2, 2, rows, cols),
            vm(2, 2, rows, cols),
            vm(2, rows, cols),
            vm(rows, cols),
            vm(rows, cols),
        ]

    def cut_chain(rows, cols):
        side = chain(rows, cols // 2)
        return [vm(2, 2, 2, rows, cols)] + side[:1] + side[1:4] + side[3:4]

    flat = vm(tokens, width)
    sizes = [sum(size for _, size in columns) for _, columns in pieces(width, val)]
    return pl.pallas_call(
        tail_kernel,
        in_specs=[hbm] * 14 + [vmem] * 5,
        out_specs=[hbm] * 2 + [vmem] + [hbm] * 3 + [vmem],
        out_shape=[
            shape((2, half, width), BF),
            shape((2, half, val), BF),
            shape((owner, wqkv.shape[1]), F32),
            shape((owner, width), F32),
            shape((owner, ff), F32),
            shape((owner_ff, width), F32),
            shape((16, width), F32),
        ],
        scratch_shapes=[
            flat,
            flat,
            flat,
            flat,
            pltpu.VMEM((tokens, tokens), F32),
            flat,
            pltpu.VMEM((tokens, width), F32),
            vm(*wqkv.shape),
            vm(tokens, 2 * width),
            vm(tokens, val),
            vm(tokens, val),
            pltpu.VMEM((tokens, LANES), F32),
            vm(width, tokens),
            flat,
            vm(*dwout.shape),
            vm(*f.shape),
            vm(*f2.shape),
            vm(*f3.shape),
            vm(*p.shape),
            [vm(2, 2, 2, 2, owner, size) for size in sizes],
            chain(owner, width),
            chain(owner, f.shape[-1])[1:],
            cut_chain(owner, tile)[1:],
            cut_chain(owner, tile),
            [vm(2, 2, owner_ff, width // 2)] + cut_chain(owner_ff, width)[3:],
            [chain(owner, size) for size in sizes[:2]] + [chain(owner, sizes[2])[:2]],
            vm(owner, sizes[2]),
            vm(3, owner, sizes[2]),
            vm(owner, sizes[2]),
            pltpu.VMEM((4, 8, width), F32),
            [pltpu.VMEM(n + (8, width), F32) for n in ((), (len(FLIPS),), ())],
            pltpu.VMEM((4, 4, width), F32),
            [pltpu.VMEM(n + (4, width), F32) for n in ((), (len(FLIPS),), ())],
            pltpu.VMEM((owner, ff), F32),
            pltpu.VMEM((owner_ff, width), F32),
            pltpu.VMEM((owner, width), F32),
            pltpu.SemaphoreType.DMA((14,)),
            pltpu.SemaphoreType.DMA((6,)),
            pltpu.SemaphoreType.DMA((6,)),
            pltpu.SemaphoreType.DMA((6,)),
            pltpu.SemaphoreType.DMA((11, 6)),
            pltpu.SemaphoreType.DMA((11, 6)),
            pltpu.SemaphoreType.DMA((3, len(FLIPS))),
            pltpu.SemaphoreType.DMA((3, len(FLIPS))),
        ],
        compiler_params=pltpu.CompilerParams(
            collective_id=2, has_side_effects=True, vmem_limit_bytes=62 * MIB
        ),
        name="tail",
    )(q, k, v, do, bias, x, act1t, gmid, wqkv, dwout, f, f2, f3, p, lse, dots, g1, dbfc, small)


def finish_kernel(*refs):
    wide_in, sums = refs[:7], refs[7]
    wide_out, small_out, held, sem = refs[8:15], refs[15:24], refs[24], refs[25]
    loads = [pltpu.make_async_copy(src, dst, sem.at[0, n]) for n, (src, dst) in enumerate(zip(wide_in, held))]
    stores = [pltpu.make_async_copy(src, dst, sem.at[1, n]) for n, (src, dst) in enumerate(zip(held, wide_out))]
    for load in loads:
        load.start()
    b = lax.axis_index("batch")
    rows = sums[0:8, :]
    width = rows.shape[1]
    long = jnp.concatenate([sums[8 + n : 9 + n, :] for n in range(4)], axis=1)
    long = jnp.broadcast_to(long, (8, 4 * width))
    for at, ref in zip((4, 5, 6, 7, 3, 1, 2, None, 0), small_out):
        size = ref.shape[0]
        source = long if at is None else rows
        line = 0 if at is None else at
        length = source.shape[1]
        turned = pltpu.roll(source, lax.rem(length - b * size, length), 1)
        ref[...] = turned[line, :size]
    for load, store in zip(loads, stores):
        load.wait()
        store.start()
    for store in stores:
        store.wait()


def finish(wide, sums, sizes):
    hbm = pl.BlockSpec(memory_space=pl.ANY)
    vmem = pl.BlockSpec(memory_space=pltpu.VMEM)
    shape = jax.ShapeDtypeStruct
    return pl.pallas_call(
        finish_kernel,
        in_specs=[hbm] * 7 + [vmem],
        out_specs=[hbm] * 7 + [vmem] * 9,
        out_shape=[shape(a.shape, a.dtype) for a in wide] + [shape((n,), F32) for n in sizes],
        scratch_shapes=[
            [pltpu.VMEM(a.shape, a.dtype) for a in wide],
            pltpu.SemaphoreType.DMA((2, 7)),
        ],
        compiler_params=pltpu.CompilerParams(vmem_limit_bytes=60 * MIB),
        name="finish",
    )(*wide, sums)


def paired(
    inputs,
    first_values,
    segments,
    ln1_gain,
    first_norm_bias,
    w_qkv,
    b_query,
    b_value,
    w_out,
    b_out,
    ln2_gain,
    second_norm_bias,
    w_fc,
    b_fc,
    w_proj,
    b_proj,
    cotangent,
):
    half, width = inputs.shape[1], inputs.shape[2]
    val = first_values.shape[2]
    x, q, k, v, att, act2, mid, lse, bias, act1t, cot_far = front(
        inputs,
        first_values,
        segments,
        cotangent,
        ln1_gain,
        first_norm_bias,
        w_qkv,
        b_query,
        b_value,
        w_out,
        b_out,
        ln2_gain,
        second_norm_bias,
    )
    layer_out, gmid, gatt, dwout, f, f2, f3, p, dots, dbfc, small = feed(
        act2, cotangent, cot_far, mid, att, ln2_gain, b_proj, w_out, w_fc, b_fc, w_proj
    )
    owner = width // 16
    *wide, sums = tail(
        q,
        k,
        v,
        gatt,
        bias,
        x,
        act1t,
        gmid,
        w_qkv,
        dwout,
        f,
        f2,
        f3,
        p,
        lse,
        dots,
        ln1_gain,
        dbfc,
        small,
    )
    sizes = [owner, owner, owner, val // 16, owner, owner, owner, w_fc.shape[1] // 16, owner]
    out = finish([layer_out] + wide, sums, sizes)
    layer_out, grad_inputs, grad_first, gwqkv, gwout, gwfc, gwproj = out[:7]
    g1, b1, bq, bv, bo, g2, b2, bf, bp = out[7:]
    return (
        layer_out,
        grad_inputs,
        grad_first,
        g1,
        b1,
        gwqkv,
        bq,
        bv,
        gwout,
        bo,
        g2,
        b2,
        gwfc,
        bf,
        gwproj,
        bp,
    )


MICRO = 2


def as_sent(shard):
    return jax.tree.map(lambda a: a.astype(jnp.bfloat16) if a.dtype == jnp.float32 else a, shard)


def apply_norm(values_in, norm_gain, shift_bias):
    mean_val = jnp.mean(values_in, axis=-1, keepdims=True)
    centred_rows = values_in - mean_val
    inverse_deviation = lax.rsqrt(
        jnp.mean(centred_rows * centred_rows, axis=-1, keepdims=True) + EPS
    )
    standardized = centred_rows * inverse_deviation
    return (standardized * norm_gain + shift_bias, standardized, inverse_deviation)


def apply_norm_backward(upstream_gradient, standardized, inverse_deviation, norm_gain):
    scaled_rows = upstream_gradient * norm_gain
    first_average = jnp.mean(scaled_rows, axis=-1, keepdims=True)
    second_average = jnp.mean(scaled_rows * standardized, axis=-1, keepdims=True)
    incoming_gradient = inverse_deviation * (
        scaled_rows - first_average - standardized * second_average
    )
    return (
        incoming_gradient,
        jnp.sum(upstream_gradient * standardized, axis=(0, 1)),
        jnp.sum(upstream_gradient, axis=(0, 1)),
    )


def gelu_tanh(values_in):
    cubic = values_in + 0.044715 * values_in * values_in * values_in
    return 0.5 * values_in * (1.0 + jnp.tanh(0.7978845608028654 * cubic))


def heads_of(values_in):
    return values_in.reshape(values_in.shape[0], values_in.shape[1], HEADS, HEAD_DIM)


def visible(seg_query, seg_key, query_pos, key_pos):
    same = seg_query[:, :, None] == seg_key[:, None, :]
    causal = key_pos[None, :] <= query_pos[:, None]
    live = seg_query[:, :, None] >= 0
    diagonal = key_pos[None, :] == query_pos[:, None]
    return (same & causal[None] & live | diagonal[None])[:, :, None, :]


def score_block(query4, key4, mask):
    raw = jnp.einsum("rqhd,rkhd->rqhk", query4, key4, preferred_element_type=jnp.float32)
    return jnp.where(mask, raw * HEAD_DIM ** (-0.5), NEG)


def grad_block(query4, key4, value4, dout4, log_total, out_dot, mask):
    probs = jnp.where(mask, jnp.exp(score_block(query4, key4, mask) - log_total[..., None]), 0.0)
    probs_low = probs.astype(jnp.bfloat16)
    grad_probs = jnp.einsum("rqhd,rkhd->rqhk", dout4, value4, preferred_element_type=jnp.float32)
    grad_scores = (probs * (grad_probs - out_dot[..., None]) * HEAD_DIM ** (-0.5)).astype(
        jnp.bfloat16
    )
    return (probs_low, grad_scores)


def spread(
    inputs,
    first_values,
    segments,
    ln1_gain,
    first_norm_bias,
    w_qkv,
    b_query,
    b_value,
    w_out,
    b_out,
    ln2_gain,
    second_norm_bias,
    w_fc,
    b_fc,
    w_proj,
    b_proj,
    cotangent,
):
    all_seg = lax.all_gather(segments, "blk", axis=1, tiled=True)
    block_len = inputs.shape[1]
    model_width = inputs.shape[2]
    val_width = first_values.shape[2]
    rows_mb = inputs.shape[0] // MICRO
    own_pos = lax.axis_index("blk") * block_len + jnp.arange(block_len)
    first_gain = ln1_gain.astype(jnp.float32)
    second_gain = ln2_gain.astype(jnp.float32)
    outputs = []
    input_grads = []
    first_grads = []
    totals = None
    for micro_step in range(MICRO):
        first_row = micro_step * rows_mb
        last_row = first_row + rows_mb
        residual_stream = inputs[first_row:last_row].astype(jnp.float32)
        first_part = first_values[first_row:last_row]
        seg_local = segments[first_row:last_row]
        seg_row = all_seg[first_row:last_row]
        cot_part = cotangent[first_row:last_row]
        first_normed_rows, first_standardized, first_inverse_deviation = apply_norm(
            residual_stream, first_gain, first_norm_bias.astype(jnp.float32)
        )
        act1 = first_normed_rows.astype(jnp.bfloat16)
        projected = jnp.einsum("rbd,de->rbe", act1, w_qkv, preferred_element_type=jnp.float32)
        queries = (projected[..., :model_width] + b_query.astype(jnp.float32)).astype(jnp.bfloat16)
        keys_low = projected[..., model_width : 2 * model_width].astype(jnp.bfloat16)
        fresh = (projected[..., 2 * model_width :] + b_value.astype(jnp.float32)).astype(
            jnp.bfloat16
        )
        values_low = jnp.concatenate([fresh, first_part], axis=-1)
        query4 = heads_of(queries)
        key_part = lax.all_gather(keys_low, "blk", axis=1, tiled=True)
        value_part = lax.all_gather(values_low, "blk", axis=1, tiled=True)
        span = key_part.shape[1]
        key_pos = jnp.arange(span)
        mask = visible(seg_local, seg_row, own_pos, key_pos)
        scores = score_block(query4, heads_of(key_part), mask)
        old_max = jnp.full((rows_mb, block_len, HEADS), NEG, jnp.float32)
        new_max = jnp.maximum(old_max, jnp.max(scores, axis=-1))
        weights = jnp.where(mask, jnp.exp(scores - new_max[..., None]), 0.0)
        new_sum = jnp.sum(weights, axis=-1)
        new_acc = jnp.einsum(
            "rqhk,rkhd->rqhd",
            weights.astype(jnp.bfloat16),
            heads_of(value_part),
            preferred_element_type=jnp.float32,
        )
        attention4 = new_acc / new_sum[..., None]
        log_total = new_max + jnp.log(new_sum)
        attention_low = attention4.reshape(rows_mb, block_len, model_width).astype(jnp.bfloat16)
        branch = jnp.einsum("rbd,de->rbe", attention_low, w_out, preferred_element_type=jnp.float32)
        middle_state = residual_stream + branch + b_out.astype(jnp.float32)
        second_normed_rows, second_standardized, second_inverse_deviation = apply_norm(
            middle_state, second_gain, second_norm_bias.astype(jnp.float32)
        )
        act2 = second_normed_rows.astype(jnp.bfloat16)
        pre_gelu = jnp.einsum(
            "rbd,df->rbf", act2, w_fc, preferred_element_type=jnp.float32
        ) + b_fc.astype(jnp.float32)
        hidden = gelu_tanh(pre_gelu).astype(jnp.bfloat16)
        result = middle_state + jnp.einsum(
            "rbf,fd->rbd", hidden, w_proj, preferred_element_type=jnp.float32
        )
        result = result + b_proj.astype(jnp.float32)
        outputs.append(result.astype(jnp.bfloat16))
        upstream_gradient = cot_part.astype(jnp.float32)
        grad_wproj = jnp.einsum("rbf,rbd->fd", hidden, cot_part, preferred_element_type=jnp.float32)
        grad_bproj = jnp.sum(upstream_gradient, axis=(0, 1))
        grad_hidden = jnp.einsum(
            "rbd,fd->rbf", cot_part, w_proj, preferred_element_type=jnp.float32
        )
        gelu_value, gelu_pull = jax.vjp(gelu_tanh, pre_gelu)
        grad_pre = gelu_pull(grad_hidden)[0].astype(jnp.bfloat16)
        grad_wfc = jnp.einsum("rbd,rbf->df", act2, grad_pre, preferred_element_type=jnp.float32)
        grad_bfc = jnp.sum(grad_pre.astype(jnp.float32), axis=(0, 1))
        second_activation_gradient = jnp.einsum(
            "rbf,df->rbd", grad_pre, w_fc, preferred_element_type=jnp.float32
        )
        second_norm_gradient, second_gain_gradient, second_bias_gradient = apply_norm_backward(
            second_activation_gradient, second_standardized, second_inverse_deviation, second_gain
        )
        grad_middle = upstream_gradient + second_norm_gradient
        grad_branch = grad_middle.astype(jnp.bfloat16)
        grad_wout = jnp.einsum(
            "rbd,rbe->de", attention_low, grad_branch, preferred_element_type=jnp.float32
        )
        grad_bout = jnp.sum(grad_branch.astype(jnp.float32), axis=(0, 1))
        grad_attention = jnp.einsum(
            "rbe,de->rbd", grad_branch, w_out, preferred_element_type=jnp.float32
        ).astype(jnp.bfloat16)
        dout4 = heads_of(grad_attention)
        out_dot = jnp.sum(dout4.astype(jnp.float32) * attention4, axis=-1)
        back_key_part = lax.all_gather(keys_low, "blk", axis=1, tiled=True)
        back_value_part = lax.all_gather(values_low, "blk", axis=1, tiled=True)
        back_span = back_key_part.shape[1]
        back_key_pos = jnp.arange(back_span)
        back_mask = visible(seg_local, seg_row, own_pos, back_key_pos)
        part_key4 = heads_of(back_key_part)
        probs_low, grad_scores = grad_block(
            query4, part_key4, heads_of(back_value_part), dout4, log_total, out_dot, back_mask
        )
        query_acc = jnp.einsum(
            "rqhk,rkhd->rqhd", grad_scores, part_key4, preferred_element_type=jnp.float32
        )
        key_piece = jnp.einsum(
            "rqhk,rqhd->rkhd", grad_scores, query4, preferred_element_type=jnp.float32
        ).reshape(rows_mb, back_span, model_width)
        value_piece = jnp.einsum(
            "rqhk,rqhd->rkhd", probs_low, dout4, preferred_element_type=jnp.float32
        ).reshape(rows_mb, back_span, model_width)
        query_acc, key_acc, value_acc = (query_acc, key_piece, value_piece)
        grad_keys, grad_values = (
            lax.psum_scatter(
                key_acc.astype(jnp.bfloat16), "blk", scatter_dimension=1, tiled=True
            ).astype(jnp.float32),
            lax.psum_scatter(
                value_acc.astype(jnp.bfloat16), "blk", scatter_dimension=1, tiled=True
            ).astype(jnp.float32),
        )
        grad_query = query_acc.reshape(rows_mb, block_len, model_width)
        grad_qkv = jnp.concatenate(
            [
                grad_query.astype(jnp.bfloat16),
                grad_keys.astype(jnp.bfloat16),
                grad_values[..., :val_width].astype(jnp.bfloat16),
            ],
            axis=-1,
        )
        first_grads.append(grad_values[..., val_width:].astype(jnp.bfloat16))
        grad_wqkv = jnp.einsum("rbd,rbe->de", act1, grad_qkv, preferred_element_type=jnp.float32)
        grad_bquery = jnp.sum(grad_qkv[..., :model_width].astype(jnp.float32), axis=(0, 1))
        grad_bvalue = jnp.sum(grad_qkv[..., 2 * model_width :].astype(jnp.float32), axis=(0, 1))
        first_activation_gradient = jnp.einsum(
            "rbe,de->rbd", grad_qkv, w_qkv, preferred_element_type=jnp.float32
        )
        first_norm_gradient, first_gain_gradient, first_bias_gradient = apply_norm_backward(
            first_activation_gradient, first_standardized, first_inverse_deviation, first_gain
        )
        input_grads.append((grad_middle + first_norm_gradient).astype(jnp.bfloat16))
        gradient_set = (
            first_gain_gradient,
            first_bias_gradient,
            grad_wqkv,
            grad_bquery,
            grad_bvalue,
            grad_wout,
            grad_bout,
            second_gain_gradient,
            second_bias_gradient,
            grad_wfc,
            grad_bfc,
            grad_wproj,
            grad_bproj,
        )
        if totals is None:
            totals = gradient_set
        else:
            totals = tuple((older + newer for older, newer in zip(totals, gradient_set)))
    totals = jax.tree.map(
        lambda part: part.astype(jnp.float32),
        lax.psum_scatter(as_sent(totals), "batch", scatter_dimension=0, tiled=True),
    )
    totals = jax.tree.map(lambda part: part.astype(jnp.float32), lax.psum(as_sent(totals), "blk"))
    return (
        jnp.concatenate(outputs, axis=0),
        jnp.concatenate(input_grads, axis=0),
        jnp.concatenate(first_grads, axis=0),
    ) + tuple(totals)


def layer(inputs, *rest):
    whole_rows = lax.axis_size("blk") == inputs.shape[0] == 2 and inputs.shape[1] == 2 * QB
    whole_rows = whole_rows and lax.axis_size("batch") == 16
    return (paired if whole_rows else spread)(inputs, *rest)


def solution(mesh):
    rows = P("batch", "blk", None)
    flat = P("batch")
    wide = P("batch", None)
    return jax.shard_map(
        layer,
        mesh=mesh,
        in_specs=(rows, rows, P("batch", "blk")) + (P(),) * 13 + (rows,),
        out_specs=(rows, rows, rows)
        + (flat, flat, wide, flat, flat, wide, flat, flat, flat, wide, flat, wide, flat),
        check_vma=False,
    )
```

```python
import functools

import jax
import jax.numpy as jnp
from jax import lax
from jax.experimental import pallas as pl
from jax.experimental.pallas import tpu as pltpu
from jax.sharding import PartitionSpec as P

HEADS = 12
HEAD_DIM = 64
PAIRS = HEADS // 2
LANES = 2 * HEAD_DIM
EPS = 1e-05
NEG = -1e30
QB = 256
F32 = jnp.float32
BF = jnp.bfloat16
MIB = 2**20
MESH = pl.DeviceIdType.MESH


def nn(a, b):
    return lax.dot_general(a, b, (((1,), (0,)), ((), ())), preferred_element_type=F32)


def nt(a, b):
    return lax.dot_general(a, b, (((1,), (1,)), ((), ())), preferred_element_type=F32)


def tn(a, b):
    return lax.dot_general(a, b, (((0,), (0,)), ((), ())), preferred_element_type=F32)


def norm_parts(rows):
    mean = jnp.mean(rows, axis=-1, keepdims=True)
    centred = rows - mean
    inverse = lax.rsqrt(jnp.mean(centred * centred, axis=-1, keepdims=True) + EPS)
    return centred * inverse, inverse


def norm_pull(grad, xhat, inverse, gain):
    scaled = grad * gain
    first = jnp.mean(scaled, axis=-1, keepdims=True)
    second = jnp.mean(scaled * xhat, axis=-1, keepdims=True)
    return inverse * (scaled - first - xhat * second)


def row(ref):
    return ref[...].astype(F32).reshape(1, -1)


def column_sum(rows):
    return jnp.sum(rows, axis=0, keepdims=True)


def spot():
    b = lax.axis_index("batch")
    core = lax.rem(b, 2)
    x = lax.rem(lax.div(b, 2), 2)
    near = lax.rem(lax.div(b, 4), 2)
    far = lax.div(b, 8)
    return b, core, x, near, far


def partners():
    b, core, x, near, far = spot()
    return [
        {"batch": b + 1 - 2 * core},
        {"batch": b + 2 - 4 * x},
        {"batch": b + 4 - 8 * near},
        {"batch": b + 8 - 16 * far},
        {"blk": 1 - lax.axis_index("blk")},
    ]


FLIPS = [(f, n, x) for f in range(2) for n in range(2) for x in range(2) if f + n + x]


def flipped(flip):
    _, core, x, near, far = spot()
    at = [own + turn * (1 - 2 * own) for own, turn in zip((far, near, x), flip)]
    return tuple(at) + (core,), {"batch": ((at[0] * 2 + at[1]) * 2 + at[2]) * 2 + core}


def greet(friends):
    barrier = pltpu.get_barrier_semaphore()
    for friend in friends:
        pl.semaphore_signal(barrier, inc=1, device_id=friend, device_id_type=MESH)


def meet(friends):
    pl.semaphore_wait(pltpu.get_barrier_semaphore(), len(friends))


def push(src, dst, send_sem, recv_sem, friend):
    copy = pltpu.make_async_remote_copy(
        src_ref=src,
        dst_ref=dst,
        send_sem=send_sem,
        recv_sem=recv_sem,
        device_id=friend,
        device_id_type=MESH,
    )
    return copy


def add_into(dst, src):
    dst[...] = dst[...] + src[...]


PLACES = ("core", "x", "near", "far")


class Sum:
    def __init__(self, held, got, dims, order, send_sem, recv_sem, cut_columns=True):
        self.held, self.got, self.dims, self.order = held, got, dims, order
        self.send_sem, self.recv_sem, self.cut_columns = send_sem, recv_sem, cut_columns

    def cut(self, stage, keep):
        name = self.order[stage]
        done = self.order[:stage]
        _, core, x, near, far = spot()
        own = {"core": core, "x": x, "near": near, "far": far}
        at = []
        for dim in self.dims:
            if dim == name:
                at.append(own[dim] if keep else 1 - own[dim])
            else:
                at.append(own[dim] if dim in done else slice(None))
        if self.cut_columns and (name == "half" or "half" in done):
            me = lax.axis_index("blk")
            size = self.held.shape[-1] // 2
            side = 1 - me if name == "half" and not keep else me
            at += [slice(None), pl.ds(pl.multiple_of(side * size, size), size)]
        return tuple(at)

    def copy(self, stage):
        name = self.order[stage]
        return push(
            self.held.at[self.cut(stage, False)],
            self.got[stage],
            self.send_sem.at[stage],
            self.recv_sem.at[stage],
            partners()[PLACES.index(name) if name in PLACES else 4],
        )

    def start(self, stage):
        self.copy(stage).start()

    def take(self, stage):
        self.copy(stage).wait()
        mine = self.held.at[self.cut(stage, True)]
        came = self.got[stage]
        lead = came.shape[:-2]
        count = 1
        for size in lead:
            count *= size
        for n in range(count):
            at = []
            for size in reversed(lead):
                at.insert(0, n % size)
                n //= size
            at = tuple(at)
            add_into(mine.at[at] if at else mine, came.at[at] if at else came)
        if stage + 1 < len(self.order):
            self.start(stage + 1)

    def last(self):
        stage = len(self.order) - 1
        self.copy(stage).wait()
        return self.held[self.cut(stage, True)].astype(F32), self.got[stage][...].astype(F32)


class Vectors:
    def __init__(self, held, got, place, sems, far_sems):
        self.held, self.got, self.place = held, got, place
        self.sems, self.far_sems = sems, far_sems

    def copies(self, stage):
        src = self.held.at[stage]
        if stage == 1:
            return [
                push(
                    src,
                    self.got[1].at[n],
                    self.far_sems[0].at[self.place, n],
                    self.far_sems[1].at[self.place, n],
                    flipped(flip)[1],
                )
                for n, flip in enumerate(FLIPS)
            ]
        friend = partners()[stage * 2]
        return [push(src, self.got[stage], self.sems[0].at[stage], self.sems[1].at[stage], friend)]

    def start(self, stage):
        for copy in self.copies(stage):
            copy.start()

    def take(self, stage):
        for copy in self.copies(stage):
            copy.wait()
        if stage == 1:
            total = self.held[1]
            for n in range(len(FLIPS)):
                total = total + self.got[1][n]
        else:
            total = self.held[stage] + self.got[stage][...]
        self.held[stage + 1] = total
        if stage < 2:
            self.start(stage + 1)


def front_kernel(
    x_in,
    fv_in,
    seg_in,
    cot_in,
    g1_ref,
    b1_ref,
    wqkv_in,
    bq_ref,
    bv_ref,
    wout_in,
    bout_ref,
    g2_ref,
    b2_ref,
    x_out,
    q_out,
    k_out,
    v_out,
    att_out,
    act2_out,
    mid_out,
    lse_ref,
    bias_out,
    act1t_out,
    cot_out,
    xs,
    qs,
    ks,
    vs,
    atts,
    act2s,
    mids,
    bias,
    wqkv,
    wout,
    segrow,
    segsend,
    segcol,
    act1ts,
    turned,
    held,
    in_sem,
    out_sem,
    send_sem,
    recv_sem,
):
    half = x_in.shape[1]
    tokens = 2 * half
    width = x_in.shape[2]
    val = fv_in.shape[2]
    steps = tokens // QB
    me = lax.axis_index("blk")
    other = 1 - me
    mine = pl.multiple_of(me * half, half)
    theirs = pl.multiple_of(other * half, half)

    def local_in(i, src, dst):
        copy = pltpu.make_async_copy(src, dst, in_sem.at[i])
        copy.start()
        return copy

    own_x = local_in(0, x_in.at[me], xs.at[pl.ds(mine, half)])
    own_fv = local_in(1, fv_in.at[me], vs.at[pl.ds(mine, half), pl.ds(val, val)])
    own_w = local_in(2, wqkv_in, wqkv)
    own_wo = local_in(3, wout_in, wout)
    first, second = seg_in[0:1, :], seg_in[1:2, :]
    segsend[...] = jnp.broadcast_to(jnp.where(me == 0, second, first), segsend.shape)

    barrier = pltpu.get_barrier_semaphore()
    pl.semaphore_signal(barrier, inc=1, device_id={"blk": other}, device_id_type=MESH)
    pl.semaphore_wait(barrier, 1)

    def remote(i, src, dst):
        copy = pltpu.make_async_remote_copy(
            src_ref=src,
            dst_ref=dst,
            send_sem=send_sem.at[i],
            recv_sem=recv_sem.at[i],
            device_id={"blk": other},
            device_id_type=MESH,
        )
        copy.start()
        return copy

    part = half // 2
    far_seg = remote(2, segsend, segrow.at[:, pl.ds(mine, half)])
    far_x = [
        remote(
            c,
            x_in.at[other, pl.ds(c * part, part)],
            xs.at[pl.ds(pl.multiple_of(mine + c * part, part), part)],
        )
        for c in range(2)
    ]
    far_fv = remote(3, fv_in.at[other], vs.at[pl.ds(mine, half), pl.ds(val, val)])
    far_cot = remote(4, cot_in.at[other, pl.ds(0, part)], cot_out)

    own_row = jnp.broadcast_to(jnp.where(me == 0, first, second), (8, half))
    segrow[:, pl.ds(mine, half)] = own_row

    def project(start):
        rows = pl.ds(pl.multiple_of(start, QB), QB)
        xhat, _ = norm_parts(xs[rows, :].astype(F32))
        act1 = (xhat * row(g1_ref) + row(b1_ref)).astype(BF)
        act1ts[:, rows] = act1.T
        out = nn(act1, wqkv[...])
        query = (out[:, :width] + row(bq_ref)).astype(BF)
        qs[rows, :] = query * jnp.asarray(HEAD_DIM**-0.5, BF)
        ks[rows, :] = out[:, width : 2 * width].astype(BF)
        vs[rows, pl.ds(0, val)] = (out[:, 2 * width :] + row(bv_ref)).astype(BF)

    low = lax.broadcasted_iota(jnp.int32, (1, LANES), 1) < HEAD_DIM
    count = half // QB

    def at(start):
        return pl.ds(pl.multiple_of(start, QB), QB)

    def turn_segments(start):
        for c in range(half // LANES):
            place = pl.ds(pl.multiple_of(start + c * LANES, LANES), LANES)
            line = segrow[0:1, place].astype(F32)
            segcol[place, :] = jnp.broadcast_to(line, (LANES, LANES)).T

    def mask_block(key_start, query_start, diagonal):
        key = segcol[at(key_start), :]
        key = jnp.concatenate([key] * (QB // LANES), axis=1)
        query = segrow[0:1, at(query_start)].astype(F32)
        seen = (key == query) & (query >= 0.0)
        if diagonal:
            down = lax.broadcasted_iota(jnp.int32, (QB, QB), 0)
            across = lax.broadcasted_iota(jnp.int32, (QB, QB), 1)
            seen = (seen & (down <= across)) | (down == across)
        bias[at(key_start), at(query_start)] = jnp.where(seen, 0.0, NEG)

    def mask_half(start):
        turn_segments(start)
        for i in range(count):
            for j in range(i + 1):
                mask_block(start + j * QB, start + i * QB, i == j)

    def attend(p, items):
        cols = pl.ds(pl.multiple_of(p * LANES, LANES), LANES)
        done = {}

        def score(first, span, query, h, more):
            keys = pl.ds(pl.multiple_of(first, QB), span)
            q = qs[at(query), cols]
            q = jnp.where(low if h == 0 else ~low, q, jnp.zeros_like(q))
            return nt(ks[keys, cols], q) + bias[keys, at(query)]

        def finish(first, span, query, h, more, s):
            keys = pl.ds(pl.multiple_of(first, QB), span)
            rows = at(query)
            top = jnp.max(s, axis=0, keepdims=True)
            if more:
                before = lse_ref[p, h : h + 1, rows]
                top = jnp.maximum(top, before)
            e = jnp.exp(s - top)
            total = jnp.sum(e, axis=0, keepdims=True)
            if more:
                total = total + jnp.exp(before - top)
            log_total = top + jnp.log(total)
            lse_ref[p, h : h + 1, rows] = log_total
            lines = slice(h * HEAD_DIM, (h + 1) * HEAD_DIM)
            out = nn(turned[lines, keys], e.astype(BF)) * (1.0 / total)
            if more:
                out = out + held[p, lines, rows] * jnp.exp(before - log_total)
            held[p, lines, rows] = out
            done[h] = out.astype(BF)
            if h == 1:
                atts[rows, cols] = jnp.concatenate([done[0], done[1]], axis=0).T

        waiting = []
        for item in items:
            waiting.append(item + (score(*item),))
            if len(waiting) > 3:
                finish(*waiting.pop(0))
        for item in waiting:
            finish(*item)

    def half_items(start):
        return [
            (start, (i + 1) * QB, start + i * QB, h, False) for i in range(count) for h in range(2)
        ]

    cross_items = [
        (0, half, half + i * QB, h, True) for i in range(count) for h in range(2)
    ]

    own_x.wait()
    own_w.wait()
    for c in range(count):
        project(mine + c * QB)
    mask_half(mine)
    own_fv.wait()

    @pl.loop(0, PAIRS)
    def _(p):
        cols = pl.ds(pl.multiple_of(p * LANES, LANES), LANES)
        turned[:, pl.ds(mine, half)] = vs[pl.ds(mine, half), cols].T
        attend(p, half_items(mine))

    far_seg.wait()
    mask_half(theirs)
    for i in range(count):
        for j in range(count):
            mask_block(j * QB, half + i * QB, False)

    for c in range(2):
        far_x[c].wait()
        project(theirs + c * part)

    outs = []

    def local_out(src, dst):
        copy = pltpu.make_async_copy(src, dst, out_sem.at[len(outs)])
        copy.start()
        outs.append(copy)

    local_out(act1ts, act1t_out)
    local_out(xs, x_out)
    local_out(qs, q_out)
    local_out(ks, k_out)

    for j in range(steps):
        cut = (pl.ds(j * QB, QB), pl.ds(j * QB, tokens - j * QB))
        local_out(bias.at[cut], bias_out.at[cut])

    @pl.loop(0, PAIRS)
    def _(p):
        @pl.when(p == PAIRS // 2)
        def _():
            far_fv.wait()

        cols = pl.ds(pl.multiple_of(p * LANES, LANES), LANES)
        turned[...] = vs[:, cols].T
        attend(p, half_items(theirs) + cross_items)

    local_out(atts, att_out)
    local_out(vs, v_out)
    own_wo.wait()
    for c in range(steps):
        rows = slice(c * QB, (c + 1) * QB)
        middle = xs[rows, :].astype(F32) + nn(atts[rows, :], wout[...]) + row(bout_ref)
        mids[rows, :] = middle
        xhat, _ = norm_parts(middle)
        act2s[rows, :] = (xhat * row(g2_ref) + row(b2_ref)).astype(BF)
        local_out(mids.at[rows, :], mid_out.at[rows, :])
        local_out(act2s.at[rows, :], act2_out.at[rows, :])
    for copy in outs:
        copy.wait()
    far_cot.wait()


def front(x, fv, seg, cot, g1, b1, wqkv, bq, bv, wout, bout, g2, b2):
    half, width, val = x.shape[1], x.shape[2], fv.shape[2]
    tokens = 2 * half
    hbm = pl.BlockSpec(memory_space=pl.ANY)
    vmem = pl.BlockSpec(memory_space=pltpu.VMEM)
    flat = jax.ShapeDtypeStruct((tokens, width), BF)
    shape = jax.ShapeDtypeStruct
    return pl.pallas_call(
        front_kernel,
        in_specs=[hbm, hbm, vmem, hbm, vmem, vmem, hbm, vmem, vmem, hbm, vmem, vmem, vmem],
        out_specs=[hbm] * 7 + [vmem] + [hbm] * 3,
        out_shape=[
            flat,
            flat,
            flat,
            flat,
            flat,
            flat,
            shape((tokens, width), F32),
            shape((PAIRS, 2, tokens), F32),
            shape((tokens, tokens), F32),
            shape((width, tokens), BF),
            shape((half // 2, width), BF),
        ],
        scratch_shapes=[
            pltpu.VMEM((tokens, width), BF),
            pltpu.VMEM((tokens, width), BF),
            pltpu.VMEM((tokens, width), BF),
            pltpu.VMEM((tokens, width), BF),
            pltpu.VMEM((tokens, width), BF),
            pltpu.VMEM((tokens, width), BF),
            pltpu.VMEM((tokens, width), F32),
            pltpu.VMEM((tokens, tokens), F32),
            pltpu.VMEM(wqkv.shape, BF),
            pltpu.VMEM(wout.shape, BF),
            pltpu.VMEM((8, tokens), jnp.int32),
            pltpu.VMEM((8, half), jnp.int32),
            pltpu.VMEM((tokens, LANES), F32),
            pltpu.VMEM((width, tokens), BF),
            pltpu.VMEM((LANES, tokens), BF),
            pltpu.VMEM((PAIRS, LANES, tokens), F32),
            pltpu.SemaphoreType.DMA((5,)),
            pltpu.SemaphoreType.DMA((8 + 3 * tokens // QB,)),
            pltpu.SemaphoreType.DMA((5,)),
            pltpu.SemaphoreType.DMA((5,)),
        ],
        compiler_params=pltpu.CompilerParams(
            collective_id=0, has_side_effects=True, vmem_limit_bytes=56 * MIB
        ),
        name="front",
    )(x, fv, seg, cot, g1, b1, wqkv, bq, bv, wout, bout, g2, b2)


def feed_kernel(
    act2,
    g2_ref,
    bproj_ref,
    bfc_ref,
    wfc,
    wproj,
    cot_in,
    cot_far,
    mid_in,
    att_in,
    wout_in,
    lout_out,
    gmid_out,
    gatt_out,
    dwout_out,
    f_out,
    f2_out,
    f3_out,
    p_out,
    dots,
    dbfc,
    small,
    cots,
    mids,
    atts,
    wout,
    acc,
    act2t,
    hid,
    slope,
    dpre,
    louts,
    gatts,
    dwouts,
    sel,
    bias,
    gf,
    gp,
    rf0,
    rp0,
    rfh,
    rp1,
    in_sem,
    out_sem,
    send_sem,
    recv_sem,
):
    t = pl.program_id(0)
    tiles = pl.num_programs(0) // 2
    tokens, width = act2.shape
    half = tokens // 2
    tile = dpre.shape[1]
    steps = tokens // QB
    count = gf.shape[0]
    _, core, x, _, _ = spot()
    me = lax.axis_index("blk")
    mine = pl.multiple_of(me * half, half)
    theirs = pl.multiple_of((1 - me) * half, half)
    both = partners()
    friends = [both[0], both[1], both[4]]
    side = pl.ds(pl.multiple_of(me * (tile // 2), tile // 2), tile // 2)

    def chain(held, got, dims, order, n):
        return Sum(held, got, dims, order, send_sem.at[n], recv_sem.at[n])

    full = ("far", "near", "x", "core")
    fcs = [chain(gf.at[n], [rf0.at[n], rfh.at[n]], full, ("core", "half"), n) for n in range(2)]
    fcs.append(chain(gf.at[2], [rf0.at[2]], full, ("core",), 2))
    projs = [chain(gp.at[n], [rp0.at[n], rp1.at[n]], full[2:], ("core", "x"), 3 + n) for n in range(4)]

    def load(n):
        src, dst = [
            (cot_in.at[me], cots.at[pl.ds(mine, half)]),
            (cot_far, cots.at[pl.ds(theirs, half // 2)]),
            (mid_in, mids),
            (att_in, atts),
            (wout_in, wout),
        ][n]
        return pltpu.make_async_copy(src, dst, in_sem.at[n])

    far_cot = push(
        cot_in.at[1 - me, pl.ds(half // 2, half // 2)],
        cots.at[pl.ds(pl.multiple_of(mine + half // 2, half // 2), half // 2)],
        send_sem.at[7, 0],
        recv_sem.at[7, 0],
        friends[2],
    )
    back = push(
        louts.at[pl.ds(theirs, half)], lout_out.at[me], send_sem.at[7, 1], recv_sem.at[7, 1], friends[2]
    )

    stores = [
        (louts.at[pl.ds(mine, half)], lout_out.at[me]),
        (acc, gmid_out),
        (gatts, gatt_out),
        (dwouts, dwout_out),
        (gf.at[3], f3_out),
    ]
    size = tile // 2
    stores += [
        (gf.at[n, :, :, :, core, :, side], f_out.at[:, :, :, :, n * size : (n + 1) * size]) for n in range(2)
    ]
    stores.append((gf.at[2, :, :, :, core], f2_out))
    stores += [(gp.at[n, x, core], p_out.at[n // 2, n % 2]) for n in range(4)]

    def store(n):
        return pltpu.make_async_copy(stores[n][0], stores[n][1], out_sem.at[n])

    def at_step(k, *actions):
        @pl.when(t == k)
        def _():
            for action in actions:
                action()

    @pl.when(t == 0)
    def _():
        for n in range(5):
            load(n).start()
        greet(friends)
        act2t[...] = act2[...].T
        for n in range(count):
            bias[n] = row(bfc_ref)[:, n * tile : (n + 1) * tile]
        acc[...] = jnp.zeros_like(acc)
        head = lax.broadcasted_iota(jnp.int32, sel.shape, 0)
        feature = lax.broadcasted_iota(jnp.int32, sel.shape, 1)
        inside = (feature >= head * HEAD_DIM) & (feature < (head + 1) * HEAD_DIM)
        sel[...] = jnp.where(inside, 1.0, 0.0).astype(BF)

    @pl.when(t < tiles)
    def _():
        for c in range(steps):
            rows = slice(c * QB, (c + 1) * QB)
            u = nn(act2[rows, :], wfc[...]) + bias[t]
            square = u * u
            bend = jnp.tanh(u * (0.7978845608028654 + (0.7978845608028654 * 0.044715) * square))
            halfway = 0.5 + 0.5 * bend
            hidden = (u * halfway).astype(BF)
            hid[t, rows, :] = hidden
            slope[t, rows, :] = (
                halfway
                + (u * (0.5 - 0.5 * bend * bend))
                * (0.7978845608028654 + (3 * 0.7978845608028654 * 0.044715) * square)
            ).astype(BF)
            acc[rows, :] += nn(hidden, wproj[...])

    @pl.when(t == 0)
    def _():
        meet(friends)
        far_cot.start()

    @pl.when(t == tiles - 1)
    def _():
        load(2).wait()
        for c in range(steps):
            rows = slice(c * QB, (c + 1) * QB)
            louts[rows, :] = (mids[rows, :] + acc[rows, :] + row(bproj_ref)).astype(BF)
        back.start()
        store(0).start()
        acc[...] = jnp.zeros_like(acc)
        load(0).wait()
        load(1).wait()
        far_cot.wait()

    @pl.when(t >= tiles)
    def _():
        n = t - tiles
        total = None
        for c in range(steps):
            rows = slice(c * QB, (c + 1) * QB)
            grad = (nt(cots[rows, :], wproj[...]) * slope[n, rows, :].astype(F32)).astype(BF)
            dpre[rows, :] = grad
            acc[rows, :] += nt(grad, wfc[...])
            part = column_sum(grad.astype(F32))
            total = part if total is None else total + part
            if c == 2:
                for k in range(3):
                    at_step(tiles + k + 1, lambda k=k: projs[k].take(0), lambda k=k: fcs[k].take(0))
        dbfc[...] = total
        gp[n] = tn(hid[n], cots[...]).astype(BF).reshape(gp.shape[1:])
        gf[n] = nn(act2t[...], dpre[...]).astype(BF).reshape(gf.shape[1:])

    for k in range(3):
        at_step(tiles + k, lambda k=k: projs[k].start(0), lambda k=k: fcs[k].start(0))
    at_step(tiles + 3, lambda: projs[3].start(0))

    @pl.when(t == 2 * tiles - 1)
    def _():
        store(4).start()
        store(7).start()
        load(3).wait()
        load(4).wait()
        projs[0].take(1)
        store(8).start()
        gain = row(g2_ref)
        sums = [None] * 4
        for c in range(steps):
            rows = slice(c * QB, (c + 1) * QB)
            middle = mids[rows, :]
            upstream = cots[rows, :].astype(F32)
            xhat, inverse = norm_parts(middle)
            da = acc[rows, :]
            grad_middle = upstream + norm_pull(da, xhat, inverse, gain)
            acc[rows, :] = grad_middle
            branch = grad_middle.astype(BF)
            dpre[rows, :] = branch
            parts = [
                column_sum(upstream),
                column_sum(da * xhat),
                column_sum(da),
                column_sum(branch.astype(F32)),
            ]
            sums = [b if a is None else a + b for a, b in zip(sums, parts)]
            ga = nt(branch, wout[...]).astype(BF)
            gatts[rows, :] = ga
            product = ga.astype(F32) * atts[rows, :].astype(F32)
            big = product.astype(BF)
            rest = (product - big.astype(F32)).astype(BF)
            dot = nt(sel[...], big) + nt(sel[...], rest)
            for p in range(PAIRS):
                dots[p, :, rows] = dot[2 * p : 2 * p + 2, :]
            if c == 1:
                projs[3].take(0)
        store(1).start()
        store(2).start()
        small[...] = jnp.concatenate(sums, axis=0)
        dwouts[...] = tn(atts[...], dpre[...]).astype(BF).reshape(dwouts.shape)
        store(3).start()
        projs[1].take(1)
        store(9).start()
        fcs[0].take(1)
        store(5).start()
        projs[2].take(1)
        store(10).start()
        fcs[1].take(1)
        store(6).start()
        projs[3].take(1)
        store(11).start()
        for n in range(len(stores)):
            store(n).wait()
        back.wait()


def feed(act2, cotangent, cot_far, mid, att, g2, bproj, wout, wfc, bfc, wproj):
    tokens, width = act2.shape
    half = tokens // 2
    ff = wfc.shape[1]
    tiles = 4
    tile = ff // tiles
    owner = width // 16
    owner_ff = ff // 16
    shape = jax.ShapeDtypeStruct
    flat = shape((tokens, width), BF)
    once = pl.Buffered(1)
    hbm = pl.BlockSpec(memory_space=pl.ANY)

    def whole(s):
        return pl.BlockSpec(s, lambda t: (0,) * len(s), pipeline_mode=once)

    def vm(*s):
        return pltpu.VMEM(s, BF)

    line = whole((width,))
    return pl.pallas_call(
        feed_kernel,
        grid=(2 * tiles,),
        in_specs=[
            whole((tokens, width)),
            line,
            line,
            whole((ff,)),
            pl.BlockSpec((width, tile), lambda t: (0, lax.rem(t, tiles))),
            pl.BlockSpec((tile, width), lambda t: (lax.rem(t, tiles), 0)),
        ]
        + [hbm] * 5,
        out_specs=[hbm] * 8
        + [
            whole((PAIRS, 2, tokens)),
            pl.BlockSpec((1, tile), lambda t: (0, jnp.maximum(t - tiles, 0))),
            whole((4, width)),
        ],
        out_shape=[
            shape((2, half, width), BF),
            shape((tokens, width), F32),
            flat,
            shape((2, 2, 2, 2, owner, width), BF),
            shape((2, 2, 2, owner, tile), BF),
            shape((2, 2, 2, owner, tile), BF),
            shape((2, 2, 2, 2, owner, tile), BF),
            shape((2, 2, owner_ff, width), BF),
            shape((PAIRS, 2, tokens), F32),
            shape((1, ff), F32),
            shape((4, width), F32),
        ],
        scratch_shapes=[
            vm(tokens, width),
            pltpu.VMEM((tokens, width), F32),
            vm(tokens, width),
            vm(width, width),
            pltpu.VMEM((tokens, width), F32),
            vm(width, tokens),
            vm(tiles, tokens, tile),
            vm(tiles, tokens, tile),
            vm(tokens, tile),
            vm(tokens, width),
            vm(tokens, width),
            vm(2, 2, 2, 2, owner, width),
            vm(16, width),
            pltpu.VMEM((tiles, 1, tile), F32),
            vm(tiles, 2, 2, 2, 2, owner, tile),
            vm(tiles, 2, 2, owner_ff, width),
            vm(3, 2, 2, 2, owner, tile),
            vm(4, 2, owner_ff, width),
            vm(2, 2, 2, 2, owner, tile // 2),
            vm(4, owner_ff, width),
            pltpu.SemaphoreType.DMA((5,)),
            pltpu.SemaphoreType.DMA((12,)),
            pltpu.SemaphoreType.DMA((8, 2)),
            pltpu.SemaphoreType.DMA((8, 2)),
        ],
        compiler_params=pltpu.CompilerParams(
            collective_id=1, has_side_effects=True, vmem_limit_bytes=62 * MIB
        ),
        name="feed",
    )(act2, g2, bproj, bfc, wfc, wproj, cotangent, cot_far, mid, att, wout)


FIRST_PAIR = PAIRS // 2


def pieces(width, val):
    lanes = LANES
    return [
        (3, [(3 * lanes, 3 * lanes), (width + 3 * lanes, 3 * lanes)]),
        (5, [(0, 2 * lanes), (width, 2 * lanes), (2 * width, 2 * lanes)]),
        (6, [(2 * lanes, lanes), (width + 2 * lanes, lanes), (2 * width + 2 * lanes, lanes)]),
    ]


def tail_kernel(
    q_in,
    k_in,
    v_in,
    do_in,
    bias_in,
    x_in,
    act1t_in,
    gmid_in,
    wqkv_in,
    dwout_in,
    f_in,
    f2_in,
    f3_in,
    p_in,
    lse_ref,
    d_ref,
    g1_ref,
    dbfc_ref,
    small_in,
    gx_out,
    gf_out,
    wqkv_out,
    wout_out,
    wfc_out,
    wproj_out,
    small_out,
    q_ref,
    k_ref,
    v_ref,
    do_ref,
    bias,
    xs,
    gmid,
    wqkv,
    dqk,
    dvs,
    gfs,
    dqa,
    act1t,
    gx,
    g_out,
    g_f,
    g_f2,
    g_f3,
    g_p,
    g_q,
    r_out,
    r_f,
    r_f2,
    r_f3,
    r_p,
    r_q,
    last_sum,
    r_z,
    r_last,
    sums,
    s_got,
    late,
    l_got,
    w_fc,
    w_proj,
    w_out,
    in_sem,
    out_sem,
    back_send,
    back_recv,
    sum_send,
    sum_recv,
    far_send,
    far_recv,
):
    tokens, width = q_ref.shape
    half = tokens // 2
    val = gfs.shape[1]
    steps = tokens // QB
    me = lax.axis_index("blk")
    mine = pl.multiple_of(me * half, half)
    theirs = pl.multiple_of((1 - me) * half, half)
    _, core, x, near, far = spot()
    friends = partners()
    parts = pieces(width, val)

    sources = {
        "f3": (f3_in, g_f3),
        "out": (dwout_in, g_out),
        "p": (p_in, g_p),
        "f": (f_in, g_f),
        "f2": (f2_in, g_f2),
        "q": (q_in, q_ref),
        "k": (k_in, k_ref),
        "bias": (bias_in, bias),
        "v": (v_in, v_ref),
        "do": (do_in, do_ref),
        "act1t": (act1t_in, act1t),
        "x": (x_in, xs),
        "wqkv": (wqkv_in, wqkv),
        "gmid": (gmid_in, gmid),
    }
    loads = {
        name: pltpu.make_async_copy(src, dst, in_sem.at[n])
        for n, (name, (src, dst)) in enumerate(sources.items())
    }
    for load in loads.values():
        load.start()
    everyone = [flipped(flip)[1] for flip in FLIPS] + [friends[0], friends[4]]
    greet(everyone)
    meet(everyone)

    full = ("far", "near", "x", "core")
    down = ("core", "x", "near", "far", "pair")
    sems = iter(range(16))

    def chain(held, got, dims, order, cut_columns=True):
        n = next(sems)
        return Sum(held, got, dims, order, sum_send.at[n], sum_recv.at[n], cut_columns)

    s_out = chain(g_out, r_out, full, down)
    s_f = chain(g_f, r_f, full[:3], ("x", "near", "far", "gather"), False)
    s_f2 = chain(g_f2, r_f2, full[:3], ("half", "x", "near", "far", "gather"))
    s_f3 = chain(g_f3, r_f3, full, ("core", "half", "x", "near", "far", "gather"))
    s_p = chain(g_p, r_p, full[:2], ("half", "near", "far", "gather"))
    s_q = [chain(g, r, full, down if n < 2 else down[:2]) for n, (g, r) in enumerate(zip(g_q, r_q))]
    n_small, n_last, n_late = next(sems), next(sems), next(sems)

    def vectors(held, got, place, n):
        return Vectors(held, got, place, (sum_send.at[n], sum_recv.at[n]), (far_send, far_recv))

    s_small = vectors(sums, s_got, 0, n_small)
    s_late = vectors(late, l_got, 1, n_late)

    def z_copies():
        found = []
        for n, flip in enumerate([flip for flip in FLIPS if flip[2] == 0]):
            place, friend = flipped(flip)
            src = g_q[2].at[place]
            found.append(push(src, r_z.at[n], far_send.at[2, n], far_recv.at[2, n], friend))
        return found

    def last_x():
        s_q[2].take(1)
        for copy in z_copies():
            copy.start()

    def last_z():
        for copy in z_copies():
            copy.wait()
        total = g_q[2][far, near, x, core].astype(F32)
        for n in range(3):
            total = total + r_z[n].astype(F32)
        last_sum[...] = total.astype(BF)
        last_copy.start()

    last_copy = push(
        last_sum, r_last, sum_send.at[n_last, 0], sum_recv.at[n_last, 0], friends[4]
    )

    def give_back(n, src, dst):
        return push(src, dst, back_send.at[n], back_recv.at[n], friends[4])

    for n in range(4):
        sums[0, n : n + 1, :] = small_in[n : n + 1, :]
        sums[0, 4 + n : 5 + n, :] = dbfc_ref[:, n * width : (n + 1) * width]
    s_small.start(0)
    for name, begin in (("f3", s_f3), ("p", s_p), ("f", s_f), ("f2", s_f2), ("out", s_out)):
        loads[name].wait()
        begin.start(0)
    for name in ("q", "k", "bias", "v", "do"):
        loads[name].wait()

    low = lax.broadcasted_iota(jnp.int32, (1, LANES), 1) < HEAD_DIM
    masks = [low, ~low]
    zero = jnp.zeros((), BF)
    gain = row(g1_ref)

    def columns(at, size):
        return dqk[:, at : at + size] if at < 2 * width else dvs[:, at - 2 * width : at - 2 * width + size]

    def project_grad(n):
        at = 0
        for start, size in parts[n][1]:
            block = nn(act1t[...], columns(start, size)).astype(BF)
            g_q[n][:, :, :, :, :, at : at + size] = block.reshape(g_q[n].shape[:-1] + (size,))
            at += size
        s_q[n].start(0)

    back_gf = give_back(1, gfs.at[pl.ds(theirs, half)], gf_out.at[me])
    keep_gf = pltpu.make_async_copy(gfs.at[pl.ds(mine, half)], gf_out.at[me], out_sem.at[1])

    def take(name, stage):
        return lambda: names[name].take(stage)

    names = {"sm": s_small, "f3": s_f3, "out": s_out, "f": s_f, "p": s_p, "f2": s_f2}
    names.update({"q0": s_q[0], "q1": s_q[1]})
    plan = {
        (0, 0): [take("sm", 0), take("f3", 0), take("out", 0)],
        (1, 1): [take("f", 0)],
        (2, 1): [take("p", 0), take("sm", 1), loads["act1t"].wait],
        (3, 0): [take("f", 1), lambda: project_grad(0), back_gf.start, keep_gf.start],
        (3, 1): [take("q0", 0), take("f2", 0), take("out", 1)],
        (4, 0): [take("p", 1)],
        (4, 1): [take("f3", 1), take("f", 2), take("sm", 2)],
        (5, 0): [take("q0", 1), take("out", 2), lambda: project_grad(1)],
        (5, 1): [take("q1", 0), take("f2", 1), take("p", 2)],
    }

    def act(step, middle):
        for (k, when), actions in plan.items():
            if when == middle:

                @pl.when(step == k)
                def _():
                    for action in actions:
                        action()

    @pl.loop(0, PAIRS)
    def _(step):
        act(step, 0)
        p = lax.rem(step + FIRST_PAIR, PAIRS)
        cols = pl.ds(pl.multiple_of(p * LANES, LANES), LANES)
        kcols = pl.ds(pl.multiple_of(width + p * LANES, LANES), LANES)
        q, k, v, do = q_ref[:, cols], k_ref[:, cols], v_ref[:, cols], do_ref[:, cols]
        qm = [jnp.where(m, q, zero) for m in masks]
        km = [jnp.where(m, k, zero) for m in masks]
        dom = [jnp.where(m, do, zero) for m in masks]
        dvals = []
        for j in range(steps):
            a = j * QB
            keys = slice(a, a + QB)
            dk = dv = dq = None
            for h in range(2):
                s = nt(k[keys], qm[h][a:]) + bias[keys, a:]
                probs = jnp.exp(s - lse_ref[p, h : h + 1, a:])
                dp = nt(v[keys], dom[h][a:])
                ds = (probs * (dp - d_ref[p, h : h + 1, a:])).astype(BF)
                dvh = nn(probs.astype(BF), dom[h][a:])
                dkh = nn(ds, qm[h][a:])
                dqh = tn(ds, km[h][keys])
                dk = dkh if dk is None else dk + dkh
                dv = dvh if dv is None else dv + dvh
                dq = dqh if dq is None else dq + dqh
            dqk[keys, kcols] = dk.astype(BF)
            dvals.append(dv.astype(BF))
            if j == 0:
                act(step, 1)
            if j == 0:
                dqa[...] = dq
            else:
                dqa[a:, :] += dq
        dqk[:, cols] = (dqa[...] * HEAD_DIM**-0.5).astype(BF)

        @pl.when(p < PAIRS // 2)
        def _():
            for j in range(steps):
                dvs[j * QB : (j + 1) * QB, cols] = dvals[j]

        @pl.when(p >= PAIRS // 2)
        def _():
            late = pl.ds(pl.multiple_of(p * LANES - val, LANES), LANES)
            for j in range(steps):
                gfs[j * QB : (j + 1) * QB, late] = dvals[j]

    for name in ("x", "wqkv", "gmid"):
        loads[name].wait()

    totals = [None] * 4

    def input_grad(start, size):
        rows = pl.ds(pl.multiple_of(start, size), size)
        da = nt(dqk[rows, :], wqkv[:, : 2 * width]) + nt(dvs[rows, :], wqkv[:, 2 * width :])
        xhat, inverse = norm_parts(xs[rows, :].astype(F32))
        gx[rows, :] = (gmid[rows, :] + norm_pull(da, xhat, inverse, gain)).astype(BF)
        bv = column_sum(dvs[rows, :].astype(F32))
        found = [
            column_sum(da * xhat),
            column_sum(da),
            column_sum(dqk[rows, :width].astype(F32)),
            jnp.concatenate([bv, jnp.zeros((1, width - val), F32)], axis=1),
        ]
        totals[:] = [b if a is None else a + b for a, b in zip(totals, found)]

    backs = []

    def give_rows(at, size):
        start = pl.multiple_of(theirs + at, size)
        input_grad(start, size)
        copy = give_back(2 + len(backs), gx.at[pl.ds(start, size)], gx_out.at[me, pl.ds(at, size)])
        copy.start()
        backs.append(copy)

    s_q[0].take(2)
    s_f3.take(2)
    give_rows(0, LANES)
    project_grad(2)
    s_out.take(3)
    give_rows(LANES, LANES)
    s_f2.take(2)
    s_q[2].take(0)
    give_rows(QB, LANES)
    s_q[1].take(1)
    s_q[0].take(3)
    give_rows(QB + LANES, LANES)
    s_f3.take(3)
    input_grad(mine, LANES)
    s_f2.take(3)
    input_grad(mine + LANES, LANES)
    last_x()
    input_grad(mine + QB, LANES)
    s_q[1].take(2)
    input_grad(mine + QB + LANES, LANES)
    keep_gx = pltpu.make_async_copy(gx.at[pl.ds(mine, half)], gx_out.at[me], out_sem.at[2])
    keep_gx.start()
    late[0] = jnp.concatenate(totals, axis=0)
    s_late.start(0)
    s_late.take(0)
    s_f3.take(4)
    last_z()
    s_q[1].take(3)
    s_late.take(1)

    def write(n, src, dst):
        copy = pltpu.make_async_copy(src, dst, out_sem.at[3 + n])
        copy.start()
        return copy

    side = width // 2
    for part, who in zip(s_p.last(), (me, 1 - me)):
        w_proj[:, pl.ds(pl.multiple_of(who * side, side), side)] = part
    writes = [write(0, w_proj, wproj_out)]
    tile = g_f3.shape[-1]
    side = tile // 2
    for sum_, tiles in ((s_f, (0, 1)), (s_f2, (2,)), (s_f3, (3,))):
        for part, who in zip(sum_.last(), (me, 1 - me)):
            for n, t in enumerate(tiles):
                at = pl.ds(pl.multiple_of(t * tile + who * side, side), side)
                w_fc[:, at] = part[:, n * side : (n + 1) * side]
    writes.append(write(1, w_fc, wfc_out))
    own, came = s_out.last()
    w_out[...] = own + came
    writes.append(write(2, w_out, wout_out))
    last_copy.wait()
    for n in range(3):
        if n < 2:
            own, came = s_q[n].last()
        else:
            own, came = last_sum[...].astype(F32), r_last[...].astype(F32)
        part = own + came
        at = 0
        for start, size in parts[n][1]:
            wqkv_out[:, start : start + size] = part[:, at : at + size]
            at += size
    s_late.take(2)
    small_out[...] = jnp.concatenate(
        [sums[3, 0:4, :], late[3], sums[3, 4:8, :], jnp.zeros((4, width), F32)], axis=0
    )
    back_gf.wait()
    for copy in backs:
        copy.wait()
    for copy in writes:
        copy.wait()
    keep_gf.wait()
    keep_gx.wait()


def tail(
    q, k, v, do, bias, x, act1t, gmid, wqkv, dwout, f, f2, f3, p, lse, dots, g1, dbfc, small
):
    tokens, width = q.shape
    half = tokens // 2
    val = wqkv.shape[1] - 2 * width
    owner = width // 16
    owner_ff = dbfc.shape[1] // 16
    ff = dbfc.shape[1]
    tile = f3.shape[-1]
    shape = jax.ShapeDtypeStruct
    hbm = pl.BlockSpec(memory_space=pl.ANY)
    vmem = pl.BlockSpec(memory_space=pltpu.VMEM)

    def vm(*s):
        return pltpu.VMEM(s, BF)

    def chain(rows, cols):
        return [
            vm(2, 2, 2, rows, cols),
            vm(2, 2, rows, cols),
            vm(2, rows, cols),
            vm(rows, cols),
            vm(rows, cols),
        ]

    def cut_chain(rows, cols):
        side = chain(rows, cols // 2)
        return [vm(2, 2, 2, rows, cols)] + side[:1] + side[1:4] + side[3:4]

    flat = vm(tokens, width)
    sizes = [sum(size for _, size in columns) for _, columns in pieces(width, val)]
    return pl.pallas_call(
        tail_kernel,
        in_specs=[hbm] * 14 + [vmem] * 5,
        out_specs=[hbm] * 2 + [vmem] + [hbm] * 3 + [vmem],
        out_shape=[
            shape((2, half, width), BF),
            shape((2, half, val), BF),
            shape((owner, wqkv.shape[1]), F32),
            shape((owner, width), F32),
            shape((owner, ff), F32),
            shape((owner_ff, width), F32),
            shape((16, width), F32),
        ],
        scratch_shapes=[
            flat,
            flat,
            flat,
            flat,
            pltpu.VMEM((tokens, tokens), F32),
            flat,
            pltpu.VMEM((tokens, width), F32),
            vm(*wqkv.shape),
            vm(tokens, 2 * width),
            vm(tokens, val),
            vm(tokens, val),
            pltpu.VMEM((tokens, LANES), F32),
            vm(width, tokens),
            flat,
            vm(*dwout.shape),
            vm(*f.shape),
            vm(*f2.shape),
            vm(*f3.shape),
            vm(*p.shape),
            [vm(2, 2, 2, 2, owner, size) for size in sizes],
            chain(owner, width),
            chain(owner, f.shape[-1])[1:],
            cut_chain(owner, tile)[1:],
            cut_chain(owner, tile),
            [vm(2, 2, owner_ff, width // 2)] + cut_chain(owner_ff, width)[3:],
            [chain(owner, size) for size in sizes[:2]] + [chain(owner, sizes[2])[:2]],
            vm(owner, sizes[2]),
            vm(3, owner, sizes[2]),
            vm(owner, sizes[2]),
            pltpu.VMEM((4, 8, width), F32),
            [pltpu.VMEM(n + (8, width), F32) for n in ((), (len(FLIPS),), ())],
            pltpu.VMEM((4, 4, width), F32),
            [pltpu.VMEM(n + (4, width), F32) for n in ((), (len(FLIPS),), ())],
            pltpu.VMEM((owner, ff), F32),
            pltpu.VMEM((owner_ff, width), F32),
            pltpu.VMEM((owner, width), F32),
            pltpu.SemaphoreType.DMA((14,)),
            pltpu.SemaphoreType.DMA((6,)),
            pltpu.SemaphoreType.DMA((6,)),
            pltpu.SemaphoreType.DMA((6,)),
            pltpu.SemaphoreType.DMA((11, 6)),
            pltpu.SemaphoreType.DMA((11, 6)),
            pltpu.SemaphoreType.DMA((3, len(FLIPS))),
            pltpu.SemaphoreType.DMA((3, len(FLIPS))),
        ],
        compiler_params=pltpu.CompilerParams(
            collective_id=2, has_side_effects=True, vmem_limit_bytes=62 * MIB
        ),
        name="tail",
    )(q, k, v, do, bias, x, act1t, gmid, wqkv, dwout, f, f2, f3, p, lse, dots, g1, dbfc, small)


def finish_kernel(*refs):
    wide_in, sums = refs[:7], refs[7]
    wide_out, small_out, held, sem = refs[8:15], refs[15:24], refs[24], refs[25]
    loads = [pltpu.make_async_copy(src, dst, sem.at[0, n]) for n, (src, dst) in enumerate(zip(wide_in, held))]
    stores = [pltpu.make_async_copy(src, dst, sem.at[1, n]) for n, (src, dst) in enumerate(zip(held, wide_out))]
    for load in loads:
        load.start()
    b = lax.axis_index("batch")
    rows = sums[0:8, :]
    width = rows.shape[1]
    long = jnp.concatenate([sums[8 + n : 9 + n, :] for n in range(4)], axis=1)
    long = jnp.broadcast_to(long, (8, 4 * width))
    for at, ref in zip((4, 5, 6, 7, 3, 1, 2, None, 0), small_out):
        size = ref.shape[0]
        source = long if at is None else rows
        line = 0 if at is None else at
        length = source.shape[1]
        turned = pltpu.roll(source, lax.rem(length - b * size, length), 1)
        ref[...] = turned[line, :size]
    for load, store in zip(loads, stores):
        load.wait()
        store.start()
    for store in stores:
        store.wait()


def finish(wide, sums, sizes):
    hbm = pl.BlockSpec(memory_space=pl.ANY)
    vmem = pl.BlockSpec(memory_space=pltpu.VMEM)
    shape = jax.ShapeDtypeStruct
    return pl.pallas_call(
        finish_kernel,
        in_specs=[hbm] * 7 + [vmem],
        out_specs=[hbm] * 7 + [vmem] * 9,
        out_shape=[shape(a.shape, a.dtype) for a in wide] + [shape((n,), F32) for n in sizes],
        scratch_shapes=[
            [pltpu.VMEM(a.shape, a.dtype) for a in wide],
            pltpu.SemaphoreType.DMA((2, 7)),
        ],
        compiler_params=pltpu.CompilerParams(vmem_limit_bytes=60 * MIB),
        name="finish",
    )(*wide, sums)


def paired(
    inputs,
    first_values,
    segments,
    ln1_gain,
    first_norm_bias,
    w_qkv,
    b_query,
    b_value,
    w_out,
    b_out,
    ln2_gain,
    second_norm_bias,
    w_fc,
    b_fc,
    w_proj,
    b_proj,
    cotangent,
):
    half, width = inputs.shape[1], inputs.shape[2]
    val = first_values.shape[2]
    x, q, k, v, att, act2, mid, lse, bias, act1t, cot_far = front(
        inputs,
        first_values,
        segments,
        cotangent,
        ln1_gain,
        first_norm_bias,
        w_qkv,
        b_query,
        b_value,
        w_out,
        b_out,
        ln2_gain,
        second_norm_bias,
    )
    layer_out, gmid, gatt, dwout, f, f2, f3, p, dots, dbfc, small = feed(
        act2, cotangent, cot_far, mid, att, ln2_gain, b_proj, w_out, w_fc, b_fc, w_proj
    )
    owner = width // 16
    *wide, sums = tail(
        q,
        k,
        v,
        gatt,
        bias,
        x,
        act1t,
        gmid,
        w_qkv,
        dwout,
        f,
        f2,
        f3,
        p,
        lse,
        dots,
        ln1_gain,
        dbfc,
        small,
    )
    sizes = [owner, owner, owner, val // 16, owner, owner, owner, w_fc.shape[1] // 16, owner]
    out = finish([layer_out] + wide, sums, sizes)
    layer_out, grad_inputs, grad_first, gwqkv, gwout, gwfc, gwproj = out[:7]
    g1, b1, bq, bv, bo, g2, b2, bf, bp = out[7:]
    return (
        layer_out,
        grad_inputs,
        grad_first,
        g1,
        b1,
        gwqkv,
        bq,
        bv,
        gwout,
        bo,
        g2,
        b2,
        gwfc,
        bf,
        gwproj,
        bp,
    )


MICRO = 2


def as_sent(shard):
    return jax.tree.map(lambda a: a.astype(jnp.bfloat16) if a.dtype == jnp.float32 else a, shard)


def apply_norm(values_in, norm_gain, shift_bias):
    mean_val = jnp.mean(values_in, axis=-1, keepdims=True)
    centred_rows = values_in - mean_val
    inverse_deviation = lax.rsqrt(
        jnp.mean(centred_rows * centred_rows, axis=-1, keepdims=True) + EPS
    )
    standardized = centred_rows * inverse_deviation
    return (standardized * norm_gain + shift_bias, standardized, inverse_deviation)


def apply_norm_backward(upstream_gradient, standardized, inverse_deviation, norm_gain):
    scaled_rows = upstream_gradient * norm_gain
    first_average = jnp.mean(scaled_rows, axis=-1, keepdims=True)
    second_average = jnp.mean(scaled_rows * standardized, axis=-1, keepdims=True)
    incoming_gradient = inverse_deviation * (
        scaled_rows - first_average - standardized * second_average
    )
    return (
        incoming_gradient,
        jnp.sum(upstream_gradient * standardized, axis=(0, 1)),
        jnp.sum(upstream_gradient, axis=(0, 1)),
    )


def gelu_tanh(values_in):
    cubic = values_in + 0.044715 * values_in * values_in * values_in
    return 0.5 * values_in * (1.0 + jnp.tanh(0.7978845608028654 * cubic))


def heads_of(values_in):
    return values_in.reshape(values_in.shape[0], values_in.shape[1], HEADS, HEAD_DIM)


def visible(seg_query, seg_key, query_pos, key_pos):
    same = seg_query[:, :, None] == seg_key[:, None, :]
    causal = key_pos[None, :] <= query_pos[:, None]
    live = seg_query[:, :, None] >= 0
    diagonal = key_pos[None, :] == query_pos[:, None]
    return (same & causal[None] & live | diagonal[None])[:, :, None, :]


def score_block(query4, key4, mask):
    raw = jnp.einsum("rqhd,rkhd->rqhk", query4, key4, preferred_element_type=jnp.float32)
    return jnp.where(mask, raw * HEAD_DIM ** (-0.5), NEG)


def grad_block(query4, key4, value4, dout4, log_total, out_dot, mask):
    probs = jnp.where(mask, jnp.exp(score_block(query4, key4, mask) - log_total[..., None]), 0.0)
    probs_low = probs.astype(jnp.bfloat16)
    grad_probs = jnp.einsum("rqhd,rkhd->rqhk", dout4, value4, preferred_element_type=jnp.float32)
    grad_scores = (probs * (grad_probs - out_dot[..., None]) * HEAD_DIM ** (-0.5)).astype(
        jnp.bfloat16
    )
    return (probs_low, grad_scores)


def spread(
    inputs,
    first_values,
    segments,
    ln1_gain,
    first_norm_bias,
    w_qkv,
    b_query,
    b_value,
    w_out,
    b_out,
    ln2_gain,
    second_norm_bias,
    w_fc,
    b_fc,
    w_proj,
    b_proj,
    cotangent,
):
    all_seg = lax.all_gather(segments, "blk", axis=1, tiled=True)
    block_len = inputs.shape[1]
    model_width = inputs.shape[2]
    val_width = first_values.shape[2]
    rows_mb = inputs.shape[0] // MICRO
    own_pos = lax.axis_index("blk") * block_len + jnp.arange(block_len)
    first_gain = ln1_gain.astype(jnp.float32)
    second_gain = ln2_gain.astype(jnp.float32)
    outputs = []
    input_grads = []
    first_grads = []
    totals = None
    for micro_step in range(MICRO):
        first_row = micro_step * rows_mb
        last_row = first_row + rows_mb
        residual_stream = inputs[first_row:last_row].astype(jnp.float32)
        first_part = first_values[first_row:last_row]
        seg_local = segments[first_row:last_row]
        seg_row = all_seg[first_row:last_row]
        cot_part = cotangent[first_row:last_row]
        first_normed_rows, first_standardized, first_inverse_deviation = apply_norm(
            residual_stream, first_gain, first_norm_bias.astype(jnp.float32)
        )
        act1 = first_normed_rows.astype(jnp.bfloat16)
        projected = jnp.einsum("rbd,de->rbe", act1, w_qkv, preferred_element_type=jnp.float32)
        queries = (projected[..., :model_width] + b_query.astype(jnp.float32)).astype(jnp.bfloat16)
        keys_low = projected[..., model_width : 2 * model_width].astype(jnp.bfloat16)
        fresh = (projected[..., 2 * model_width :] + b_value.astype(jnp.float32)).astype(
            jnp.bfloat16
        )
        values_low = jnp.concatenate([fresh, first_part], axis=-1)
        query4 = heads_of(queries)
        key_part = lax.all_gather(keys_low, "blk", axis=1, tiled=True)
        value_part = lax.all_gather(values_low, "blk", axis=1, tiled=True)
        span = key_part.shape[1]
        key_pos = jnp.arange(span)
        mask = visible(seg_local, seg_row, own_pos, key_pos)
        scores = score_block(query4, heads_of(key_part), mask)
        old_max = jnp.full((rows_mb, block_len, HEADS), NEG, jnp.float32)
        new_max = jnp.maximum(old_max, jnp.max(scores, axis=-1))
        weights = jnp.where(mask, jnp.exp(scores - new_max[..., None]), 0.0)
        new_sum = jnp.sum(weights, axis=-1)
        new_acc = jnp.einsum(
            "rqhk,rkhd->rqhd",
            weights.astype(jnp.bfloat16),
            heads_of(value_part),
            preferred_element_type=jnp.float32,
        )
        attention4 = new_acc / new_sum[..., None]
        log_total = new_max + jnp.log(new_sum)
        attention_low = attention4.reshape(rows_mb, block_len, model_width).astype(jnp.bfloat16)
        branch = jnp.einsum("rbd,de->rbe", attention_low, w_out, preferred_element_type=jnp.float32)
        middle_state = residual_stream + branch + b_out.astype(jnp.float32)
        second_normed_rows, second_standardized, second_inverse_deviation = apply_norm(
            middle_state, second_gain, second_norm_bias.astype(jnp.float32)
        )
        act2 = second_normed_rows.astype(jnp.bfloat16)
        pre_gelu = jnp.einsum(
            "rbd,df->rbf", act2, w_fc, preferred_element_type=jnp.float32
        ) + b_fc.astype(jnp.float32)
        hidden = gelu_tanh(pre_gelu).astype(jnp.bfloat16)
        result = middle_state + jnp.einsum(
            "rbf,fd->rbd", hidden, w_proj, preferred_element_type=jnp.float32
        )
        result = result + b_proj.astype(jnp.float32)
        outputs.append(result.astype(jnp.bfloat16))
        upstream_gradient = cot_part.astype(jnp.float32)
        grad_wproj = jnp.einsum("rbf,rbd->fd", hidden, cot_part, preferred_element_type=jnp.float32)
        grad_bproj = jnp.sum(upstream_gradient, axis=(0, 1))
        grad_hidden = jnp.einsum(
            "rbd,fd->rbf", cot_part, w_proj, preferred_element_type=jnp.float32
        )
        gelu_value, gelu_pull = jax.vjp(gelu_tanh, pre_gelu)
        grad_pre = gelu_pull(grad_hidden)[0].astype(jnp.bfloat16)
        grad_wfc = jnp.einsum("rbd,rbf->df", act2, grad_pre, preferred_element_type=jnp.float32)
        grad_bfc = jnp.sum(grad_pre.astype(jnp.float32), axis=(0, 1))
        second_activation_gradient = jnp.einsum(
            "rbf,df->rbd", grad_pre, w_fc, preferred_element_type=jnp.float32
        )
        second_norm_gradient, second_gain_gradient, second_bias_gradient = apply_norm_backward(
            second_activation_gradient, second_standardized, second_inverse_deviation, second_gain
        )
        grad_middle = upstream_gradient + second_norm_gradient
        grad_branch = grad_middle.astype(jnp.bfloat16)
        grad_wout = jnp.einsum(
            "rbd,rbe->de", attention_low, grad_branch, preferred_element_type=jnp.float32
        )
        grad_bout = jnp.sum(grad_branch.astype(jnp.float32), axis=(0, 1))
        grad_attention = jnp.einsum(
            "rbe,de->rbd", grad_branch, w_out, preferred_element_type=jnp.float32
        ).astype(jnp.bfloat16)
        dout4 = heads_of(grad_attention)
        out_dot = jnp.sum(dout4.astype(jnp.float32) * attention4, axis=-1)
        back_key_part = lax.all_gather(keys_low, "blk", axis=1, tiled=True)
        back_value_part = lax.all_gather(values_low, "blk", axis=1, tiled=True)
        back_span = back_key_part.shape[1]
        back_key_pos = jnp.arange(back_span)
        back_mask = visible(seg_local, seg_row, own_pos, back_key_pos)
        part_key4 = heads_of(back_key_part)
        probs_low, grad_scores = grad_block(
            query4, part_key4, heads_of(back_value_part), dout4, log_total, out_dot, back_mask
        )
        query_acc = jnp.einsum(
            "rqhk,rkhd->rqhd", grad_scores, part_key4, preferred_element_type=jnp.float32
        )
        key_piece = jnp.einsum(
            "rqhk,rqhd->rkhd", grad_scores, query4, preferred_element_type=jnp.float32
        ).reshape(rows_mb, back_span, model_width)
        value_piece = jnp.einsum(
            "rqhk,rqhd->rkhd", probs_low, dout4, preferred_element_type=jnp.float32
        ).reshape(rows_mb, back_span, model_width)
        query_acc, key_acc, value_acc = (query_acc, key_piece, value_piece)
        grad_keys, grad_values = (
            lax.psum_scatter(
                key_acc.astype(jnp.bfloat16), "blk", scatter_dimension=1, tiled=True
            ).astype(jnp.float32),
            lax.psum_scatter(
                value_acc.astype(jnp.bfloat16), "blk", scatter_dimension=1, tiled=True
            ).astype(jnp.float32),
        )
        grad_query = query_acc.reshape(rows_mb, block_len, model_width)
        grad_qkv = jnp.concatenate(
            [
                grad_query.astype(jnp.bfloat16),
                grad_keys.astype(jnp.bfloat16),
                grad_values[..., :val_width].astype(jnp.bfloat16),
            ],
            axis=-1,
        )
        first_grads.append(grad_values[..., val_width:].astype(jnp.bfloat16))
        grad_wqkv = jnp.einsum("rbd,rbe->de", act1, grad_qkv, preferred_element_type=jnp.float32)
        grad_bquery = jnp.sum(grad_qkv[..., :model_width].astype(jnp.float32), axis=(0, 1))
        grad_bvalue = jnp.sum(grad_qkv[..., 2 * model_width :].astype(jnp.float32), axis=(0, 1))
        first_activation_gradient = jnp.einsum(
            "rbe,de->rbd", grad_qkv, w_qkv, preferred_element_type=jnp.float32
        )
        first_norm_gradient, first_gain_gradient, first_bias_gradient = apply_norm_backward(
            first_activation_gradient, first_standardized, first_inverse_deviation, first_gain
        )
        input_grads.append((grad_middle + first_norm_gradient).astype(jnp.bfloat16))
        gradient_set = (
            first_gain_gradient,
            first_bias_gradient,
            grad_wqkv,
            grad_bquery,
            grad_bvalue,
            grad_wout,
            grad_bout,
            second_gain_gradient,
            second_bias_gradient,
            grad_wfc,
            grad_bfc,
            grad_wproj,
            grad_bproj,
        )
        if totals is None:
            totals = gradient_set
        else:
            totals = tuple((older + newer for older, newer in zip(totals, gradient_set)))
    totals = jax.tree.map(
        lambda part: part.astype(jnp.float32),
        lax.psum_scatter(as_sent(totals), "batch", scatter_dimension=0, tiled=True),
    )
    totals = jax.tree.map(lambda part: part.astype(jnp.float32), lax.psum(as_sent(totals), "blk"))
    return (
        jnp.concatenate(outputs, axis=0),
        jnp.concatenate(input_grads, axis=0),
        jnp.concatenate(first_grads, axis=0),
    ) + tuple(totals)


def layer(inputs, *rest):
    whole_rows = lax.axis_size("blk") == inputs.shape[0] == 2 and inputs.shape[1] == 2 * QB
    whole_rows = whole_rows and lax.axis_size("batch") == 16
    return (paired if whole_rows else spread)(inputs, *rest)


def solution(mesh):
    rows = P("batch", "blk", None)
    flat = P("batch")
    wide = P("batch", None)
    return jax.shard_map(
        layer,
        mesh=mesh,
        in_specs=(rows, rows, P("batch", "blk")) + (P(),) * 13 + (rows,),
        out_specs=(rows, rows, rows)
        + (flat, flat, wide, flat, flat, wide, flat, flat, flat, wide, flat, wide, flat),
        check_vma=False,
    )
```

```python
import functools

import jax
import jax.numpy as jnp
from jax import lax
from jax.experimental import pallas as pl
from jax.experimental.pallas import tpu as pltpu
from jax.sharding import PartitionSpec as P

HEADS = 12
HEAD_DIM = 64
PAIRS = HEADS // 2
LANES = 2 * HEAD_DIM
EPS = 1e-05
NEG = -1e30
QB = 256
F32 = jnp.float32
BF = jnp.bfloat16
MIB = 2**20
MESH = pl.DeviceIdType.MESH


def nn(a, b):
    return lax.dot_general(a, b, (((1,), (0,)), ((), ())), preferred_element_type=F32)


def nt(a, b):
    return lax.dot_general(a, b, (((1,), (1,)), ((), ())), preferred_element_type=F32)


def tn(a, b):
    return lax.dot_general(a, b, (((0,), (0,)), ((), ())), preferred_element_type=F32)


def norm_parts(rows):
    mean = jnp.mean(rows, axis=-1, keepdims=True)
    centred = rows - mean
    inverse = lax.rsqrt(jnp.mean(centred * centred, axis=-1, keepdims=True) + EPS)
    return centred * inverse, inverse


def norm_pull(grad, xhat, inverse, gain):
    scaled = grad * gain
    first = jnp.mean(scaled, axis=-1, keepdims=True)
    second = jnp.mean(scaled * xhat, axis=-1, keepdims=True)
    return inverse * (scaled - first - xhat * second)


def row(ref):
    return ref[...].astype(F32).reshape(1, -1)


def column_sum(rows):
    return jnp.sum(rows, axis=0, keepdims=True)


def spot():
    b = lax.axis_index("batch")
    core = lax.rem(b, 2)
    x = lax.rem(lax.div(b, 2), 2)
    near = lax.rem(lax.div(b, 4), 2)
    far = lax.div(b, 8)
    return b, core, x, near, far


def partners():
    b, core, x, near, far = spot()
    return [
        {"batch": b + 1 - 2 * core},
        {"batch": b + 2 - 4 * x},
        {"batch": b + 4 - 8 * near},
        {"batch": b + 8 - 16 * far},
        {"blk": 1 - lax.axis_index("blk")},
    ]


FLIPS = [(f, n, x) for f in range(2) for n in range(2) for x in range(2) if f + n + x]


def flipped(flip):
    _, core, x, near, far = spot()
    at = [own + turn * (1 - 2 * own) for own, turn in zip((far, near, x), flip)]
    return tuple(at) + (core,), {"batch": ((at[0] * 2 + at[1]) * 2 + at[2]) * 2 + core}


def greet(friends):
    barrier = pltpu.get_barrier_semaphore()
    for friend in friends:
        pl.semaphore_signal(barrier, inc=1, device_id=friend, device_id_type=MESH)


def meet(friends):
    pl.semaphore_wait(pltpu.get_barrier_semaphore(), len(friends))


def push(src, dst, send_sem, recv_sem, friend):
    copy = pltpu.make_async_remote_copy(
        src_ref=src,
        dst_ref=dst,
        send_sem=send_sem,
        recv_sem=recv_sem,
        device_id=friend,
        device_id_type=MESH,
    )
    return copy


def add_into(dst, src):
    dst[...] = dst[...] + src[...]


PLACES = ("core", "x", "near", "far")


class Sum:
    def __init__(self, held, got, dims, order, send_sem, recv_sem, cut_columns=True):
        self.held, self.got, self.dims, self.order = held, got, dims, order
        self.send_sem, self.recv_sem, self.cut_columns = send_sem, recv_sem, cut_columns

    def cut(self, stage, keep):
        name = self.order[stage]
        done = self.order[:stage]
        _, core, x, near, far = spot()
        own = {"core": core, "x": x, "near": near, "far": far}
        at = []
        for dim in self.dims:
            if dim == name:
                at.append(own[dim] if keep else 1 - own[dim])
            else:
                at.append(own[dim] if dim in done else slice(None))
        if self.cut_columns and (name == "half" or "half" in done):
            me = lax.axis_index("blk")
            size = self.held.shape[-1] // 2
            side = 1 - me if name == "half" and not keep else me
            at += [slice(None), pl.ds(pl.multiple_of(side * size, size), size)]
        return tuple(at)

    def copy(self, stage):
        name = self.order[stage]
        return push(
            self.held.at[self.cut(stage, False)],
            self.got[stage],
            self.send_sem.at[stage],
            self.recv_sem.at[stage],
            partners()[PLACES.index(name) if name in PLACES else 4],
        )

    def start(self, stage):
        self.copy(stage).start()

    def take(self, stage):
        self.copy(stage).wait()
        mine = self.held.at[self.cut(stage, True)]
        came = self.got[stage]
        lead = came.shape[:-2]
        count = 1
        for size in lead:
            count *= size
        for n in range(count):
            at = []
            for size in reversed(lead):
                at.insert(0, n % size)
                n //= size
            at = tuple(at)
            add_into(mine.at[at] if at else mine, came.at[at] if at else came)
        if stage + 1 < len(self.order):
            self.start(stage + 1)

    def last(self):
        stage = len(self.order) - 1
        self.copy(stage).wait()
        return self.held[self.cut(stage, True)].astype(F32), self.got[stage][...].astype(F32)


class Vectors:
    def __init__(self, held, got, place, sems, far_sems):
        self.held, self.got, self.place = held, got, place
        self.sems, self.far_sems = sems, far_sems

    def copies(self, stage):
        src = self.held.at[stage]
        if stage == 1:
            return [
                push(
                    src,
                    self.got[1].at[n],
                    self.far_sems[0].at[self.place, n],
                    self.far_sems[1].at[self.place, n],
                    flipped(flip)[1],
                )
                for n, flip in enumerate(FLIPS)
            ]
        friend = partners()[stage * 2]
        return [push(src, self.got[stage], self.sems[0].at[stage], self.sems[1].at[stage], friend)]

    def start(self, stage):
        for copy in self.copies(stage):
            copy.start()

    def take(self, stage):
        for copy in self.copies(stage):
            copy.wait()
        if stage == 1:
            total = self.held[1]
            for n in range(len(FLIPS)):
                total = total + self.got[1][n]
        else:
            total = self.held[stage] + self.got[stage][...]
        self.held[stage + 1] = total
        if stage < 2:
            self.start(stage + 1)


def front_kernel(
    x_in,
    fv_in,
    seg_in,
    cot_in,
    g1_ref,
    b1_ref,
    wqkv_in,
    bq_ref,
    bv_ref,
    wout_in,
    bout_ref,
    g2_ref,
    b2_ref,
    x_out,
    q_out,
    k_out,
    v_out,
    att_out,
    act2_out,
    mid_out,
    lse_ref,
    bias_out,
    act1t_out,
    cot_out,
    xs,
    qs,
    ks,
    vs,
    atts,
    act2s,
    mids,
    bias,
    wqkv,
    wout,
    segrow,
    segsend,
    segcol,
    act1ts,
    turned,
    held,
    in_sem,
    out_sem,
    send_sem,
    recv_sem,
):
    half = x_in.shape[1]
    tokens = 2 * half
    width = x_in.shape[2]
    val = fv_in.shape[2]
    steps = tokens // QB
    me = lax.axis_index("blk")
    other = 1 - me
    mine = pl.multiple_of(me * half, half)
    theirs = pl.multiple_of(other * half, half)

    def local_in(i, src, dst):
        copy = pltpu.make_async_copy(src, dst, in_sem.at[i])
        copy.start()
        return copy

    own_x = local_in(0, x_in.at[me], xs.at[pl.ds(mine, half)])
    own_fv = local_in(1, fv_in.at[me], vs.at[pl.ds(mine, half), pl.ds(val, val)])
    own_w = local_in(2, wqkv_in, wqkv)
    own_wo = local_in(3, wout_in, wout)
    first, second = seg_in[0:1, :], seg_in[1:2, :]
    segsend[...] = jnp.broadcast_to(jnp.where(me == 0, second, first), segsend.shape)

    barrier = pltpu.get_barrier_semaphore()
    pl.semaphore_signal(barrier, inc=1, device_id={"blk": other}, device_id_type=MESH)
    pl.semaphore_wait(barrier, 1)

    def remote(i, src, dst):
        copy = pltpu.make_async_remote_copy(
            src_ref=src,
            dst_ref=dst,
            send_sem=send_sem.at[i],
            recv_sem=recv_sem.at[i],
            device_id={"blk": other},
            device_id_type=MESH,
        )
        copy.start()
        return copy

    part = half // 2
    far_seg = remote(2, segsend, segrow.at[:, pl.ds(mine, half)])
    far_x = [
        remote(
            c,
            x_in.at[other, pl.ds(c * part, part)],
            xs.at[pl.ds(pl.multiple_of(mine + c * part, part), part)],
        )
        for c in range(2)
    ]
    far_fv = remote(3, fv_in.at[other], vs.at[pl.ds(mine, half), pl.ds(val, val)])
    far_cot = remote(4, cot_in.at[other, pl.ds(0, part)], cot_out)

    own_row = jnp.broadcast_to(jnp.where(me == 0, first, second), (8, half))
    segrow[:, pl.ds(mine, half)] = own_row

    def project(start):
        rows = pl.ds(pl.multiple_of(start, QB), QB)
        xhat, _ = norm_parts(xs[rows, :].astype(F32))
        act1 = (xhat * row(g1_ref) + row(b1_ref)).astype(BF)
        act1ts[:, rows] = act1.T
        out = nn(act1, wqkv[...])
        query = (out[:, :width] + row(bq_ref)).astype(BF)
        qs[rows, :] = query * jnp.asarray(HEAD_DIM**-0.5, BF)
        ks[rows, :] = out[:, width : 2 * width].astype(BF)
        vs[rows, pl.ds(0, val)] = (out[:, 2 * width :] + row(bv_ref)).astype(BF)

    low = lax.broadcasted_iota(jnp.int32, (1, LANES), 1) < HEAD_DIM
    count = half // QB

    def at(start):
        return pl.ds(pl.multiple_of(start, QB), QB)

    def turn_segments(start):
        for c in range(half // LANES):
            place = pl.ds(pl.multiple_of(start + c * LANES, LANES), LANES)
            line = segrow[0:1, place].astype(F32)
            segcol[place, :] = jnp.broadcast_to(line, (LANES, LANES)).T

    def mask_block(key_start, query_start, diagonal):
        key = segcol[at(key_start), :]
        key = jnp.concatenate([key] * (QB // LANES), axis=1)
        query = segrow[0:1, at(query_start)].astype(F32)
        seen = (key == query) & (query >= 0.0)
        if diagonal:
            down = lax.broadcasted_iota(jnp.int32, (QB, QB), 0)
            across = lax.broadcasted_iota(jnp.int32, (QB, QB), 1)
            seen = (seen & (down <= across)) | (down == across)
        bias[at(key_start), at(query_start)] = jnp.where(seen, 0.0, NEG)

    def mask_half(start):
        turn_segments(start)
        for i in range(count):
            for j in range(i + 1):
                mask_block(start + j * QB, start + i * QB, i == j)

    def attend(p, items):
        cols = pl.ds(pl.multiple_of(p * LANES, LANES), LANES)
        done = {}

        def score(first, span, query, h, more):
            keys = pl.ds(pl.multiple_of(first, QB), span)
            q = qs[at(query), cols]
            q = jnp.where(low if h == 0 else ~low, q, jnp.zeros_like(q))
            return nt(ks[keys, cols], q) + bias[keys, at(query)]

        def finish(first, span, query, h, more, s):
            keys = pl.ds(pl.multiple_of(first, QB), span)
            rows = at(query)
            top = jnp.max(s, axis=0, keepdims=True)
            if more:
                before = lse_ref[p, h : h + 1, rows]
                top = jnp.maximum(top, before)
            e = jnp.exp(s - top)
            total = jnp.sum(e, axis=0, keepdims=True)
            if more:
                total = total + jnp.exp(before - top)
            log_total = top + jnp.log(total)
            lse_ref[p, h : h + 1, rows] = log_total
            lines = slice(h * HEAD_DIM, (h + 1) * HEAD_DIM)
            out = nn(turned[lines, keys], e.astype(BF)) * (1.0 / total)
            if more:
                out = out + held[p, lines, rows] * jnp.exp(before - log_total)
            held[p, lines, rows] = out
            done[h] = out.astype(BF)
            if h == 1:
                atts[rows, cols] = jnp.concatenate([done[0], done[1]], axis=0).T

        waiting = []
        for item in items:
            waiting.append(item + (score(*item),))
            if len(waiting) > 3:
                finish(*waiting.pop(0))
        for item in waiting:
            finish(*item)

    def half_items(start):
        return [
            (start, (i + 1) * QB, start + i * QB, h, False) for i in range(count) for h in range(2)
        ]

    cross_items = [
        (0, half, half + i * QB, h, True) for i in range(count) for h in range(2)
    ]

    own_x.wait()
    own_w.wait()
    for c in range(count):
        project(mine + c * QB)
    mask_half(mine)
    own_fv.wait()

    @pl.loop(0, PAIRS)
    def _(p):
        cols = pl.ds(pl.multiple_of(p * LANES, LANES), LANES)
        turned[:, pl.ds(mine, half)] = vs[pl.ds(mine, half), cols].T
        attend(p, half_items(mine))

    far_seg.wait()
    mask_half(theirs)
    for i in range(count):
        for j in range(count):
            mask_block(j * QB, half + i * QB, False)

    for c in range(2):
        far_x[c].wait()
        project(theirs + c * part)

    outs = []

    def local_out(src, dst):
        copy = pltpu.make_async_copy(src, dst, out_sem.at[len(outs)])
        copy.start()
        outs.append(copy)

    local_out(act1ts, act1t_out)
    local_out(xs, x_out)
    local_out(qs, q_out)
    local_out(ks, k_out)

    for j in range(steps):
        cut = (pl.ds(j * QB, QB), pl.ds(j * QB, tokens - j * QB))
        local_out(bias.at[cut], bias_out.at[cut])

    @pl.loop(0, PAIRS)
    def _(p):
        @pl.when(p == PAIRS // 2)
        def _():
            far_fv.wait()

        cols = pl.ds(pl.multiple_of(p * LANES, LANES), LANES)
        turned[...] = vs[:, cols].T
        attend(p, half_items(theirs) + cross_items)

    local_out(atts, att_out)
    local_out(vs, v_out)
    own_wo.wait()
    for c in range(steps):
        rows = slice(c * QB, (c + 1) * QB)
        middle = xs[rows, :].astype(F32) + nn(atts[rows, :], wout[...]) + row(bout_ref)
        mids[rows, :] = middle
        xhat, _ = norm_parts(middle)
        act2s[rows, :] = (xhat * row(g2_ref) + row(b2_ref)).astype(BF)
        local_out(mids.at[rows, :], mid_out.at[rows, :])
        local_out(act2s.at[rows, :], act2_out.at[rows, :])
    for copy in outs:
        copy.wait()
    far_cot.wait()


def front(x, fv, seg, cot, g1, b1, wqkv, bq, bv, wout, bout, g2, b2):
    half, width, val = x.shape[1], x.shape[2], fv.shape[2]
    tokens = 2 * half
    hbm = pl.BlockSpec(memory_space=pl.ANY)
    vmem = pl.BlockSpec(memory_space=pltpu.VMEM)
    flat = jax.ShapeDtypeStruct((tokens, width), BF)
    shape = jax.ShapeDtypeStruct
    return pl.pallas_call(
        front_kernel,
        in_specs=[hbm, hbm, vmem, hbm, vmem, vmem, hbm, vmem, vmem, hbm, vmem, vmem, vmem],
        out_specs=[hbm] * 7 + [vmem] + [hbm] * 3,
        out_shape=[
            flat,
            flat,
            flat,
            flat,
            flat,
            flat,
            shape((tokens, width), F32),
            shape((PAIRS, 2, tokens), F32),
            shape((tokens, tokens), F32),
            shape((width, tokens), BF),
            shape((half // 2, width), BF),
        ],
        scratch_shapes=[
            pltpu.VMEM((tokens, width), BF),
            pltpu.VMEM((tokens, width), BF),
            pltpu.VMEM((tokens, width), BF),
            pltpu.VMEM((tokens, width), BF),
            pltpu.VMEM((tokens, width), BF),
            pltpu.VMEM((tokens, width), BF),
            pltpu.VMEM((tokens, width), F32),
            pltpu.VMEM((tokens, tokens), F32),
            pltpu.VMEM(wqkv.shape, BF),
            pltpu.VMEM(wout.shape, BF),
            pltpu.VMEM((8, tokens), jnp.int32),
            pltpu.VMEM((8, half), jnp.int32),
            pltpu.VMEM((tokens, LANES), F32),
            pltpu.VMEM((width, tokens), BF),
            pltpu.VMEM((LANES, tokens), BF),
            pltpu.VMEM((PAIRS, LANES, tokens), F32),
            pltpu.SemaphoreType.DMA((5,)),
            pltpu.SemaphoreType.DMA((8 + 3 * tokens // QB,)),
            pltpu.SemaphoreType.DMA((5,)),
            pltpu.SemaphoreType.DMA((5,)),
        ],
        compiler_params=pltpu.CompilerParams(
            collective_id=0, has_side_effects=True, vmem_limit_bytes=56 * MIB
        ),
        name="front",
    )(x, fv, seg, cot, g1, b1, wqkv, bq, bv, wout, bout, g2, b2)


def feed_kernel(
    act2,
    g2_ref,
    bproj_ref,
    bfc_ref,
    wfc,
    wproj,
    cot_in,
    cot_far,
    mid_in,
    att_in,
    wout_in,
    lout_out,
    gmid_out,
    gatt_out,
    dwout_out,
    f_out,
    f2_out,
    f3_out,
    p_out,
    dots,
    dbfc,
    small,
    cots,
    mids,
    atts,
    wout,
    acc,
    act2t,
    hid,
    slope,
    dpre,
    louts,
    gatts,
    dwouts,
    sel,
    bias,
    gf,
    gp,
    rf0,
    rp0,
    rfh,
    rp1,
    in_sem,
    out_sem,
    send_sem,
    recv_sem,
):
    t = pl.program_id(0)
    tiles = pl.num_programs(0) // 2
    tokens, width = act2.shape
    half = tokens // 2
    tile = dpre.shape[1]
    steps = tokens // QB
    count = gf.shape[0]
    _, core, x, _, _ = spot()
    me = lax.axis_index("blk")
    mine = pl.multiple_of(me * half, half)
    theirs = pl.multiple_of((1 - me) * half, half)
    both = partners()
    friends = [both[0], both[1], both[4]]
    side = pl.ds(pl.multiple_of(me * (tile // 2), tile // 2), tile // 2)

    def chain(held, got, dims, order, n):
        return Sum(held, got, dims, order, send_sem.at[n], recv_sem.at[n])

    full = ("far", "near", "x", "core")
    fcs = [chain(gf.at[n], [rf0.at[n], rfh.at[n]], full, ("core", "half"), n) for n in range(2)]
    fcs.append(chain(gf.at[2], [rf0.at[2]], full, ("core",), 2))
    projs = [chain(gp.at[n], [rp0.at[n], rp1.at[n]], full[2:], ("core", "x"), 3 + n) for n in range(4)]

    def load(n):
        src, dst = [
            (cot_in.at[me], cots.at[pl.ds(mine, half)]),
            (cot_far, cots.at[pl.ds(theirs, half // 2)]),
            (mid_in, mids),
            (att_in, atts),
            (wout_in, wout),
        ][n]
        return pltpu.make_async_copy(src, dst, in_sem.at[n])

    far_cot = push(
        cot_in.at[1 - me, pl.ds(half // 2, half // 2)],
        cots.at[pl.ds(pl.multiple_of(mine + half // 2, half // 2), half // 2)],
        send_sem.at[7, 0],
        recv_sem.at[7, 0],
        friends[2],
    )
    back = push(
        louts.at[pl.ds(theirs, half)], lout_out.at[me], send_sem.at[7, 1], recv_sem.at[7, 1], friends[2]
    )

    stores = [
        (louts.at[pl.ds(mine, half)], lout_out.at[me]),
        (acc, gmid_out),
        (gatts, gatt_out),
        (dwouts, dwout_out),
        (gf.at[3], f3_out),
    ]
    size = tile // 2
    stores += [
        (gf.at[n, :, :, :, core, :, side], f_out.at[:, :, :, :, n * size : (n + 1) * size]) for n in range(2)
    ]
    stores.append((gf.at[2, :, :, :, core], f2_out))
    stores += [(gp.at[n, x, core], p_out.at[n // 2, n % 2]) for n in range(4)]

    def store(n):
        return pltpu.make_async_copy(stores[n][0], stores[n][1], out_sem.at[n])

    def at_step(k, *actions):
        @pl.when(t == k)
        def _():
            for action in actions:
                action()

    @pl.when(t == 0)
    def _():
        for n in range(5):
            load(n).start()
        greet(friends)
        act2t[...] = act2[...].T
        for n in range(count):
            bias[n] = row(bfc_ref)[:, n * tile : (n + 1) * tile]
        acc[...] = jnp.zeros_like(acc)
        head = lax.broadcasted_iota(jnp.int32, sel.shape, 0)
        feature = lax.broadcasted_iota(jnp.int32, sel.shape, 1)
        inside = (feature >= head * HEAD_DIM) & (feature < (head + 1) * HEAD_DIM)
        sel[...] = jnp.where(inside, 1.0, 0.0).astype(BF)

    @pl.when(t < tiles)
    def _():
        for c in range(steps):
            rows = slice(c * QB, (c + 1) * QB)
            u = nn(act2[rows, :], wfc[...]) + bias[t]
            square = u * u
            bend = jnp.tanh(u * (0.7978845608028654 + (0.7978845608028654 * 0.044715) * square))
            halfway = 0.5 + 0.5 * bend
            hidden = (u * halfway).astype(BF)
            hid[t, rows, :] = hidden
            slope[t, rows, :] = (
                halfway
                + (u * (0.5 - 0.5 * bend * bend))
                * (0.7978845608028654 + (3 * 0.7978845608028654 * 0.044715) * square)
            ).astype(BF)
            acc[rows, :] += nn(hidden, wproj[...])

    @pl.when(t == 0)
    def _():
        meet(friends)
        far_cot.start()

    @pl.when(t == tiles - 1)
    def _():
        load(2).wait()
        for c in range(steps):
            rows = slice(c * QB, (c + 1) * QB)
            louts[rows, :] = (mids[rows, :] + acc[rows, :] + row(bproj_ref)).astype(BF)
        back.start()
        store(0).start()
        acc[...] = jnp.zeros_like(acc)
        load(0).wait()
        load(1).wait()
        far_cot.wait()

    @pl.when(t >= tiles)
    def _():
        n = t - tiles
        total = None
        for c in range(steps):
            rows = slice(c * QB, (c + 1) * QB)
            grad = (nt(cots[rows, :], wproj[...]) * slope[n, rows, :].astype(F32)).astype(BF)
            dpre[rows, :] = grad
            acc[rows, :] += nt(grad, wfc[...])
            part = column_sum(grad.astype(F32))
            total = part if total is None else total + part
            if c == 2:
                for k in range(3):
                    at_step(tiles + k + 1, lambda k=k: projs[k].take(0), lambda k=k: fcs[k].take(0))
        dbfc[...] = total
        gp[n] = tn(hid[n], cots[...]).astype(BF).reshape(gp.shape[1:])
        gf[n] = nn(act2t[...], dpre[...]).astype(BF).reshape(gf.shape[1:])

    for k in range(3):
        at_step(tiles + k, lambda k=k: projs[k].start(0), lambda k=k: fcs[k].start(0))
    at_step(tiles + 3, lambda: projs[3].start(0))

    @pl.when(t == 2 * tiles - 1)
    def _():
        store(4).start()
        store(7).start()
        load(3).wait()
        load(4).wait()
        projs[0].take(1)
        store(8).start()
        gain = row(g2_ref)
        sums = [None] * 4
        for c in range(steps):
            rows = slice(c * QB, (c + 1) * QB)
            middle = mids[rows, :]
            upstream = cots[rows, :].astype(F32)
            xhat, inverse = norm_parts(middle)
            da = acc[rows, :]
            grad_middle = upstream + norm_pull(da, xhat, inverse, gain)
            acc[rows, :] = grad_middle
            branch = grad_middle.astype(BF)
            dpre[rows, :] = branch
            parts = [
                column_sum(upstream),
                column_sum(da * xhat),
                column_sum(da),
                column_sum(branch.astype(F32)),
            ]
            sums = [b if a is None else a + b for a, b in zip(sums, parts)]
            ga = nt(branch, wout[...]).astype(BF)
            gatts[rows, :] = ga
            product = ga.astype(F32) * atts[rows, :].astype(F32)
            big = product.astype(BF)
            rest = (product - big.astype(F32)).astype(BF)
            dot = nt(sel[...], big) + nt(sel[...], rest)
            for p in range(PAIRS):
                dots[p, :, rows] = dot[2 * p : 2 * p + 2, :]
            if c == 1:
                projs[3].take(0)
        store(1).start()
        store(2).start()
        small[...] = jnp.concatenate(sums, axis=0)
        dwouts[...] = tn(atts[...], dpre[...]).astype(BF).reshape(dwouts.shape)
        store(3).start()
        projs[1].take(1)
        store(9).start()
        fcs[0].take(1)
        store(5).start()
        projs[2].take(1)
        store(10).start()
        fcs[1].take(1)
        store(6).start()
        projs[3].take(1)
        store(11).start()
        for n in range(len(stores)):
            store(n).wait()
        back.wait()


def feed(act2, cotangent, cot_far, mid, att, g2, bproj, wout, wfc, bfc, wproj):
    tokens, width = act2.shape
    half = tokens // 2
    ff = wfc.shape[1]
    tiles = 4
    tile = ff // tiles
    owner = width // 16
    owner_ff = ff // 16
    shape = jax.ShapeDtypeStruct
    flat = shape((tokens, width), BF)
    once = pl.Buffered(1)
    hbm = pl.BlockSpec(memory_space=pl.ANY)

    def whole(s):
        return pl.BlockSpec(s, lambda t: (0,) * len(s), pipeline_mode=once)

    def vm(*s):
        return pltpu.VMEM(s, BF)

    line = whole((width,))
    return pl.pallas_call(
        feed_kernel,
        grid=(2 * tiles,),
        in_specs=[
            whole((tokens, width)),
            line,
            line,
            whole((ff,)),
            pl.BlockSpec((width, tile), lambda t: (0, lax.rem(t, tiles))),
            pl.BlockSpec((tile, width), lambda t: (lax.rem(t, tiles), 0)),
        ]
        + [hbm] * 5,
        out_specs=[hbm] * 8
        + [
            whole((PAIRS, 2, tokens)),
            pl.BlockSpec((1, tile), lambda t: (0, jnp.maximum(t - tiles, 0))),
            whole((4, width)),
        ],
        out_shape=[
            shape((2, half, width), BF),
            shape((tokens, width), F32),
            flat,
            shape((2, 2, 2, 2, owner, width), BF),
            shape((2, 2, 2, owner, tile), BF),
            shape((2, 2, 2, owner, tile), BF),
            shape((2, 2, 2, 2, owner, tile), BF),
            shape((2, 2, owner_ff, width), BF),
            shape((PAIRS, 2, tokens), F32),
            shape((1, ff), F32),
            shape((4, width), F32),
        ],
        scratch_shapes=[
            vm(tokens, width),
            pltpu.VMEM((tokens, width), F32),
            vm(tokens, width),
            vm(width, width),
            pltpu.VMEM((tokens, width), F32),
            vm(width, tokens),
            vm(tiles, tokens, tile),
            vm(tiles, tokens, tile),
            vm(tokens, tile),
            vm(tokens, width),
            vm(tokens, width),
            vm(2, 2, 2, 2, owner, width),
            vm(16, width),
            pltpu.VMEM((tiles, 1, tile), F32),
            vm(tiles, 2, 2, 2, 2, owner, tile),
            vm(tiles, 2, 2, owner_ff, width),
            vm(3, 2, 2, 2, owner, tile),
            vm(4, 2, owner_ff, width),
            vm(2, 2, 2, 2, owner, tile // 2),
            vm(4, owner_ff, width),
            pltpu.SemaphoreType.DMA((5,)),
            pltpu.SemaphoreType.DMA((12,)),
            pltpu.SemaphoreType.DMA((8, 2)),
            pltpu.SemaphoreType.DMA((8, 2)),
        ],
        compiler_params=pltpu.CompilerParams(
            collective_id=1, has_side_effects=True, vmem_limit_bytes=62 * MIB
        ),
        name="feed",
    )(act2, g2, bproj, bfc, wfc, wproj, cotangent, cot_far, mid, att, wout)


FIRST_PAIR = PAIRS // 2


def pieces(width, val):
    lanes = LANES
    return [
        (3, [(3 * lanes, 3 * lanes), (width + 3 * lanes, 3 * lanes)]),
        (5, [(0, 2 * lanes), (width, 2 * lanes), (2 * width, 2 * lanes)]),
        (6, [(2 * lanes, lanes), (width + 2 * lanes, lanes), (2 * width + 2 * lanes, lanes)]),
    ]


def tail_kernel(
    q_in,
    k_in,
    v_in,
    do_in,
    bias_in,
    x_in,
    act1t_in,
    gmid_in,
    wqkv_in,
    dwout_in,
    f_in,
    f2_in,
    f3_in,
    p_in,
    lse_ref,
    d_ref,
    g1_ref,
    dbfc_ref,
    small_in,
    gx_out,
    gf_out,
    wqkv_out,
    wout_out,
    wfc_out,
    wproj_out,
    small_out,
    q_ref,
    k_ref,
    v_ref,
    do_ref,
    bias,
    xs,
    gmid,
    wqkv,
    dqk,
    dvs,
    gfs,
    dqa,
    act1t,
    gx,
    g_out,
    g_f,
    g_f2,
    g_f3,
    g_p,
    g_q,
    r_out,
    r_f,
    r_f2,
    r_f3,
    r_p,
    r_q,
    last_sum,
    r_z,
    r_last,
    sums,
    s_got,
    late,
    l_got,
    w_fc,
    w_proj,
    w_out,
    in_sem,
    out_sem,
    back_send,
    back_recv,
    sum_send,
    sum_recv,
    far_send,
    far_recv,
):
    tokens, width = q_ref.shape
    half = tokens // 2
    val = gfs.shape[1]
    steps = tokens // QB
    me = lax.axis_index("blk")
    mine = pl.multiple_of(me * half, half)
    theirs = pl.multiple_of((1 - me) * half, half)
    _, core, x, near, far = spot()
    friends = partners()
    parts = pieces(width, val)

    sources = {
        "f3": (f3_in, g_f3),
        "out": (dwout_in, g_out),
        "p": (p_in, g_p),
        "f": (f_in, g_f),
        "f2": (f2_in, g_f2),
        "q": (q_in, q_ref),
        "k": (k_in, k_ref),
        "bias": (bias_in, bias),
        "v": (v_in, v_ref),
        "do": (do_in, do_ref),
        "act1t": (act1t_in, act1t),
        "x": (x_in, xs),
        "wqkv": (wqkv_in, wqkv),
        "gmid": (gmid_in, gmid),
    }
    loads = {
        name: pltpu.make_async_copy(src, dst, in_sem.at[n])
        for n, (name, (src, dst)) in enumerate(sources.items())
    }
    for load in loads.values():
        load.start()
    everyone = [flipped(flip)[1] for flip in FLIPS] + [friends[0], friends[4]]
    greet(everyone)
    meet(everyone)

    full = ("far", "near", "x", "core")
    down = ("core", "x", "near", "far", "pair")
    sems = iter(range(16))

    def chain(held, got, dims, order, cut_columns=True):
        n = next(sems)
        return Sum(held, got, dims, order, sum_send.at[n], sum_recv.at[n], cut_columns)

    s_out = chain(g_out, r_out, full, down)
    s_f = chain(g_f, r_f, full[:3], ("x", "near", "far", "gather"), False)
    s_f2 = chain(g_f2, r_f2, full[:3], ("half", "x", "near", "far", "gather"))
    s_f3 = chain(g_f3, r_f3, full, ("core", "half", "x", "near", "far", "gather"))
    s_p = chain(g_p, r_p, full[:2], ("half", "near", "far", "gather"))
    s_q = [chain(g, r, full, down if n < 2 else down[:2]) for n, (g, r) in enumerate(zip(g_q, r_q))]
    n_small, n_last, n_late = next(sems), next(sems), next(sems)

    def vectors(held, got, place, n):
        return Vectors(held, got, place, (sum_send.at[n], sum_recv.at[n]), (far_send, far_recv))

    s_small = vectors(sums, s_got, 0, n_small)
    s_late = vectors(late, l_got, 1, n_late)

    def z_copies():
        found = []
        for n, flip in enumerate([flip for flip in FLIPS if flip[2] == 0]):
            place, friend = flipped(flip)
            src = g_q[2].at[place]
            found.append(push(src, r_z.at[n], far_send.at[2, n], far_recv.at[2, n], friend))
        return found

    def last_x():
        s_q[2].take(1)
        for copy in z_copies():
            copy.start()

    def last_z():
        for copy in z_copies():
            copy.wait()
        total = g_q[2][far, near, x, core].astype(F32)
        for n in range(3):
            total = total + r_z[n].astype(F32)
        last_sum[...] = total.astype(BF)
        last_copy.start()

    last_copy = push(
        last_sum, r_last, sum_send.at[n_last, 0], sum_recv.at[n_last, 0], friends[4]
    )

    def give_back(n, src, dst):
        return push(src, dst, back_send.at[n], back_recv.at[n], friends[4])

    for n in range(4):
        sums[0, n : n + 1, :] = small_in[n : n + 1, :]
        sums[0, 4 + n : 5 + n, :] = dbfc_ref[:, n * width : (n + 1) * width]
    s_small.start(0)
    for name, begin in (("f3", s_f3), ("p", s_p), ("f", s_f), ("f2", s_f2), ("out", s_out)):
        loads[name].wait()
        begin.start(0)
    for name in ("q", "k", "bias", "v", "do"):
        loads[name].wait()

    low = lax.broadcasted_iota(jnp.int32, (1, LANES), 1) < HEAD_DIM
    masks = [low, ~low]
    zero = jnp.zeros((), BF)
    gain = row(g1_ref)

    def columns(at, size):
        return dqk[:, at : at + size] if at < 2 * width else dvs[:, at - 2 * width : at - 2 * width + size]

    def project_grad(n):
        at = 0
        for start, size in parts[n][1]:
            block = nn(act1t[...], columns(start, size)).astype(BF)
            g_q[n][:, :, :, :, :, at : at + size] = block.reshape(g_q[n].shape[:-1] + (size,))
            at += size
        s_q[n].start(0)

    back_gf = give_back(1, gfs.at[pl.ds(theirs, half)], gf_out.at[me])
    keep_gf = pltpu.make_async_copy(gfs.at[pl.ds(mine, half)], gf_out.at[me], out_sem.at[1])

    def take(name, stage):
        return lambda: names[name].take(stage)

    names = {"sm": s_small, "f3": s_f3, "out": s_out, "f": s_f, "p": s_p, "f2": s_f2}
    names.update({"q0": s_q[0], "q1": s_q[1]})
    plan = {
        (0, 1): [take("sm", 0), take("f3", 0), take("out", 0)],
        (1, 1): [take("f", 0)],
        (2, 1): [take("p", 0), take("sm", 1), loads["act1t"].wait],
        (3, 0): [take("f", 1), lambda: project_grad(0), back_gf.start, keep_gf.start],
        (3, 1): [take("q0", 0), take("f2", 0), take("out", 1)],
        (4, 0): [take("p", 1)],
        (4, 1): [take("f3", 1), take("f", 2), take("sm", 2)],
        (5, 0): [take("q0", 1), take("out", 2), lambda: project_grad(1)],
        (5, 1): [take("q1", 0), take("f2", 1), take("p", 2)],
    }

    def act(step, middle):
        for (k, when), actions in plan.items():
            if when == middle:

                @pl.when(step == k)
                def _():
                    for action in actions:
                        action()

    @pl.loop(0, PAIRS)
    def _(step):
        act(step, 0)
        p = lax.rem(step + FIRST_PAIR, PAIRS)
        cols = pl.ds(pl.multiple_of(p * LANES, LANES), LANES)
        kcols = pl.ds(pl.multiple_of(width + p * LANES, LANES), LANES)
        q, k, v, do = q_ref[:, cols], k_ref[:, cols], v_ref[:, cols], do_ref[:, cols]
        qm = [jnp.where(m, q, zero) for m in masks]
        km = [jnp.where(m, k, zero) for m in masks]
        dom = [jnp.where(m, do, zero) for m in masks]
        dvals = []
        for j in range(steps):
            a = j * QB
            keys = slice(a, a + QB)
            dk = dv = dq = None
            for h in range(2):
                s = nt(k[keys], qm[h][a:]) + bias[keys, a:]
                probs = jnp.exp(s - lse_ref[p, h : h + 1, a:])
                dp = nt(v[keys], dom[h][a:])
                ds = (probs * (dp - d_ref[p, h : h + 1, a:])).astype(BF)
                dvh = nn(probs.astype(BF), dom[h][a:])
                dkh = nn(ds, qm[h][a:])
                dqh = tn(ds, km[h][keys])
                dk = dkh if dk is None else dk + dkh
                dv = dvh if dv is None else dv + dvh
                dq = dqh if dq is None else dq + dqh
            dqk[keys, kcols] = dk.astype(BF)
            dvals.append(dv.astype(BF))
            if j == 0:
                act(step, 1)
            if j == 0:
                dqa[...] = dq
            else:
                dqa[a:, :] += dq
        dqk[:, cols] = (dqa[...] * HEAD_DIM**-0.5).astype(BF)

        @pl.when(p < PAIRS // 2)
        def _():
            for j in range(steps):
                dvs[j * QB : (j + 1) * QB, cols] = dvals[j]

        @pl.when(p >= PAIRS // 2)
        def _():
            late = pl.ds(pl.multiple_of(p * LANES - val, LANES), LANES)
            for j in range(steps):
                gfs[j * QB : (j + 1) * QB, late] = dvals[j]

    for name in ("x", "wqkv", "gmid"):
        loads[name].wait()

    totals = [None] * 4

    def input_grad(start, size):
        rows = pl.ds(pl.multiple_of(start, size), size)
        da = nt(dqk[rows, :], wqkv[:, : 2 * width]) + nt(dvs[rows, :], wqkv[:, 2 * width :])
        xhat, inverse = norm_parts(xs[rows, :].astype(F32))
        gx[rows, :] = (gmid[rows, :] + norm_pull(da, xhat, inverse, gain)).astype(BF)
        bv = column_sum(dvs[rows, :].astype(F32))
        found = [
            column_sum(da * xhat),
            column_sum(da),
            column_sum(dqk[rows, :width].astype(F32)),
            jnp.concatenate([bv, jnp.zeros((1, width - val), F32)], axis=1),
        ]
        totals[:] = [b if a is None else a + b for a, b in zip(totals, found)]

    backs = []

    def give_rows(at, size):
        start = pl.multiple_of(theirs + at, size)
        input_grad(start, size)
        copy = give_back(2 + len(backs), gx.at[pl.ds(start, size)], gx_out.at[me, pl.ds(at, size)])
        copy.start()
        backs.append(copy)

    give_rows(0, LANES)
    project_grad(2)
    s_q[0].take(2)
    s_f3.take(2)
    s_out.take(3)
    give_rows(LANES, LANES)
    s_f2.take(2)
    s_q[2].take(0)
    give_rows(QB, LANES)
    s_q[1].take(1)
    s_q[0].take(3)
    give_rows(QB + LANES, LANES)
    s_f3.take(3)
    input_grad(mine, LANES)
    s_f2.take(3)
    input_grad(mine + LANES, LANES)
    last_x()
    input_grad(mine + QB, LANES)
    s_q[1].take(2)
    input_grad(mine + QB + LANES, LANES)
    keep_gx = pltpu.make_async_copy(gx.at[pl.ds(mine, half)], gx_out.at[me], out_sem.at[2])
    keep_gx.start()
    late[0] = jnp.concatenate(totals, axis=0)
    s_late.start(0)
    s_late.take(0)
    s_f3.take(4)
    last_z()
    s_q[1].take(3)
    s_late.take(1)

    def write(n, src, dst):
        copy = pltpu.make_async_copy(src, dst, out_sem.at[3 + n])
        copy.start()
        return copy

    side = width // 2
    for part, who in zip(s_p.last(), (me, 1 - me)):
        w_proj[:, pl.ds(pl.multiple_of(who * side, side), side)] = part
    writes = [write(0, w_proj, wproj_out)]
    tile = g_f3.shape[-1]
    side = tile // 2
    for sum_, tiles in ((s_f, (0, 1)), (s_f2, (2,)), (s_f3, (3,))):
        for part, who in zip(sum_.last(), (me, 1 - me)):
            for n, t in enumerate(tiles):
                at = pl.ds(pl.multiple_of(t * tile + who * side, side), side)
                w_fc[:, at] = part[:, n * side : (n + 1) * side]
    writes.append(write(1, w_fc, wfc_out))
    own, came = s_out.last()
    w_out[...] = own + came
    writes.append(write(2, w_out, wout_out))
    last_copy.wait()
    for n in range(3):
        if n < 2:
            own, came = s_q[n].last()
        else:
            own, came = last_sum[...].astype(F32), r_last[...].astype(F32)
        part = own + came
        at = 0
        for start, size in parts[n][1]:
            wqkv_out[:, start : start + size] = part[:, at : at + size]
            at += size
    s_late.take(2)
    small_out[...] = jnp.concatenate(
        [sums[3, 0:4, :], late[3], sums[3, 4:8, :], jnp.zeros((4, width), F32)], axis=0
    )
    back_gf.wait()
    for copy in backs:
        copy.wait()
    for copy in writes:
        copy.wait()
    keep_gf.wait()
    keep_gx.wait()


def tail(
    q, k, v, do, bias, x, act1t, gmid, wqkv, dwout, f, f2, f3, p, lse, dots, g1, dbfc, small
):
    tokens, width = q.shape
    half = tokens // 2
    val = wqkv.shape[1] - 2 * width
    owner = width // 16
    owner_ff = dbfc.shape[1] // 16
    ff = dbfc.shape[1]
    tile = f3.shape[-1]
    shape = jax.ShapeDtypeStruct
    hbm = pl.BlockSpec(memory_space=pl.ANY)
    vmem = pl.BlockSpec(memory_space=pltpu.VMEM)

    def vm(*s):
        return pltpu.VMEM(s, BF)

    def chain(rows, cols):
        return [
            vm(2, 2, 2, rows, cols),
            vm(2, 2, rows, cols),
            vm(2, rows, cols),
            vm(rows, cols),
            vm(rows, cols),
        ]

    def cut_chain(rows, cols):
        side = chain(rows, cols // 2)
        return [vm(2, 2, 2, rows, cols)] + side[:1] + side[1:4] + side[3:4]

    flat = vm(tokens, width)
    sizes = [sum(size for _, size in columns) for _, columns in pieces(width, val)]
    return pl.pallas_call(
        tail_kernel,
        in_specs=[hbm] * 14 + [vmem] * 5,
        out_specs=[hbm] * 2 + [vmem] + [hbm] * 3 + [vmem],
        out_shape=[
            shape((2, half, width), BF),
            shape((2, half, val), BF),
            shape((owner, wqkv.shape[1]), F32),
            shape((owner, width), F32),
            shape((owner, ff), F32),
            shape((owner_ff, width), F32),
            shape((16, width), F32),
        ],
        scratch_shapes=[
            flat,
            flat,
            flat,
            flat,
            pltpu.VMEM((tokens, tokens), F32),
            flat,
            pltpu.VMEM((tokens, width), F32),
            vm(*wqkv.shape),
            vm(tokens, 2 * width),
            vm(tokens, val),
            vm(tokens, val),
            pltpu.VMEM((tokens, LANES), F32),
            vm(width, tokens),
            flat,
            vm(*dwout.shape),
            vm(*f.shape),
            vm(*f2.shape),
            vm(*f3.shape),
            vm(*p.shape),
            [vm(2, 2, 2, 2, owner, size) for size in sizes],
            chain(owner, width),
            chain(owner, f.shape[-1])[1:],
            cut_chain(owner, tile)[1:],
            cut_chain(owner, tile),
            [vm(2, 2, owner_ff, width // 2)] + cut_chain(owner_ff, width)[3:],
            [chain(owner, size) for size in sizes[:2]] + [chain(owner, sizes[2])[:2]],
            vm(owner, sizes[2]),
            vm(3, owner, sizes[2]),
            vm(owner, sizes[2]),
            pltpu.VMEM((4, 8, width), F32),
            [pltpu.VMEM(n + (8, width), F32) for n in ((), (len(FLIPS),), ())],
            pltpu.VMEM((4, 4, width), F32),
            [pltpu.VMEM(n + (4, width), F32) for n in ((), (len(FLIPS),), ())],
            pltpu.VMEM((owner, ff), F32),
            pltpu.VMEM((owner_ff, width), F32),
            pltpu.VMEM((owner, width), F32),
            pltpu.SemaphoreType.DMA((14,)),
            pltpu.SemaphoreType.DMA((6,)),
            pltpu.SemaphoreType.DMA((6,)),
            pltpu.SemaphoreType.DMA((6,)),
            pltpu.SemaphoreType.DMA((11, 6)),
            pltpu.SemaphoreType.DMA((11, 6)),
            pltpu.SemaphoreType.DMA((3, len(FLIPS))),
            pltpu.SemaphoreType.DMA((3, len(FLIPS))),
        ],
        compiler_params=pltpu.CompilerParams(
            collective_id=2, has_side_effects=True, vmem_limit_bytes=62 * MIB
        ),
        name="tail",
    )(q, k, v, do, bias, x, act1t, gmid, wqkv, dwout, f, f2, f3, p, lse, dots, g1, dbfc, small)


def finish_kernel(*refs):
    wide_in, sums = refs[:7], refs[7]
    wide_out, small_out, held, sem = refs[8:15], refs[15:24], refs[24], refs[25]
    loads = [pltpu.make_async_copy(src, dst, sem.at[0, n]) for n, (src, dst) in enumerate(zip(wide_in, held))]
    stores = [pltpu.make_async_copy(src, dst, sem.at[1, n]) for n, (src, dst) in enumerate(zip(held, wide_out))]
    for load in loads:
        load.start()
    b = lax.axis_index("batch")
    rows = sums[0:8, :]
    width = rows.shape[1]
    long = jnp.concatenate([sums[8 + n : 9 + n, :] for n in range(4)], axis=1)
    long = jnp.broadcast_to(long, (8, 4 * width))
    for at, ref in zip((4, 5, 6, 7, 3, 1, 2, None, 0), small_out):
        size = ref.shape[0]
        source = long if at is None else rows
        line = 0 if at is None else at
        length = source.shape[1]
        turned = pltpu.roll(source, lax.rem(length - b * size, length), 1)
        ref[...] = turned[line, :size]
    for load, store in zip(loads, stores):
        load.wait()
        store.start()
    for store in stores:
        store.wait()


def finish(wide, sums, sizes):
    hbm = pl.BlockSpec(memory_space=pl.ANY)
    vmem = pl.BlockSpec(memory_space=pltpu.VMEM)
    shape = jax.ShapeDtypeStruct
    return pl.pallas_call(
        finish_kernel,
        in_specs=[hbm] * 7 + [vmem],
        out_specs=[hbm] * 7 + [vmem] * 9,
        out_shape=[shape(a.shape, a.dtype) for a in wide] + [shape((n,), F32) for n in sizes],
        scratch_shapes=[
            [pltpu.VMEM(a.shape, a.dtype) for a in wide],
            pltpu.SemaphoreType.DMA((2, 7)),
        ],
        compiler_params=pltpu.CompilerParams(vmem_limit_bytes=60 * MIB),
        name="finish",
    )(*wide, sums)


def paired(
    inputs,
    first_values,
    segments,
    ln1_gain,
    first_norm_bias,
    w_qkv,
    b_query,
    b_value,
    w_out,
    b_out,
    ln2_gain,
    second_norm_bias,
    w_fc,
    b_fc,
    w_proj,
    b_proj,
    cotangent,
):
    half, width = inputs.shape[1], inputs.shape[2]
    val = first_values.shape[2]
    x, q, k, v, att, act2, mid, lse, bias, act1t, cot_far = front(
        inputs,
        first_values,
        segments,
        cotangent,
        ln1_gain,
        first_norm_bias,
        w_qkv,
        b_query,
        b_value,
        w_out,
        b_out,
        ln2_gain,
        second_norm_bias,
    )
    layer_out, gmid, gatt, dwout, f, f2, f3, p, dots, dbfc, small = feed(
        act2, cotangent, cot_far, mid, att, ln2_gain, b_proj, w_out, w_fc, b_fc, w_proj
    )
    owner = width // 16
    *wide, sums = tail(
        q,
        k,
        v,
        gatt,
        bias,
        x,
        act1t,
        gmid,
        w_qkv,
        dwout,
        f,
        f2,
        f3,
        p,
        lse,
        dots,
        ln1_gain,
        dbfc,
        small,
    )
    sizes = [owner, owner, owner, val // 16, owner, owner, owner, w_fc.shape[1] // 16, owner]
    out = finish([layer_out] + wide, sums, sizes)
    layer_out, grad_inputs, grad_first, gwqkv, gwout, gwfc, gwproj = out[:7]
    g1, b1, bq, bv, bo, g2, b2, bf, bp = out[7:]
    return (
        layer_out,
        grad_inputs,
        grad_first,
        g1,
        b1,
        gwqkv,
        bq,
        bv,
        gwout,
        bo,
        g2,
        b2,
        gwfc,
        bf,
        gwproj,
        bp,
    )


MICRO = 2


def as_sent(shard):
    return jax.tree.map(lambda a: a.astype(jnp.bfloat16) if a.dtype == jnp.float32 else a, shard)


def apply_norm(values_in, norm_gain, shift_bias):
    mean_val = jnp.mean(values_in, axis=-1, keepdims=True)
    centred_rows = values_in - mean_val
    inverse_deviation = lax.rsqrt(
        jnp.mean(centred_rows * centred_rows, axis=-1, keepdims=True) + EPS
    )
    standardized = centred_rows * inverse_deviation
    return (standardized * norm_gain + shift_bias, standardized, inverse_deviation)


def apply_norm_backward(upstream_gradient, standardized, inverse_deviation, norm_gain):
    scaled_rows = upstream_gradient * norm_gain
    first_average = jnp.mean(scaled_rows, axis=-1, keepdims=True)
    second_average = jnp.mean(scaled_rows * standardized, axis=-1, keepdims=True)
    incoming_gradient = inverse_deviation * (
        scaled_rows - first_average - standardized * second_average
    )
    return (
        incoming_gradient,
        jnp.sum(upstream_gradient * standardized, axis=(0, 1)),
        jnp.sum(upstream_gradient, axis=(0, 1)),
    )


def gelu_tanh(values_in):
    cubic = values_in + 0.044715 * values_in * values_in * values_in
    return 0.5 * values_in * (1.0 + jnp.tanh(0.7978845608028654 * cubic))


def heads_of(values_in):
    return values_in.reshape(values_in.shape[0], values_in.shape[1], HEADS, HEAD_DIM)


def visible(seg_query, seg_key, query_pos, key_pos):
    same = seg_query[:, :, None] == seg_key[:, None, :]
    causal = key_pos[None, :] <= query_pos[:, None]
    live = seg_query[:, :, None] >= 0
    diagonal = key_pos[None, :] == query_pos[:, None]
    return (same & causal[None] & live | diagonal[None])[:, :, None, :]


def score_block(query4, key4, mask):
    raw = jnp.einsum("rqhd,rkhd->rqhk", query4, key4, preferred_element_type=jnp.float32)
    return jnp.where(mask, raw * HEAD_DIM ** (-0.5), NEG)


def grad_block(query4, key4, value4, dout4, log_total, out_dot, mask):
    probs = jnp.where(mask, jnp.exp(score_block(query4, key4, mask) - log_total[..., None]), 0.0)
    probs_low = probs.astype(jnp.bfloat16)
    grad_probs = jnp.einsum("rqhd,rkhd->rqhk", dout4, value4, preferred_element_type=jnp.float32)
    grad_scores = (probs * (grad_probs - out_dot[..., None]) * HEAD_DIM ** (-0.5)).astype(
        jnp.bfloat16
    )
    return (probs_low, grad_scores)


def spread(
    inputs,
    first_values,
    segments,
    ln1_gain,
    first_norm_bias,
    w_qkv,
    b_query,
    b_value,
    w_out,
    b_out,
    ln2_gain,
    second_norm_bias,
    w_fc,
    b_fc,
    w_proj,
    b_proj,
    cotangent,
):
    all_seg = lax.all_gather(segments, "blk", axis=1, tiled=True)
    block_len = inputs.shape[1]
    model_width = inputs.shape[2]
    val_width = first_values.shape[2]
    rows_mb = inputs.shape[0] // MICRO
    own_pos = lax.axis_index("blk") * block_len + jnp.arange(block_len)
    first_gain = ln1_gain.astype(jnp.float32)
    second_gain = ln2_gain.astype(jnp.float32)
    outputs = []
    input_grads = []
    first_grads = []
    totals = None
    for micro_step in range(MICRO):
        first_row = micro_step * rows_mb
        last_row = first_row + rows_mb
        residual_stream = inputs[first_row:last_row].astype(jnp.float32)
        first_part = first_values[first_row:last_row]
        seg_local = segments[first_row:last_row]
        seg_row = all_seg[first_row:last_row]
        cot_part = cotangent[first_row:last_row]
        first_normed_rows, first_standardized, first_inverse_deviation = apply_norm(
            residual_stream, first_gain, first_norm_bias.astype(jnp.float32)
        )
        act1 = first_normed_rows.astype(jnp.bfloat16)
        projected = jnp.einsum("rbd,de->rbe", act1, w_qkv, preferred_element_type=jnp.float32)
        queries = (projected[..., :model_width] + b_query.astype(jnp.float32)).astype(jnp.bfloat16)
        keys_low = projected[..., model_width : 2 * model_width].astype(jnp.bfloat16)
        fresh = (projected[..., 2 * model_width :] + b_value.astype(jnp.float32)).astype(
            jnp.bfloat16
        )
        values_low = jnp.concatenate([fresh, first_part], axis=-1)
        query4 = heads_of(queries)
        key_part = lax.all_gather(keys_low, "blk", axis=1, tiled=True)
        value_part = lax.all_gather(values_low, "blk", axis=1, tiled=True)
        span = key_part.shape[1]
        key_pos = jnp.arange(span)
        mask = visible(seg_local, seg_row, own_pos, key_pos)
        scores = score_block(query4, heads_of(key_part), mask)
        old_max = jnp.full((rows_mb, block_len, HEADS), NEG, jnp.float32)
        new_max = jnp.maximum(old_max, jnp.max(scores, axis=-1))
        weights = jnp.where(mask, jnp.exp(scores - new_max[..., None]), 0.0)
        new_sum = jnp.sum(weights, axis=-1)
        new_acc = jnp.einsum(
            "rqhk,rkhd->rqhd",
            weights.astype(jnp.bfloat16),
            heads_of(value_part),
            preferred_element_type=jnp.float32,
        )
        attention4 = new_acc / new_sum[..., None]
        log_total = new_max + jnp.log(new_sum)
        attention_low = attention4.reshape(rows_mb, block_len, model_width).astype(jnp.bfloat16)
        branch = jnp.einsum("rbd,de->rbe", attention_low, w_out, preferred_element_type=jnp.float32)
        middle_state = residual_stream + branch + b_out.astype(jnp.float32)
        second_normed_rows, second_standardized, second_inverse_deviation = apply_norm(
            middle_state, second_gain, second_norm_bias.astype(jnp.float32)
        )
        act2 = second_normed_rows.astype(jnp.bfloat16)
        pre_gelu = jnp.einsum(
            "rbd,df->rbf", act2, w_fc, preferred_element_type=jnp.float32
        ) + b_fc.astype(jnp.float32)
        hidden = gelu_tanh(pre_gelu).astype(jnp.bfloat16)
        result = middle_state + jnp.einsum(
            "rbf,fd->rbd", hidden, w_proj, preferred_element_type=jnp.float32
        )
        result = result + b_proj.astype(jnp.float32)
        outputs.append(result.astype(jnp.bfloat16))
        upstream_gradient = cot_part.astype(jnp.float32)
        grad_wproj = jnp.einsum("rbf,rbd->fd", hidden, cot_part, preferred_element_type=jnp.float32)
        grad_bproj = jnp.sum(upstream_gradient, axis=(0, 1))
        grad_hidden = jnp.einsum(
            "rbd,fd->rbf", cot_part, w_proj, preferred_element_type=jnp.float32
        )
        gelu_value, gelu_pull = jax.vjp(gelu_tanh, pre_gelu)
        grad_pre = gelu_pull(grad_hidden)[0].astype(jnp.bfloat16)
        grad_wfc = jnp.einsum("rbd,rbf->df", act2, grad_pre, preferred_element_type=jnp.float32)
        grad_bfc = jnp.sum(grad_pre.astype(jnp.float32), axis=(0, 1))
        second_activation_gradient = jnp.einsum(
            "rbf,df->rbd", grad_pre, w_fc, preferred_element_type=jnp.float32
        )
        second_norm_gradient, second_gain_gradient, second_bias_gradient = apply_norm_backward(
            second_activation_gradient, second_standardized, second_inverse_deviation, second_gain
        )
        grad_middle = upstream_gradient + second_norm_gradient
        grad_branch = grad_middle.astype(jnp.bfloat16)
        grad_wout = jnp.einsum(
            "rbd,rbe->de", attention_low, grad_branch, preferred_element_type=jnp.float32
        )
        grad_bout = jnp.sum(grad_branch.astype(jnp.float32), axis=(0, 1))
        grad_attention = jnp.einsum(
            "rbe,de->rbd", grad_branch, w_out, preferred_element_type=jnp.float32
        ).astype(jnp.bfloat16)
        dout4 = heads_of(grad_attention)
        out_dot = jnp.sum(dout4.astype(jnp.float32) * attention4, axis=-1)
        back_key_part = lax.all_gather(keys_low, "blk", axis=1, tiled=True)
        back_value_part = lax.all_gather(values_low, "blk", axis=1, tiled=True)
        back_span = back_key_part.shape[1]
        back_key_pos = jnp.arange(back_span)
        back_mask = visible(seg_local, seg_row, own_pos, back_key_pos)
        part_key4 = heads_of(back_key_part)
        probs_low, grad_scores = grad_block(
            query4, part_key4, heads_of(back_value_part), dout4, log_total, out_dot, back_mask
        )
        query_acc = jnp.einsum(
            "rqhk,rkhd->rqhd", grad_scores, part_key4, preferred_element_type=jnp.float32
        )
        key_piece = jnp.einsum(
            "rqhk,rqhd->rkhd", grad_scores, query4, preferred_element_type=jnp.float32
        ).reshape(rows_mb, back_span, model_width)
        value_piece = jnp.einsum(
            "rqhk,rqhd->rkhd", probs_low, dout4, preferred_element_type=jnp.float32
        ).reshape(rows_mb, back_span, model_width)
        query_acc, key_acc, value_acc = (query_acc, key_piece, value_piece)
        grad_keys, grad_values = (
            lax.psum_scatter(
                key_acc.astype(jnp.bfloat16), "blk", scatter_dimension=1, tiled=True
            ).astype(jnp.float32),
            lax.psum_scatter(
                value_acc.astype(jnp.bfloat16), "blk", scatter_dimension=1, tiled=True
            ).astype(jnp.float32),
        )
        grad_query = query_acc.reshape(rows_mb, block_len, model_width)
        grad_qkv = jnp.concatenate(
            [
                grad_query.astype(jnp.bfloat16),
                grad_keys.astype(jnp.bfloat16),
                grad_values[..., :val_width].astype(jnp.bfloat16),
            ],
            axis=-1,
        )
        first_grads.append(grad_values[..., val_width:].astype(jnp.bfloat16))
        grad_wqkv = jnp.einsum("rbd,rbe->de", act1, grad_qkv, preferred_element_type=jnp.float32)
        grad_bquery = jnp.sum(grad_qkv[..., :model_width].astype(jnp.float32), axis=(0, 1))
        grad_bvalue = jnp.sum(grad_qkv[..., 2 * model_width :].astype(jnp.float32), axis=(0, 1))
        first_activation_gradient = jnp.einsum(
            "rbe,de->rbd", grad_qkv, w_qkv, preferred_element_type=jnp.float32
        )
        first_norm_gradient, first_gain_gradient, first_bias_gradient = apply_norm_backward(
            first_activation_gradient, first_standardized, first_inverse_deviation, first_gain
        )
        input_grads.append((grad_middle + first_norm_gradient).astype(jnp.bfloat16))
        gradient_set = (
            first_gain_gradient,
            first_bias_gradient,
            grad_wqkv,
            grad_bquery,
            grad_bvalue,
            grad_wout,
            grad_bout,
            second_gain_gradient,
            second_bias_gradient,
            grad_wfc,
            grad_bfc,
            grad_wproj,
            grad_bproj,
        )
        if totals is None:
            totals = gradient_set
        else:
            totals = tuple((older + newer for older, newer in zip(totals, gradient_set)))
    totals = jax.tree.map(
        lambda part: part.astype(jnp.float32),
        lax.psum_scatter(as_sent(totals), "batch", scatter_dimension=0, tiled=True),
    )
    totals = jax.tree.map(lambda part: part.astype(jnp.float32), lax.psum(as_sent(totals), "blk"))
    return (
        jnp.concatenate(outputs, axis=0),
        jnp.concatenate(input_grads, axis=0),
        jnp.concatenate(first_grads, axis=0),
    ) + tuple(totals)


def layer(inputs, *rest):
    whole_rows = lax.axis_size("blk") == inputs.shape[0] == 2 and inputs.shape[1] == 2 * QB
    whole_rows = whole_rows and lax.axis_size("batch") == 16
    return (paired if whole_rows else spread)(inputs, *rest)


def solution(mesh):
    rows = P("batch", "blk", None)
    flat = P("batch")
    wide = P("batch", None)
    return jax.shard_map(
        layer,
        mesh=mesh,
        in_specs=(rows, rows, P("batch", "blk")) + (P(),) * 13 + (rows,),
        out_specs=(rows, rows, rows)
        + (flat, flat, wide, flat, flat, wide, flat, flat, flat, wide, flat, wide, flat),
        check_vma=False,
    )
```
